32 devices in a mesh: pack: 8 (over y, x, core), seq: 4 (over z).
Axes of the slice: x: 2, y: 2, z: 4, core: 2. Of those that a mesh axis runs over, the one named last changes fastest.
Arguments:
- patches: bfloat16 [48, 1024, 768], P('pack', 'seq'), may hold values from -6 to 6
- lengths: int32 [48, 16], P('pack'), may hold values from 1 to 128, 1024 in all within a row
- keep_mask: int32 [48, 1024], P('pack'), may hold values 0 or 1
- labels: int32 [48, 16], replicated, may hold values from 0 to 21842
- step_count: int32 [1], replicated, may hold values from 2 to 20
- embed_weight: float32 [768, 768], P(None, ('pack', 'seq')), may hold values from -0.21875 to 0.21875
- embed_first: float32 [768, 768], P(None, ('pack', 'seq')), may hold values from -0.00030517578 to 0.00030517578
- embed_second: float32 [768, 768], P(None, ('pack', 'seq')), may hold values from 1.2450748e-08 to 5.033281e-08
- qkv_weight: float32 [768, 2304], P(None, ('pack', 'seq')), may hold values from -0.21875 to 0.21875
- qkv_moment: float32 [768, 2304], P(None, ('pack', 'seq')), may hold values from -0.0029296875 to 0.0029296875
- output_weight: float32 [768, 768], P(None, ('pack', 'seq')), may hold values from -0.625 to 0.625
- output_moment: float32 [768, 768], P(None, ('pack', 'seq')), may hold values from -0.0029296875 to 0.0029296875
- up_weight: float32 [768, 3072], P(None, ('pack', 'seq')), may hold values from -0.21875 to 0.21875
- up_moment: float32 [768, 3072], P(None, ('pack', 'seq')), may hold values from -0.0029296875 to 0.0029296875
- down_weight: float32 [768, 3072], P(None, ('pack', 'seq')), may hold values from -0.109375 to 0.109375
- down_moment: float32 [768, 3072], P(None, ('pack', 'seq')), may hold values from -0.0029296875 to 0.0029296875
- small_params: float32 [15, 768], P(None, ('pack', 'seq')), may hold values from -0.5 to 1.4, as said below
- small_first: float32 [15, 768], P(None, ('pack', 'seq')), may hold values from -0.0024414062 to 0.0024414062
- small_second: float32 [15, 768], P(None, ('pack', 'seq')), may hold values from 7.9684787e-07 to 3.2213e-06
- head_weight: float32 [768, 21856], P('seq', 'pack'), may hold values from -0.21875 to 0.21875
- head_first: float32 [768, 21856], P('seq', 'pack'), may hold values from -0.00015258789 to 0.00015258789
- head_second: float32 [768, 21856], P('seq', 'pack'), may hold values from 3.1593836e-09 to 1.2518313e-08
- head_bias: float32 [21856], P(('pack', 'seq')), may hold values from -6 to 6
- bias_first: float32 [21856], P(('pack', 'seq')), may hold values from -0.00012207031 to 0.00012207031
- bias_second: float32 [21856], P(('pack', 'seq')), may hold values from 1.4313102e-09 to 5.7252407e-09
Outputs:
- loss_value: float32 [], replicated
- grad_norm: float32 [], replicated
- new_embed: float32 [768, 768], P(None, ('pack', 'seq'))
- new_embed_first: float32 [768, 768], P(None, ('pack', 'seq'))
- new_embed_second: float32 [768, 768], P(None, ('pack', 'seq'))
- new_qkv: float32 [768, 2304], P(None, ('pack', 'seq'))
- new_qkv_moment: float32 [768, 2304], P(None, ('pack', 'seq'))
- new_output: float32 [768, 768], P(None, ('pack', 'seq'))
- new_output_moment: float32 [768, 768], P(None, ('pack', 'seq'))
- new_up: float32 [768, 3072], P(None, ('pack', 'seq'))
- new_up_moment: float32 [768, 3072], P(None, ('pack', 'seq'))
- new_down: float32 [768, 3072], P(None, ('pack', 'seq'))
- new_down_moment: float32 [768, 3072], P(None, ('pack', 'seq'))
- new_small: float32 [15, 768], P(None, ('pack', 'seq'))
- new_small_first: float32 [15, 768], P(None, ('pack', 'seq'))
- new_small_second: float32 [15, 768], P(None, ('pack', 'seq'))
- new_head: float32 [768, 21856], P('seq', 'pack')
- new_head_first: float32 [768, 21856], P('seq', 'pack')
- new_head_second: float32 [768, 21856], P('seq', 'pack')
- new_bias: float32 [21856], P(('pack', 'seq'))
- new_bias_first: float32 [21856], P(('pack', 'seq'))
- new_bias_second: float32 [21856], P(('pack', 'seq'))
The draws below stay inside these ranges and needn't reach their ends.
Inputs may be any that keep to these rules, and one draw needn't show every extreme that they name: Each pack's 16 lengths sum to 1024, and its longest is exactly 128. `small_params`: rows 0, 2 and 4 lie in [0.6, 1.4], the other rows in [-0.5, 0.5].
All inputs are finite; a program needn't handle non-finite values. No bound on the sum of `keep_mask` on one device may be relied on, other than what follows from the above.
Results may differ from the reference program's by a relative error of at most 0.00055.
The reference program's roundings to bfloat16 on the way count: a program that leaves them out, or rounds other values in their place, can miss the bound.
Values may be sent and summed in bfloat16 or wider, within the bound.
No kernel may reach another device: no remote copies, remote signals or barrier semaphores. Data moves between devices by JAX's collectives and lax.ppermute only.
A program may use at most 384 MiB of HBM per device.

```python
import math
import jax
import jax.numpy as jnp
import numpy as np
from jax import lax

D = 768
HEADS = 12
HEAD_DIM = 64
FF = 3072
PATCH_IN = 768
LABELS = 21843
PACK_LEN = 1024
IMG_PACK = 16
MAXLEN = 128
NS_STEPS = 2
PACKS = 48
IMAGES = 768
LABELS_PAD = 21856


def draw_small_params(key, part):
    gain_draw = jax.random.uniform(jax.random.fold_in(key, 11), (15, D), jnp.float32, 0.6, 1.4)
    shift_draw = jax.random.uniform(jax.random.fold_in(key, 12), (15, D), jnp.float32, -0.5, 0.5)
    row_index = jnp.arange(15)[:, None]
    gain_rows = (row_index == 0) | (row_index == 2) | (row_index == 4)
    return jnp.where(gain_rows, gain_draw, shift_draw)


def touch_ends(values, rng, least, largest):
    longest = values.shape.index(max(values.shape))
    spots = []
    for shift in (0, 1):
        where = [jax.random.randint(jax.random.fold_in(rng, axis), (), 0, length) for axis, length in enumerate(values.shape)]
        where[longest] = (where[longest] + shift) % values.shape[longest]
        spots.append(tuple(where))
    return values.at[spots[0]].set(least).at[spots[1]].set(largest)


def block_levels(stream_key, shape, shards, low, top_value):
    def one(dim, blocks):
        draws = jax.random.uniform(jax.random.fold_in(jax.random.fold_in(stream_key, 6), dim), (blocks,), jnp.float32, low / len(shards), top_value / len(shards))
        return jnp.repeat(jnp.exp(draws), shape[dim] // blocks).reshape((-1,) + (1,) * (len(shape) - dim - 1))

    loudness = one(*shards[0])
    for cut in shards[1:]:
        loudness = loudness * one(*cut)
    return loudness


def profile(number_of, total, limit, skew):
    portions = [(1 << 20) // math.isqrt(grade ** skew) + 1 for grade in range(2, number_of + 1)]
    spare, holding = total - limit - (number_of - 1), [1] * (number_of - 1)
    while spare > 0:
        movable = [i for i in range(number_of - 1) if holding[i] < limit]
        mass, left = sum([portions[i] for i in movable]), spare
        for i in movable:
            addition = min(limit - holding[i], max(1, left * portions[i] // mass), spare)
            holding[i] = holding[i] + addition
            spare = spare - addition
    return np.array([limit] + holding)


def uneven(key, amount, total, limit, slope):
    if amount == 2:
        one = jax.random.randint(key, (), max(1, total - limit), min(limit, total - 1) + 1)
        return jnp.stack([one, total - one])
    sizes = jnp.asarray(profile(amount, total, limit, slope), jnp.int32)
    couples = (amount - 1) // 2
    giver, receiver = sizes[1:1 + 2 * couples:2], sizes[2:2 + 2 * couples:2]
    margin = jnp.minimum(giver - 1, limit - receiver)
    passed = jax.random.randint(jax.random.fold_in(key, 1), (couples,), 0, 1 << 20) % (margin + 1)
    sizes = sizes.at[1:1 + 2 * couples:2].set(giver - passed).at[2:2 + 2 * couples:2].set(receiver + passed)
    return sizes[jax.random.permutation(jax.random.fold_in(key, 2), amount)]


def centred(own_key, shape, scale, bound, split=(), kind=jnp.bfloat16):
    array = scale * jax.random.normal(own_key, shape, jnp.float32)
    if split:
        array = array * block_levels(own_key, shape, split, -0.22, 0.18)
    return jnp.clip(array, -bound, bound).astype(kind)


def setup_inputs(seed: int = 0) -> dict:
    seeds = jax.random.split(jax.random.key(seed), 26)
    patches = centred(seeds[0], (PACKS, PACK_LEN, PATCH_IN), 1.0, 6.0, ((0, 8), (1, 4)))
    lengths = jax.vmap(lambda own: uneven(own, IMG_PACK, PACK_LEN, MAXLEN, 2))(jax.random.split(seeds[1], PACKS)).reshape((PACKS, IMG_PACK)).astype(jnp.int32)
    keep_mask = touch_ends((jax.random.randint(seeds[2], (PACKS, PACK_LEN), 0, 4) < 3).astype(jnp.int32), jax.random.fold_in(seeds[2], 1), 0, 1)
    labels = touch_ends(jax.random.randint(seeds[3], (PACKS, IMG_PACK), 0, LABELS), jax.random.fold_in(seeds[3], 1), 0, LABELS - 1).astype(jnp.int32)
    step_count = jax.random.randint(seeds[4], (1,), 2, 21).astype(jnp.int32)
    embed_weight = centred(seeds[5], (PATCH_IN, D), PATCH_IN ** -0.5, 0.21875, ((1, 32),), jnp.float32)
    embed_first = centred(seeds[6], (PATCH_IN, D), (0.33 / (D * PACKS * PACK_LEN) ** 0.5), 0.00030517578, ((1, 32),), jnp.float32)
    embed_second = jnp.clip(jnp.exp(math.log(5.0332811696307544e-08) - 1.3968765 * jax.random.uniform(seeds[7], (PATCH_IN, D), jnp.float32) ** block_levels(seeds[7], (PATCH_IN, D), ((1, 32),), -0.2, 0.2)), 1.2450747988168587e-08, 5.0332811696307544e-08)
    qkv_weight = centred(seeds[8], (D, 3 * D), D ** -0.5, 0.21875, ((1, 32),), jnp.float32)
    qkv_moment = centred(seeds[9], (D, 3 * D), (3 / (D * PACKS * PACK_LEN) ** 0.5), 0.0029296875, ((1, 32),), jnp.float32)
    output_weight = centred(seeds[10], (D, D), (D // 8) ** -0.5, 0.625, ((1, 32),), jnp.float32)
    output_moment = centred(seeds[11], (D, D), (3 / (D * PACKS * PACK_LEN) ** 0.5), 0.0029296875, ((1, 32),), jnp.float32)
    up_weight = centred(seeds[12], (D, FF), D ** -0.5, 0.21875, ((1, 32),), jnp.float32)
    up_moment = centred(seeds[13], (D, FF), (3 / (D * PACKS * PACK_LEN) ** 0.5), 0.0029296875, ((1, 32),), jnp.float32)
    down_weight = centred(seeds[14], (D, FF), FF ** -0.5, 0.109375, ((1, 32),), jnp.float32)
    down_moment = centred(seeds[15], (D, FF), (3 / (D * PACKS * PACK_LEN) ** 0.5), 0.0029296875, ((1, 32),), jnp.float32)
    small_params = draw_small_params(jax.random.fold_in(seeds[25], 71), 0)
    small_first = centred(seeds[17], (15, D), (0.33 / (D * IMAGES) ** 0.5), 0.0024414062, ((1, 32),), jnp.float32)
    small_second = jnp.clip(jnp.exp(math.log(3.221299948563683e-06) - 1.3968765 * jax.random.uniform(seeds[18], (15, D), jnp.float32) ** block_levels(seeds[18], (15, D), ((1, 32),), -0.2, 0.2)), 7.968478712427896e-07, 3.221299948563683e-06)
    head_weight = centred(seeds[19], (D, LABELS_PAD), D ** -0.5, 0.21875, ((0, 4), (1, 8)), jnp.float32)
    head_first = centred(seeds[20], (D, LABELS_PAD), (0.11 / (IMAGES * LABELS) ** 0.5), 0.00015258789, ((0, 4), (1, 8)), jnp.float32)
    head_second = jnp.clip(jnp.exp(math.log(1.2518312608733595e-08) - 1.37681562 * jax.random.uniform(seeds[21], (D, LABELS_PAD), jnp.float32) ** block_levels(seeds[21], (D, LABELS_PAD), ((0, 4), (1, 8)), -0.2, 0.2)), 3.1593836435916955e-09, 1.2518312608733595e-08)
    head_bias = centred(seeds[22], (LABELS_PAD,), 1.0, 6.0, ((0, 32),), jnp.float32)
    bias_first = centred(seeds[23], (LABELS_PAD,), (0.11 / (PATCH_IN * D + 4 * D * D + 2 * D * FF + D * LABELS_PAD) ** 0.5), 0.00012207031, ((0, 32),), jnp.float32)
    bias_second = jnp.clip(jnp.exp(math.log(5.725240725951153e-09) - 1.3862944 * jax.random.uniform(seeds[24], (LABELS_PAD,), jnp.float32) ** block_levels(seeds[24], (LABELS_PAD,), ((0, 32),), -0.2, 0.2)), 1.4313101814877882e-09, 5.725240725951153e-09)
    return {"patches": patches, "lengths": lengths, "keep_mask": keep_mask, "labels": labels, "step_count": step_count, "embed_weight": embed_weight, "embed_first": embed_first, "embed_second": embed_second, "qkv_weight": qkv_weight, "qkv_moment": qkv_moment, "output_weight": output_weight, "output_moment": output_moment, "up_weight": up_weight, "up_moment": up_moment, "down_weight": down_weight, "down_moment": down_moment, "small_params": small_params, "small_first": small_first, "small_second": small_second, "head_weight": head_weight, "head_first": head_first, "head_second": head_second, "head_bias": head_bias, "bias_first": bias_first, "bias_second": bias_second}


HIGHEST_PREC = lax.Precision.HIGHEST
CLIP_NORM = 1.0
MUON_MU = 0.95
MUON_RATE = 1.0
ADAM_RATE = 0.02
BETA_ONE = 0.9
BETA_TWO = 0.95
DECAY = 0.01
COEF_ONE = 3.4445
COEF_TWO = -4.775
COEF_THREE = 2.0315

@jax.custom_vjp
def low(v):
    return lax.optimization_barrier(v.astype(jnp.bfloat16)).astype(jnp.float32)

@jax.custom_vjp
def low_back(v):
    return v

def low_keep(v):
    return (low(v), None)

def low_pass(kept, grad):
    return (grad,)

def back_keep(v):
    return (v, None)

def back_low(kept, grad):
    return (low(grad),)
low.defvjp(low_keep, low_pass)
low_back.defvjp(back_keep, back_low)

def layer_norm(values, gain_row, bias_row):
    centre = values - lax.optimization_barrier(jnp.mean(values, axis=-1, keepdims=True))
    spread = lax.optimization_barrier(jnp.mean(centre * centre, axis=-1, keepdims=True))
    return centre * lax.rsqrt(spread + 1e-06) * gain_row + bias_row

def image_index(lengths_all, positions):
    ends_at = jnp.cumsum(lengths_all, axis=-1, dtype=jnp.int32)
    starts_at = ends_at - lengths_all
    image_ids = lax.optimization_barrier(jnp.sum((positions[None, :, None] >= ends_at[:, None, :]).astype(jnp.int32), axis=2, dtype=jnp.int32))
    is_first = jnp.any(positions[None, :, None] == starts_at[:, None, :], axis=2)
    inside = (positions >= 0) & (positions < PACK_LEN)
    return (jnp.where(inside[None, :], image_ids, -1), is_first)

def matmul(left, right):
    return jnp.dot(left, right, precision=HIGHEST_PREC, preferred_element_type=jnp.float32)

def pack_forward(layer_params, patch_rows, lengths_one, keep_one):
    embed_w, qkv_w, output_w, up_w, down_w, gain_bias = layer_params
    positions = jnp.arange(PACK_LEN, dtype=jnp.int32)
    image_ids, is_first = image_index(lengths_one[None, :], positions)
    image_ids = image_ids[0]
    kept = (keep_one > 0) | is_first[0]
    embedded = low_back(matmul(patch_rows, embed_w) + gain_bias[6])
    normed_one = low(layer_norm(embedded, gain_bias[0], gain_bias[1]))
    qkv_bias = jnp.concatenate([gain_bias[7], jnp.zeros_like(gain_bias[7]), gain_bias[8]])
    qkv_rows = low(low_back(matmul(normed_one, qkv_w) + qkv_bias))
    queries = qkv_rows[:, :D].reshape(PACK_LEN, HEADS, HEAD_DIM)
    keys_part = qkv_rows[:, D:2 * D].reshape(PACK_LEN, HEADS, HEAD_DIM)
    values_part = qkv_rows[:, 2 * D:].reshape(PACK_LEN, HEADS, HEAD_DIM)
    scores = low_back(jnp.einsum('she,khe->hsk', queries, keys_part, precision=HIGHEST_PREC) * HEAD_DIM ** (-0.5))
    allowed = (image_ids[:, None] == image_ids[None, :]) & kept[None, :]
    scores = jnp.where(allowed[None], scores, -1e+30)
    exp_scores = jnp.exp(scores - lax.optimization_barrier(jnp.max(scores, axis=2, keepdims=True)))
    attn_probs = exp_scores / lax.optimization_barrier(jnp.sum(exp_scores, axis=2, keepdims=True))
    attn_rows = jnp.einsum('hsk,khe->she', low(attn_probs), values_part, precision=HIGHEST_PREC).reshape(PACK_LEN, D)
    attn_rows = low(low_back(attn_rows))
    after_attn = embedded + low_back(matmul(attn_rows, output_w) + gain_bias[9])
    normed_two = low(layer_norm(after_attn, gain_bias[2], gain_bias[3]))
    up_rows = low_back(matmul(normed_two, up_w) + gain_bias[11:15].reshape(-1))
    active = low(jax.nn.gelu(up_rows, approximate=False))
    after_mlp = after_attn + low_back(matmul(active, down_w.T) + gain_bias[10])
    final_rows = layer_norm(after_mlp, gain_bias[4], gain_bias[5])
    member = ((image_ids[None, :] == jnp.arange(IMG_PACK, dtype=jnp.int32)[:, None]) & kept[None, :]).astype(jnp.float32)
    return matmul(member, final_rows) / lax.optimization_barrier(jnp.sum(member, axis=1))[:, None]

def total_loss(weights, patch_rows, lengths, keep_mask, labels):
    rounded = tuple((low(weight) for weight in weights))
    layer_params = rounded[:6]

    def one_pack(carried, operands):
        return (carried, jax.checkpoint(pack_forward)(layer_params, *operands))
    _, pooled = lax.scan(one_pack, None, (patch_rows, lengths, keep_mask))
    pooled_low = low(pooled.reshape(-1, D))
    logits = low_back(matmul(pooled_low, rounded[6]) + rounded[7])
    class_range = jnp.arange(LABELS_PAD, dtype=jnp.int32)
    valid = (class_range < LABELS).astype(jnp.float32)
    target = (labels.reshape(-1)[:, None] == class_range[None, :]).astype(jnp.float32)
    return jnp.sum(valid[None, :] * (jax.nn.softplus(logits) - target * logits)) / IMAGES

def reference(patches, lengths, keep_mask, labels, step_count, embed_weight, embed_first, embed_second, qkv_weight, qkv_moment, output_weight, output_moment, up_weight, up_moment, down_weight, down_moment, small_params, small_first, small_second, head_weight, head_first, head_second, head_bias, bias_first, bias_second):
    patch_rows = patches.astype(jnp.float32)
    params = (embed_weight, qkv_weight, output_weight, up_weight, down_weight, small_params, head_weight, head_bias)
    loss_value, pullback = jax.vjp(lambda *weights: total_loss(weights, patch_rows, lengths, keep_mask, labels), *params)
    grads = pullback(jnp.ones((), jnp.float32))
    grad_norm = jnp.sqrt(sum((jnp.sum(grad_item * grad_item) for grad_item in grads)))
    factor = jnp.minimum(1.0, CLIP_NORM / (grad_norm + 1e-06))

    def muon_update(weight, moment, gradient):
        new_moment = MUON_MU * moment + factor * gradient
        iterate = new_moment / (jnp.sqrt(jnp.sum(new_moment * new_moment)) + 1e-07)
        for iteration in range(NS_STEPS):
            gram_mat = matmul(iterate, iterate.T)
            first_pass = matmul(gram_mat, iterate)
            iterate = COEF_ONE * iterate + COEF_TWO * first_pass + COEF_THREE * matmul(gram_mat, first_pass)
        col_ratio = math.sqrt(max(1.0, weight.shape[1] / weight.shape[0]))
        return (weight * (1.0 - MUON_RATE * DECAY) - MUON_RATE * col_ratio * iterate, new_moment)
    count_float = step_count[0].astype(jnp.float32)

    def adam_update(weight, first_moment, second_moment, gradient):
        scaled = factor * gradient
        new_first = BETA_ONE * first_moment + (1.0 - BETA_ONE) * scaled
        new_second = BETA_TWO * second_moment + (1.0 - BETA_TWO) * scaled * scaled
        first_hat = new_first / (1.0 - jnp.power(BETA_ONE, count_float))
        second_hat = new_second / (1.0 - jnp.power(BETA_TWO, count_float))
        new_weight = weight - ADAM_RATE * (first_hat / (jnp.sqrt(second_hat) + 1e-08) + DECAY * weight)
        return (new_weight, new_first, new_second)
    new_embed, new_embed_first, new_embed_second = adam_update(embed_weight, embed_first, embed_second, grads[0])
    new_qkv, new_qkv_moment = muon_update(qkv_weight, qkv_moment, grads[1])
    new_output, new_output_moment = muon_update(output_weight, output_moment, grads[2])
    new_up, new_up_moment = muon_update(up_weight, up_moment, grads[3])
    new_down, new_down_moment = muon_update(down_weight, down_moment, grads[4])
    new_small, new_small_first, new_small_second = adam_update(small_params, small_first, small_second, grads[5])
    new_head, new_head_first, new_head_second = adam_update(head_weight, head_first, head_second, grads[6])
    new_bias, new_bias_first, new_bias_second = adam_update(head_bias, bias_first, bias_second, grads[7])
    return (loss_value, grad_norm, new_embed, new_embed_first, new_embed_second, new_qkv, new_qkv_moment, new_output, new_output_moment, new_up, new_up_moment, new_down, new_down_moment, new_small, new_small_first, new_small_second, new_head, new_head_first, new_head_second, new_bias, new_bias_first, new_bias_second)
```

```python
import math

import jax
import jax.numpy as jnp
from jax import lax
from jax.experimental import pallas as pl
from jax.experimental.pallas import tpu as pltpu
from jax.sharding import PartitionSpec as P

HEAD_DIM = 64
LABELS = 21843
PACK_LEN = 1024
MAXLEN = 128
NS_STEPS = 2
BLOCK = 128
PAIR = 2 * HEAD_DIM

HIGHEST_PREC = lax.Precision.HIGHEST
NS_PREC = lax.Precision.HIGH
CLIP_NORM = 1.0
MUON_MU = 0.95
MUON_RATE = 1.0
ADAM_RATE = 0.02
BETA_ONE = 0.9
BETA_TWO = 0.95
DECAY = 0.01
COEF_ONE = 3.4445
COEF_TWO = -4.775
COEF_THREE = 2.0315
SCALE = HEAD_DIM ** (-0.5)
LOW = jnp.bfloat16
F32 = jnp.float32
NEG = -1e30


def swap(value, axis, bit):
    return lax.ppermute(value, axis, [(i, i ^ bit) for i in range(lax.axis_size(axis))])


def pick(value, index, dim=0):
    return lax.dynamic_index_in_dim(value, index, dim, keepdims=False)


def tree_sum(parts):
    while len(parts) > 1:
        parts = [parts[i] + parts[i + 1] for i in range(0, len(parts), 2)]
    return parts[0]


def relative(value, axis):
    return [value] + [swap(value, axis, k) for k in range(1, lax.axis_size(axis))]


def absolute(parts, place):
    return [_choose(parts, place, j) for j in range(len(parts))]


def _choose(parts, place, j):
    out = parts[j]
    for other in range(1, len(parts)):
        out = jnp.where(place == other, parts[j ^ other], out)
    return out


def all_sum(value, axis):
    return tree_sum(relative(value, axis))


def pack_bits(order):
    count = lax.axis_size("pack")
    bits = [1 << b for b in reversed(range(count.bit_length() - 1))]
    others = [b for b in bits if b > 1]
    return bits, (others if order == 0 else others[::-1])


def gather_rows(shard, order):
    seq_place, pack_place = lax.axis_index("seq"), lax.axis_index("pack")
    bits, others = pack_bits(order)
    whole = jnp.concatenate(absolute(relative(shard, "seq"), seq_place), axis=0)
    whole = whole.reshape((1,) * len(bits) + whole.shape)
    for bit in others + [1]:
        dim = bits.index(bit)
        other = swap(whole, "pack", bit)
        whole = jnp.where(
            (pack_place & bit) == 0,
            jnp.concatenate([whole, other], axis=dim),
            jnp.concatenate([other, whole], axis=dim),
        )
    return whole.reshape(-1, shard.shape[1])


def halve(value, bits, order):
    pack_place = lax.axis_index("pack")
    _, others = pack_bits(order)
    left = list(bits)
    for bit in [1] + others:
        dim = left.index(bit)
        mine = (pack_place & bit) // bit
        value = pick(value, mine, dim) + swap(pick(value, 1 - mine, dim), "pack", bit)
        left.remove(bit)
    return value


def scatter_rows(grad, order):
    seq_count, seq_place = lax.axis_size("seq"), lax.axis_index("seq")
    bits, _ = pack_bits(order)
    count = lax.axis_size("pack") * seq_count
    value = grad.reshape((2,) * len(bits) + (seq_count, grad.shape[0] // count, grad.shape[1]))
    value = halve(value, bits, order)
    parts = [pick(value, seq_place)]
    parts += [swap(pick(value, seq_place ^ k), "seq", k) for k in range(1, seq_count)]
    return tree_sum(parts)


def pack_sum(value, order):
    pack_place = lax.axis_index("pack")
    bits, others = pack_bits(order)
    rows = value.shape[0] >> len(bits)
    part = halve(value.reshape((2,) * len(bits) + (rows, value.shape[1])), bits, order)
    part = part.reshape((1,) * len(bits) + part.shape)
    for bit in others[::-1] + [1]:
        dim = bits.index(bit)
        other = swap(part, "pack", bit)
        part = jnp.where(
            (pack_place & bit) == 0,
            jnp.concatenate([part, other], axis=dim),
            jnp.concatenate([other, part], axis=dim),
        )
    return part.reshape(value.shape)


def _dot(left, right, dims):
    return lax.dot_general(left, right, (dims, ((), ())), preferred_element_type=F32)


NT = ((1,), (1,))
TN = ((0,), (0,))
NN = ((1,), (0,))


def _window(ref, block, blocks, column):
    places = (jnp.maximum(block - 1, 0), block, jnp.minimum(block + 1, blocks - 1))
    return jnp.concatenate(
        [ref[pl.ds(pl.multiple_of(place * BLOCK, BLOCK), BLOCK), column : column + PAIR] for place in places],
        axis=0,
    )


def _halves(value):
    lane = lax.broadcasted_iota(jnp.int32, value.shape, 1)
    zero = jnp.zeros_like(value)
    return jnp.where(lane < HEAD_DIM, value, zero), jnp.where(lane < HEAD_DIM, zero, value)


def _merge(low, high):
    return jnp.concatenate([low[:HEAD_DIM], high[HEAD_DIM:]], axis=0).T


def attend_kernel(width, blocks, rows_ref, query_id_ref, key_id_ref, out_ref, log_ref):
    block = pl.program_id(0)
    allowed = key_id_ref[pl.ds(pl.multiple_of(block * BLOCK, BLOCK), 3 * BLOCK), :] == query_id_ref[0]
    here = pl.ds(pl.multiple_of(block * BLOCK, BLOCK), BLOCK)
    for pair in range(width // PAIR):
        column = pair * PAIR
        queries = _halves(rows_ref[here, column : column + PAIR] * SCALE)
        keys = _window(rows_ref, block, blocks, width + column)
        values = _window(rows_ref, block, blocks, 2 * width + column)
        mixed = []
        for half in range(2):
            scores = jnp.where(allowed, _dot(keys, queries[half], NT), NEG)
            top = jnp.max(scores, axis=0, keepdims=True)
            raised = jnp.exp(scores - top)
            total = jnp.sum(raised, axis=0, keepdims=True)
            probs = (raised * (1.0 / total)).astype(LOW)
            mixed.append(_dot(values, probs, TN))
            log_ref[0, 2 * pair + half : 2 * pair + half + 1, :] = top + jnp.log(total)
        out_ref[:, column : column + PAIR] = _merge(*mixed).astype(LOW)


def attend_back_kernel(
    width, blocks, rows_ref, grad_ref, log_ref, query_id_ref, key_id_ref, out_ref, key_sum, value_sum
):
    block = pl.program_id(0)

    @pl.when(block == 0)
    def _():
        key_sum[...] = jnp.zeros_like(key_sum)
        value_sum[...] = jnp.zeros_like(value_sum)

    span = pl.ds(pl.multiple_of(block * BLOCK, BLOCK), 3 * BLOCK)
    here = pl.ds(pl.multiple_of(block * BLOCK, BLOCK), BLOCK)
    allowed = key_id_ref[span, :] == query_id_ref[0]
    for pair in range(width // PAIR):
        column = pair * PAIR
        queries = _halves(rows_ref[here, column : column + PAIR] * SCALE)
        grads = _halves(grad_ref[here, column : column + PAIR])
        keys = _window(rows_ref, block, blocks, width + column)
        values = _window(rows_ref, block, blocks, 2 * width + column)
        probs_low, grad_scores, query_grads = [], [], []
        for half in range(2):
            scores = jnp.where(allowed, _dot(keys, queries[half], NT), NEG)
            probs = jnp.exp(scores - log_ref[0, 2 * pair + half : 2 * pair + half + 1, :])
            grad_probs = _dot(values, grads[half], NT)
            inner = jnp.sum(probs * grad_probs, axis=0, keepdims=True)
            grad_score = (probs * (grad_probs - inner)).astype(LOW)
            probs_low.append(probs.astype(LOW))
            grad_scores.append(grad_score)
            query_grads.append(_dot(keys, grad_score, TN))
        out_ref[here, column : column + PAIR] = (_merge(*query_grads) * SCALE).astype(LOW)
        lanes = slice(column, column + PAIR)
        key_sum[span, lanes] += _dot(
            jnp.concatenate(grad_scores, axis=1), jnp.concatenate(queries, axis=0), NN
        )
        value_sum[span, lanes] += _dot(
            jnp.concatenate(probs_low, axis=1), jnp.concatenate(grads, axis=0), NN
        )

    @pl.when(block == blocks - 1)
    def _():
        def write(place, carry):
            into = pl.ds(pl.multiple_of(place * BLOCK, BLOCK), BLOCK)
            source = pl.ds(pl.multiple_of((place + 1) * BLOCK, BLOCK), BLOCK)
            out_ref[into, width : 2 * width] = key_sum[source, :].astype(LOW)
            out_ref[into, 2 * width :] = value_sum[source, :].astype(LOW)
            return carry

        lax.fori_loop(0, blocks, write, 0)


def _params():
    return pltpu.CompilerParams(dimension_semantics=("arbitrary",), vmem_limit_bytes=56 << 20)


def attend(qkv_rows, query_id, key_id):
    rows, triple = qkv_rows.shape
    width, blocks = triple // 3, rows // BLOCK
    heads = width // HEAD_DIM
    return pl.pallas_call(
        lambda *refs: attend_kernel(width, blocks, *refs),
        grid=(blocks,),
        in_specs=[
            pl.BlockSpec((rows, triple), lambda i: (0, 0)),
            pl.BlockSpec((1, 1, BLOCK), lambda i: (i, 0, 0)),
            pl.BlockSpec((rows + 2 * BLOCK, 1), lambda i: (0, 0)),
        ],
        out_specs=[
            pl.BlockSpec((BLOCK, width), lambda i: (i, 0)),
            pl.BlockSpec((1, heads, BLOCK), lambda i: (i, 0, 0)),
        ],
        out_shape=[
            jax.ShapeDtypeStruct((rows, width), LOW),
            jax.ShapeDtypeStruct((blocks, heads, BLOCK), F32),
        ],
        compiler_params=_params(),
        cost_estimate=pl.CostEstimate(
            flops=4 * rows * 3 * BLOCK * triple, bytes_accessed=8 * rows * width, transcendentals=rows * 3 * BLOCK * heads
        ),
    )(qkv_rows, query_id, key_id)


def attend_back(qkv_rows, grad_rows, log_total, query_id, key_id):
    rows, triple = qkv_rows.shape
    width, blocks = triple // 3, rows // BLOCK
    heads = width // HEAD_DIM
    return pl.pallas_call(
        lambda *refs: attend_back_kernel(width, blocks, *refs),
        grid=(blocks,),
        in_specs=[
            pl.BlockSpec((rows, triple), lambda i: (0, 0)),
            pl.BlockSpec((rows, width), lambda i: (0, 0)),
            pl.BlockSpec((1, heads, BLOCK), lambda i: (i, 0, 0)),
            pl.BlockSpec((1, 1, BLOCK), lambda i: (i, 0, 0)),
            pl.BlockSpec((rows + 2 * BLOCK, 1), lambda i: (0, 0)),
        ],
        out_specs=pl.BlockSpec((rows, triple), lambda i: (0, 0)),
        out_shape=jax.ShapeDtypeStruct((rows, triple), LOW),
        scratch_shapes=[
            pltpu.VMEM((rows + 2 * BLOCK, width), F32),
            pltpu.VMEM((rows + 2 * BLOCK, width), F32),
        ],
        compiler_params=_params(),
        cost_estimate=pl.CostEstimate(
            flops=10 * rows * 3 * BLOCK * triple, bytes_accessed=16 * rows * width, transcendentals=rows * 3 * BLOCK * heads
        ),
    )(qkv_rows, grad_rows, log_total, query_id, key_id)


def layer_norm(values, gain_row, bias_row):
    centre = values - jnp.mean(values, axis=-1, keepdims=True)
    spread = jnp.mean(centre * centre, axis=-1, keepdims=True)
    return centre * lax.rsqrt(spread + 1e-06) * gain_row + bias_row


def norm_back(values, gain_row, bias_row, cotangent):
    _, pullback = jax.vjp(layer_norm, values, gain_row, bias_row)
    return pullback(cotangent)


def gelu(values):
    return 0.5 * values * (1.0 + lax.erf(values * math.sqrt(0.5)))


def gelu_slope(values):
    return 0.5 * (1.0 + lax.erf(values * math.sqrt(0.5))) + values * (
        math.sqrt(0.5 / math.pi) * jnp.exp(-0.5 * values * values)
    )


def mm(spec, left, right):
    return jnp.einsum(spec, left, right, preferred_element_type=F32)


def column_sum(rows):
    return jnp.sum(rows.astype(F32), axis=0)


def hmul(left, right):
    return jnp.dot(left, right, precision=NS_PREC, preferred_element_type=F32)


def ortho(columns):
    gram_mat = pack_sum(
        lax.dot_general(columns, columns, (TN, ((), ())), precision=NS_PREC, preferred_element_type=F32), 0
    )
    scale = 1.0 / (jnp.sqrt(jnp.trace(gram_mat)) + 1e-07)
    iterate = columns * scale
    gram_mat = gram_mat * scale * scale
    eye = jnp.eye(gram_mat.shape[0], dtype=F32)
    for step in range(NS_STEPS):
        if step < NS_STEPS - 1:
            square = hmul(gram_mat, gram_mat)
            poly = COEF_ONE * eye + COEF_TWO * gram_mat + COEF_THREE * square
            poly_gram = COEF_ONE * gram_mat + COEF_TWO * square + COEF_THREE * hmul(square, gram_mat)
            iterate = hmul(iterate, poly)
            gram_mat = hmul(poly, poly_gram)
        else:
            first_pass = hmul(iterate, gram_mat)
            iterate = COEF_ONE * iterate + COEF_TWO * first_pass + COEF_THREE * hmul(first_pass, gram_mat)
    return iterate


def muon(moments):
    seq_count, seq_place = lax.axis_size("seq"), lax.axis_index("seq")
    most = max(m.shape[0] for m in moments)
    filled = [jnp.pad(m, ((0, most - m.shape[0]), (0, 0))) for m in moments]
    filled += [jnp.zeros_like(filled[0])] * (seq_count - len(moments))
    stacked = jnp.stack(filled)
    parts = [pick(stacked, seq_place)]
    parts += [swap(pick(stacked, seq_place ^ k), "seq", k) for k in range(1, seq_count)]
    done = ortho(jnp.concatenate(parts, axis=0)).reshape(stacked.shape)
    back = [done[0]] + [swap(done[k], "seq", k) for k in range(1, seq_count)]
    return [_choose(back, seq_place, m)[: moments[m].shape[0]] for m in range(len(moments))]


def muon_update(weight, iterate):
    col_ratio = math.sqrt(
        max(1.0, iterate.shape[1] * lax.axis_size(("pack", "seq")) / weight.shape[0])
    )
    return weight * (1.0 - MUON_RATE * DECAY) - MUON_RATE * col_ratio * iterate


def adam_update(weight, first_moment, second_moment, gradient, factor, count_float):
    scaled = factor * gradient
    new_first = BETA_ONE * first_moment + (1.0 - BETA_ONE) * scaled
    new_second = BETA_TWO * second_moment + (1.0 - BETA_TWO) * scaled * scaled
    first_hat = new_first / (1.0 - jnp.power(BETA_ONE, count_float))
    second_hat = new_second / (1.0 - jnp.power(BETA_TWO, count_float))
    new_weight = weight - ADAM_RATE * (first_hat / (jnp.sqrt(second_hat) + 1e-08) + DECAY * weight)
    return (new_weight, new_first, new_second)


def deal_rows(lengths, keep_mask, shard_len):
    packs, images = lengths.shape
    seq_count, seq_place = lax.axis_size("seq"), lax.axis_index("seq")
    image_range = jnp.arange(images, dtype=jnp.int32)
    upto = image_range[None, :] <= image_range[:, None]
    ends = jnp.sum(jnp.where(upto[None], lengths[:, None, :], 0), axis=2, dtype=jnp.int32)
    starts = ends - lengths
    cuts = jnp.arange(1, seq_count, dtype=jnp.int32) * shard_len
    straddles = (starts[:, None, :] < cuts[None, :, None]) & (ends[:, None, :] > cuts[None, :, None])
    behind = jnp.sum(jnp.where(straddles, cuts[None, :, None] - starts[:, None, :], 0), axis=2, dtype=jnp.int32)
    ahead = jnp.sum(jnp.where(straddles, ends[:, None, :] - cuts[None, :, None], 0), axis=2, dtype=jnp.int32)
    excess = jnp.zeros_like(cuts)
    moves = []
    for pack in range(packs):
        more, less = excess + ahead[pack], excess - behind[pack]
        forward = jnp.abs(more) <= jnp.abs(less)
        excess = jnp.where(forward, more, less)
        moves.append(jnp.where(forward, ahead[pack], -behind[pack]))
    borders = jnp.concatenate(
        [
            jnp.zeros((packs, 1), jnp.int32),
            cuts[None, :] + jnp.stack(moves),
            jnp.full((packs, 1), PACK_LEN, jnp.int32),
        ],
        axis=1,
    )
    first = lax.dynamic_index_in_dim(borders, seq_place, 1, keepdims=False)
    held = lax.dynamic_index_in_dim(borders, seq_place + 1, 1, keepdims=False) - first
    pack_range = jnp.arange(packs, dtype=jnp.int32)
    before = jnp.sum(jnp.where(pack_range[None, :] < pack_range[:, None], held[None, :], 0), axis=1, dtype=jnp.int32)
    row = jnp.arange(packs * shard_len + MAXLEN, dtype=jnp.int32)
    in_pack = (row[:, None] >= before[None, :]) & (row[:, None] < (before + held)[None, :])
    valid = jnp.any(in_pack, axis=1)

    def of_pack(values):
        return jnp.sum(jnp.where(in_pack, values, 0), axis=1, dtype=jnp.int32)

    pack_of = of_pack(pack_range[None, :])
    place = of_pack(row[:, None] - before[None, :] + first[None, :])
    window = shard_len + 2 * MAXLEN
    source = jnp.where(valid, pack_of * window + place - (seq_place * shard_len - MAXLEN), -1)
    row_ends = jnp.sum(jnp.where(in_pack[:, :, None], ends[None], 0), axis=1, dtype=jnp.int32)
    row_starts = jnp.sum(jnp.where(in_pack[:, :, None], starts[None], 0), axis=1, dtype=jnp.int32)
    image_of = jnp.sum((place[:, None] >= row_ends).astype(jnp.int32), axis=1, dtype=jnp.int32)
    is_first = jnp.any(place[:, None] == row_starts, axis=1)
    keep_rows = mm("rp,pj->rj", in_pack.astype(LOW), (keep_mask > 0).astype(LOW))
    spot = jnp.arange(PACK_LEN, dtype=jnp.int32)
    kept = jnp.any((place[:, None] == spot[None, :]) & (keep_rows > 0.5), axis=1)
    live = valid & (kept | is_first)
    group = jnp.where(valid, pack_of * images + image_of, -1)

    spots = jnp.arange(PACK_LEN, dtype=jnp.int32)[None, None, :]
    inside = (spots >= starts[:, :, None]) & (spots < ends[:, :, None])
    counted = inside & ((keep_mask > 0)[:, None, :] | (spots == starts[:, :, None]))
    counts = jnp.sum(counted.astype(F32), axis=2)
    return source, group, live, counts.reshape(-1)


def body(
    patches,
    lengths,
    keep_mask,
    labels,
    step_count,
    embed_weight,
    embed_first,
    embed_second,
    qkv_weight,
    qkv_moment,
    output_weight,
    output_moment,
    up_weight,
    up_moment,
    down_weight,
    down_moment,
    small_params,
    small_first,
    small_second,
    head_weight,
    head_first,
    head_second,
    head_bias,
    bias_first,
    bias_second,
):
    packs, shard_len, patch_in = patches.shape
    images = lengths.shape[1]
    width = qkv_weight.shape[0]
    seq_count, seq_place = lax.axis_size("seq"), lax.axis_index("seq")
    pack_count, pack_place = lax.axis_size("pack"), lax.axis_index("pack")
    small_rows = small_params.shape[0]

    embed_pack = jnp.concatenate(
        [embed_weight.T, jnp.pad(small_params.T, ((0, 0), (0, BLOCK - small_rows)))], axis=1
    ).astype(LOW)
    embed_pack = gather_rows(embed_pack, 0)
    embed_full, small_full = embed_pack[:, :patch_in], embed_pack[:, patch_in : patch_in + small_rows]
    gain_bias = small_full.astype(F32).T
    qkv_full = gather_rows(qkv_weight.T.astype(LOW), 1)
    output_full = gather_rows(output_weight.T.astype(LOW), 0)
    up_shard, down_shard, _ = lax.optimization_barrier(
        (up_weight.T.astype(LOW), down_weight.T.astype(LOW), qkv_full)
    )
    up_full = gather_rows(up_shard, 0)
    down_full = gather_rows(down_shard, 1)

    ends = seq_count - 1
    from_left = lax.ppermute(patches[:, shard_len - MAXLEN :], "seq", [(i, i + 1) for i in range(ends)])
    from_right = lax.ppermute(patches[:, :MAXLEN], "seq", [(i + 1, i) for i in range(ends)])
    window = jnp.concatenate([from_left, patches, from_right], axis=1).reshape(-1, patch_in)
    source, group, live, counts = deal_rows(lengths, keep_mask, shard_len)
    chosen = (source[:, None] == jnp.arange(window.shape[0], dtype=jnp.int32)[None, :]).astype(LOW)
    tokens = mm("rw,wi->ri", chosen, window).astype(LOW)
    rows = tokens.shape[0]
    query_id = group.reshape(rows // BLOCK, 1, BLOCK)
    key_id = jnp.pad(jnp.where(live, group, -2), (BLOCK, BLOCK), constant_values=-2)[:, None]
    group_count = packs * images
    member = (
        (group[None, :] == jnp.arange(group_count, dtype=jnp.int32)[:, None]) & live[None, :]
    ).astype(F32)

    head_parts = relative(head_weight.astype(LOW), "seq")
    bias_full = jnp.concatenate(absolute(relative(head_bias.astype(LOW), "seq"), seq_place), axis=0)

    embedded = mm("ri,di->rd", tokens, embed_full) + gain_bias[6]
    normed_one = layer_norm(embedded, gain_bias[0], gain_bias[1]).astype(LOW)
    qkv_bias = jnp.concatenate([gain_bias[7], jnp.zeros_like(gain_bias[7]), gain_bias[8]])
    qkv_rows = (mm("rd,ed->re", normed_one, qkv_full) + qkv_bias).astype(LOW)
    attn_low, log_total = attend(qkv_rows, query_id, key_id)
    after_attn = embedded + mm("re,de->rd", attn_low, output_full) + gain_bias[9]
    normed_two = layer_norm(after_attn, gain_bias[2], gain_bias[3]).astype(LOW)
    up_rows = mm("rd,fd->rf", normed_two, up_full) + gain_bias[11:15].reshape(-1)
    active = gelu(up_rows).astype(LOW)
    after_mlp = after_attn + mm("rf,fd->rd", active, down_full) + gain_bias[10]
    final_rows = layer_norm(after_mlp, gain_bias[4], gain_bias[5])
    pool_sums = jnp.dot(member, final_rows, precision=HIGHEST_PREC, preferred_element_type=F32)
    pooled_mine = (pool_sums / counts[:, None]).astype(LOW)

    img_share = group_count // seq_count
    split = pooled_mine.reshape(seq_count, img_share, width)
    pooled_low = tree_sum(
        [pick(split, seq_place).astype(F32)]
        + [swap(pick(split, seq_place ^ k), "seq", k).astype(F32) for k in range(1, seq_count)]
    ).astype(LOW)
    pooled_rows = jnp.concatenate(relative(pooled_low, "pack"), axis=0)
    depth = head_weight.shape[0]
    head_full = jnp.concatenate(absolute(head_parts, seq_place), axis=0)
    label_cols = head_full.shape[1]
    logits = mm("nd,dc->nc", pooled_rows, head_full) + bias_full.astype(F32)
    label_rows = jnp.take(
        pick(labels.reshape(pack_count, seq_count, img_share), seq_place, 1),
        jnp.arange(pack_count, dtype=jnp.int32) ^ pack_place,
        axis=0,
    ).reshape(-1)
    class_ids = pack_place * label_cols + jnp.arange(label_cols, dtype=jnp.int32)
    valid = (class_ids < LABELS).astype(F32)
    target = (label_rows[:, None] == class_ids[None, :]).astype(F32)
    image_total = labels.shape[0] * labels.shape[1]
    loss_part = jnp.sum(valid[None, :] * (jax.nn.softplus(logits) - target * logits)) / image_total
    grad_logits = (valid[None, :] * (jax.nn.sigmoid(logits) - target) / image_total).astype(LOW)
    pooled_part = mm("nc,dc->nd", grad_logits, head_full).reshape(pack_count, img_share, width)
    pooled_grad = tree_sum(
        [pooled_part[0]] + [swap(pooled_part[k], "pack", k) for k in range(1, pack_count)]
    )
    pooled_grad = jnp.concatenate(absolute(relative(pooled_grad, "seq"), seq_place), axis=0)
    pooled_grad = pooled_grad / counts[:, None]

    all_pooled = jnp.concatenate(
        [pick(part.reshape(-1, seq_count, depth), seq_place, 1) for part in relative(pooled_rows, "seq")], axis=0
    )
    all_logits = jnp.concatenate(relative(grad_logits, "seq"), axis=0)
    head_grad = mm("nd,nc->dc", all_pooled, all_logits)
    bias_grad = pick(column_sum(all_logits).reshape(seq_count, -1), seq_place)

    grad_final = lax.dot_general(
        member, pooled_grad, (TN, ((), ())), precision=HIGHEST_PREC, preferred_element_type=F32
    )
    grad_mlp, grad_gain_f, grad_bias_f = norm_back(after_mlp, gain_bias[4], gain_bias[5], grad_final)
    grad_mlp_low = grad_mlp.astype(LOW)
    down_share = scatter_rows(mm("rf,rd->fd", active, grad_mlp_low), 0)
    grad_upper = (mm("rd,fd->rf", grad_mlp_low, down_full) * gelu_slope(up_rows)).astype(LOW)
    up_share = scatter_rows(mm("rf,rd->fd", grad_upper, normed_two), 1)
    grad_two, grad_gain_2, grad_bias_2 = norm_back(
        after_attn, gain_bias[2], gain_bias[3], mm("rf,fd->rd", grad_upper, up_full)
    )
    grad_attn = grad_mlp + grad_two
    grad_attn_low = grad_attn.astype(LOW)
    output_share = scatter_rows(mm("rd,re->de", grad_attn_low, attn_low), 0)
    grad_mixed = mm("rd,de->re", grad_attn_low, output_full).astype(LOW)
    grad_qkv = attend_back(qkv_rows, grad_mixed, log_total, query_id, key_id)
    qkv_share = scatter_rows(mm("re,rd->ed", grad_qkv, normed_one), 1)
    qkv_bias_grad = column_sum(grad_qkv)
    grad_one, grad_gain_1, grad_bias_1 = norm_back(
        embedded, gain_bias[0], gain_bias[1], mm("re,ed->rd", grad_qkv, qkv_full)
    )
    grad_embed_rows = (grad_attn + grad_one).astype(LOW)
    small_grad = jnp.concatenate(
        [
            jnp.stack(
                [
                    grad_gain_1,
                    grad_bias_1,
                    grad_gain_2,
                    grad_bias_2,
                    grad_gain_f,
                    grad_bias_f,
                    column_sum(grad_embed_rows),
                    qkv_bias_grad[:width],
                    qkv_bias_grad[2 * width :],
                    column_sum(grad_attn_low),
                    column_sum(grad_mlp_low),
                ]
            ),
            column_sum(grad_upper).reshape(-1, width),
        ],
        axis=0,
    )
    embed_grad = jnp.concatenate(
        [
            mm("rd,ri->di", grad_embed_rows, tokens),
            jnp.pad(small_grad, ((0, BLOCK - small_rows), (0, 0))).T,
        ],
        axis=1,
    )
    embed_pack_share = scatter_rows(embed_grad, 0)
    embed_share = embed_pack_share[:, :patch_in].T
    small_share = embed_pack_share[:, patch_in : patch_in + small_rows].T

    shares = (qkv_share, output_share, up_share, down_share, embed_share, small_share, head_grad, bias_grad)
    square_sum = sum((jnp.sum(piece * piece) for piece in shares))
    sums = jnp.broadcast_to(jnp.stack([loss_part, square_sum])[:, None], (2, BLOCK))
    sums = all_sum(all_sum(sums, "pack"), "seq")
    loss_value, square_total = sums[0, 0], sums[1, 0]
    grad_norm = jnp.sqrt(square_total)
    factor = jnp.minimum(1.0, CLIP_NORM / (grad_norm + 1e-06))
    moments = (
        MUON_MU * qkv_moment.T + factor * qkv_share,
        MUON_MU * output_moment.T + factor * output_share,
        MUON_MU * up_moment.T + factor * up_share,
        MUON_MU * down_moment.T + factor * down_share,
    )
    iterates = [iterate.T for iterate in muon(moments)]
    new_qkv = muon_update(qkv_weight, iterates[0])
    new_output = muon_update(output_weight, iterates[1])
    new_up = muon_update(up_weight, iterates[2])
    new_down = muon_update(down_weight, iterates[3])
    moments = [moment.T for moment in moments]
    count_float = step_count[0].astype(F32)
    new_embed, new_embed_first, new_embed_second = adam_update(
        embed_weight, embed_first, embed_second, embed_share, factor, count_float
    )
    new_small, new_small_first, new_small_second = adam_update(
        small_params, small_first, small_second, small_share, factor, count_float
    )
    new_head, new_head_first, new_head_second = adam_update(
        head_weight, head_first, head_second, head_grad, factor, count_float
    )
    new_bias, new_bias_first, new_bias_second = adam_update(
        head_bias, bias_first, bias_second, bias_grad, factor, count_float
    )
    return (
        loss_value,
        grad_norm,
        new_embed,
        new_embed_first,
        new_embed_second,
        new_qkv,
        moments[0],
        new_output,
        moments[1],
        new_up,
        moments[2],
        new_down,
        moments[3],
        new_small,
        new_small_first,
        new_small_second,
        new_head,
        new_head_first,
        new_head_second,
        new_bias,
        new_bias_first,
        new_bias_second,
    )


def solution(mesh):
    both = P(None, ("pack", "seq"))
    head = P("seq", "pack")
    line = P(("pack", "seq"))
    return jax.shard_map(
        body,
        mesh=mesh,
        in_specs=(P("pack", "seq", None), P("pack", None), P("pack", None), P(), P())
        + (both,) * 14
        + (head,) * 3
        + (line,) * 3,
        out_specs=(P(), P()) + (both,) * 14 + (head,) * 3 + (line,) * 3,
        check_vma=False,
    )
```

```python
import math

import jax
import jax.numpy as jnp
from jax import lax
from jax.experimental import pallas as pl
from jax.experimental.pallas import tpu as pltpu
from jax.sharding import PartitionSpec as P

HEAD_DIM = 64
LABELS = 21843
PACK_LEN = 1024
MAXLEN = 128
NS_STEPS = 2
BLOCK = 128
PAIR = 2 * HEAD_DIM

HIGHEST_PREC = lax.Precision.HIGHEST
NS_PREC = lax.Precision.HIGH
CLIP_NORM = 1.0
MUON_MU = 0.95
MUON_RATE = 1.0
ADAM_RATE = 0.02
BETA_ONE = 0.9
BETA_TWO = 0.95
DECAY = 0.01
COEF_ONE = 3.4445
COEF_TWO = -4.775
COEF_THREE = 2.0315
SCALE = HEAD_DIM ** (-0.5)
LOW = jnp.bfloat16
F32 = jnp.float32
NEG = -1e30


def swap(value, axis, bit):
    return lax.ppermute(value, axis, [(i, i ^ bit) for i in range(lax.axis_size(axis))])


def pick(value, index, dim=0):
    return lax.dynamic_index_in_dim(value, index, dim, keepdims=False)


def tree_sum(parts):
    while len(parts) > 1:
        parts = [parts[i] + parts[i + 1] for i in range(0, len(parts), 2)]
    return parts[0]


def relative(value, axis):
    return [value] + [swap(value, axis, k) for k in range(1, lax.axis_size(axis))]


def absolute(parts, place):
    return [_choose(parts, place, j) for j in range(len(parts))]


def _choose(parts, place, j):
    out = parts[j]
    for other in range(1, len(parts)):
        out = jnp.where(place == other, parts[j ^ other], out)
    return out


def all_sum(value, axis):
    return tree_sum(relative(value, axis))


def hold(*values):
    return lax.optimization_barrier(values)


def other_chips():
    return list(range(2, lax.axis_size("pack"), 2))


def relative_packs():
    same = [0] + other_chips()
    return jnp.array(same + [k + 1 for k in same], jnp.int32)


def relative_slots():
    count = lax.axis_size("pack")
    offset = lax.axis_index("pack") ^ jnp.arange(count, dtype=jnp.int32)
    return (offset >> 1) + (offset & 1) * (count // 2)


def gather_blocks(block):
    own = jnp.stack([block] + [swap(block, "pack", k) for k in other_chips()])
    return own, swap(own, "pack", 1)


def by_index(parts, place):
    if len(parts) <= 8:
        return jnp.stack(absolute(parts, place))
    value = jnp.stack(parts)
    shape, bit = value.shape, 1
    while bit < len(parts):
        value = value.reshape((-1, 2, bit) + shape[1:])
        turned = jnp.concatenate([value[:, 1:], value[:, :1]], axis=1)
        value = jnp.where((place & bit) == 0, value, turned)
        bit *= 2
    return value.reshape(shape)


def by_core(own, other, dim):
    return jnp.where(
        (lax.axis_index("pack") & 1) == 0, jnp.stack([own, other], axis=dim), jnp.stack([other, own], axis=dim)
    )


class Gather:
    def __init__(self, shard):
        self.shard = shard

    def along_seq(self):
        self.block = by_index(relative(self.shard, "seq"), lax.axis_index("seq"))
        return self.block

    def in_plane(self):
        self.parts = list(hold(self.block, *[swap(self.block, "pack", k) for k in other_chips()]))
        return self.parts[-1]

    def whole(self):
        mine = by_index(self.parts, lax.axis_index("pack") >> 1)
        cells = by_core(mine, swap(mine, "pack", 1), 1)
        return cells.reshape((-1,) + self.shard.shape)

    def halves(self):
        own = jnp.stack(self.parts)
        return own, swap(own, "pack", 1)


class Scatter:
    def __init__(self, order, width, relative=False):
        count = lax.axis_size("pack")
        self.left = [1 << b for b in reversed(range(count.bit_length() - 1))]
        chips = [b for b in self.left if b > 1]
        self.order = [1] + (chips if order == 0 else chips[::-1])
        self.relative, self.width = relative, width

    def start(self, grad):
        self.value = grad.reshape((2,) * len(self.left) + (lax.axis_size("seq"), -1, self.width))
        return self.send()

    def start_halves(self, keep, send):
        self.left.remove(1)
        self.order.remove(1)
        shape = (2,) * len(self.left) + (lax.axis_size("seq"), -1, self.width)
        self.bit, self.keep = 1, keep.reshape(shape)
        return send.reshape(shape)

    def start_joined(self, value):
        self.left.remove(1)
        self.order.remove(1)
        self.value = value
        return self.send()

    def send(self):
        self.bit = self.order.pop(0)
        dim = self.left.index(self.bit)
        self.left.remove(self.bit)
        if self.relative:
            self.keep = lax.index_in_dim(self.value, 0, dim, keepdims=False)
            return lax.index_in_dim(self.value, 1, dim, keepdims=False)
        mine = (lax.axis_index("pack") & self.bit) // self.bit
        self.keep = pick(self.value, mine, dim)
        return pick(self.value, 1 - mine, dim)

    def join(self, sent):
        self.value = self.keep + swap(sent, "pack", self.bit)

    def step(self, sent):
        self.join(sent)
        return self.send() if self.order else None

    def finish(self):
        value, count = self.value, lax.axis_size("seq")
        tail = value.shape[1:]
        bit = 1
        while bit < count:
            mine = (lax.axis_index("seq") & bit) // bit
            value = value.reshape((-1, 2) + tail)
            value = pick(value, mine, 1) + swap(pick(value, 1 - mine, 1), "seq", bit)
            bit *= 2
        return value.reshape(tail)


def late_halves(qkv_grad, output_grad):
    seq_count, pack_count = lax.axis_size("seq"), lax.axis_size("pack")
    chips = (2,) * (pack_count.bit_length() - 2)
    core = lax.axis_index("pack") & 1

    def half(which):
        pieces = [
            pick(grad.reshape(chips + (2, seq_count, -1, grad.shape[1])), which, len(chips))
            for grad in (qkv_grad, output_grad)
        ]
        return jnp.concatenate(pieces, axis=-2)

    return half(core), half(1 - core)


def pack_scatter(value):
    half = value.shape[0] // 2
    mine = value[:half] + swap(value[half:], "pack", 1)
    parts = [mine[0]] + [swap(mine[k // 2], "pack", k) for k in other_chips()]
    return tree_sum(parts)


def pack_sum(value):
    pack_place, count = lax.axis_index("pack"), lax.axis_size("pack")
    core = pack_place & 1
    split = value.reshape(count // 2, 2, -1, value.shape[1])
    mine = pick(split, core, 1) + swap(pick(split, 1 - core, 1), "pack", 1)
    chip = pack_place >> 1
    parts = [pick(mine, chip)] + [swap(pick(mine, chip ^ (k // 2)), "pack", k) for k in other_chips()]
    total = tree_sum(parts)
    mine = by_index([total] + [swap(total, "pack", k) for k in other_chips()], chip)
    return by_core(mine, swap(mine, "pack", 1), 1).reshape(value.shape)


def sum_all(value):
    value = value + swap(value, "pack", 1)
    value = tree_sum([value] + [swap(value, "pack", k) for k in other_chips()])
    return all_sum(value, "seq")


def _dot(left, right, dims):
    return lax.dot_general(left, right, (dims, ((), ())), preferred_element_type=F32)


NT = ((1,), (1,))
TN = ((0,), (0,))
NN = ((1,), (0,))


def _window(ref, block, blocks, column):
    places = (jnp.maximum(block - 1, 0), block, jnp.minimum(block + 1, blocks - 1))
    return jnp.concatenate(
        [ref[pl.ds(pl.multiple_of(place * BLOCK, BLOCK), BLOCK), column : column + PAIR] for place in places],
        axis=0,
    )


def _halves(value):
    lane = lax.broadcasted_iota(jnp.int32, value.shape, 1)
    zero = jnp.zeros_like(value)
    return jnp.where(lane < HEAD_DIM, value, zero), jnp.where(lane < HEAD_DIM, zero, value)


def _merge(low, high):
    return jnp.concatenate([low[:HEAD_DIM], high[HEAD_DIM:]], axis=0).T


def attend_kernel(width, blocks, rows_ref, query_id_ref, key_id_ref, out_ref, log_ref):
    block = pl.program_id(0)
    allowed = key_id_ref[pl.ds(pl.multiple_of(block * BLOCK, BLOCK), 3 * BLOCK), :] == query_id_ref[0]
    here = pl.ds(pl.multiple_of(block * BLOCK, BLOCK), BLOCK)
    for pair in range(width // PAIR):
        column = pair * PAIR
        queries = _halves(rows_ref[here, column : column + PAIR] * SCALE)
        keys = _window(rows_ref, block, blocks, width + column)
        values = _window(rows_ref, block, blocks, 2 * width + column)
        mixed = []
        for half in range(2):
            scores = jnp.where(allowed, _dot(keys, queries[half], NT), NEG)
            top = jnp.max(scores, axis=0, keepdims=True)
            raised = jnp.exp(scores - top)
            total = jnp.sum(raised, axis=0, keepdims=True)
            probs = (raised * (1.0 / total)).astype(LOW)
            mixed.append(_dot(values, probs, TN))
            log_ref[0, 2 * pair + half : 2 * pair + half + 1, :] = top + jnp.log(total)
        out_ref[:, column : column + PAIR] = _merge(*mixed).astype(LOW)


def attend_back_kernel(
    width, blocks, rows_ref, grad_ref, log_ref, query_id_ref, key_id_ref, out_ref, key_sum, value_sum
):
    block = pl.program_id(0)

    @pl.when(block == 0)
    def _():
        key_sum[...] = jnp.zeros_like(key_sum)
        value_sum[...] = jnp.zeros_like(value_sum)

    span = pl.ds(pl.multiple_of(block * BLOCK, BLOCK), 3 * BLOCK)
    here = pl.ds(pl.multiple_of(block * BLOCK, BLOCK), BLOCK)
    allowed = key_id_ref[span, :] == query_id_ref[0]
    for pair in range(width // PAIR):
        column = pair * PAIR
        queries = _halves(rows_ref[here, column : column + PAIR] * SCALE)
        grads = _halves(grad_ref[here, column : column + PAIR])
        keys = _window(rows_ref, block, blocks, width + column)
        values = _window(rows_ref, block, blocks, 2 * width + column)
        probs_low, grad_scores, query_grads = [], [], []
        for half in range(2):
            scores = jnp.where(allowed, _dot(keys, queries[half], NT), NEG)
            probs = jnp.exp(scores - log_ref[0, 2 * pair + half : 2 * pair + half + 1, :])
            grad_probs = _dot(values, grads[half], NT)
            inner = jnp.sum(probs * grad_probs, axis=0, keepdims=True)
            grad_score = (probs * (grad_probs - inner)).astype(LOW)
            probs_low.append(probs.astype(LOW))
            grad_scores.append(grad_score)
            query_grads.append(_dot(keys, grad_score, TN))
        out_ref[here, column : column + PAIR] = (_merge(*query_grads) * SCALE).astype(LOW)
        lanes = slice(column, column + PAIR)
        key_sum[span, lanes] += _dot(
            jnp.concatenate(grad_scores, axis=1), jnp.concatenate(queries, axis=0), NN
        )
        value_sum[span, lanes] += _dot(
            jnp.concatenate(probs_low, axis=1), jnp.concatenate(grads, axis=0), NN
        )

    @pl.when(block == blocks - 1)
    def _():
        def write(place, carry):
            into = pl.ds(pl.multiple_of(place * BLOCK, BLOCK), BLOCK)
            source = pl.ds(pl.multiple_of((place + 1) * BLOCK, BLOCK), BLOCK)
            out_ref[into, width : 2 * width] = key_sum[source, :].astype(LOW)
            out_ref[into, 2 * width :] = value_sum[source, :].astype(LOW)
            return carry

        lax.fori_loop(0, blocks, write, 0)


def _params():
    return pltpu.CompilerParams(dimension_semantics=("arbitrary",), vmem_limit_bytes=56 << 20)


def attend(qkv_rows, query_id, key_id):
    rows, triple = qkv_rows.shape
    width, blocks = triple // 3, rows // BLOCK
    heads = width // HEAD_DIM
    return pl.pallas_call(
        lambda *refs: attend_kernel(width, blocks, *refs),
        grid=(blocks,),
        in_specs=[
            pl.BlockSpec((rows, triple), lambda i: (0, 0)),
            pl.BlockSpec((1, 1, BLOCK), lambda i: (i, 0, 0)),
            pl.BlockSpec((rows + 2 * BLOCK, 1), lambda i: (0, 0)),
        ],
        out_specs=[
            pl.BlockSpec((BLOCK, width), lambda i: (i, 0)),
            pl.BlockSpec((1, heads, BLOCK), lambda i: (i, 0, 0)),
        ],
        out_shape=[
            jax.ShapeDtypeStruct((rows, width), LOW),
            jax.ShapeDtypeStruct((blocks, heads, BLOCK), F32),
        ],
        compiler_params=_params(),
        cost_estimate=pl.CostEstimate(
            flops=4 * rows * 3 * BLOCK * triple, bytes_accessed=8 * rows * width, transcendentals=rows * 3 * BLOCK * heads
        ),
    )(qkv_rows, query_id, key_id)


def attend_back(qkv_rows, grad_rows, log_total, query_id, key_id):
    rows, triple = qkv_rows.shape
    width, blocks = triple // 3, rows // BLOCK
    heads = width // HEAD_DIM
    return pl.pallas_call(
        lambda *refs: attend_back_kernel(width, blocks, *refs),
        grid=(blocks,),
        in_specs=[
            pl.BlockSpec((rows, triple), lambda i: (0, 0)),
            pl.BlockSpec((rows, width), lambda i: (0, 0)),
            pl.BlockSpec((1, heads, BLOCK), lambda i: (i, 0, 0)),
            pl.BlockSpec((1, 1, BLOCK), lambda i: (i, 0, 0)),
            pl.BlockSpec((rows + 2 * BLOCK, 1), lambda i: (0, 0)),
        ],
        out_specs=pl.BlockSpec((rows, triple), lambda i: (0, 0)),
        out_shape=jax.ShapeDtypeStruct((rows, triple), LOW),
        scratch_shapes=[
            pltpu.VMEM((rows + 2 * BLOCK, width), F32),
            pltpu.VMEM((rows + 2 * BLOCK, width), F32),
        ],
        compiler_params=_params(),
        cost_estimate=pl.CostEstimate(
            flops=10 * rows * 3 * BLOCK * triple, bytes_accessed=16 * rows * width, transcendentals=rows * 3 * BLOCK * heads
        ),
    )(qkv_rows, grad_rows, log_total, query_id, key_id)


def layer_norm(values, gain_row, bias_row):
    centre = values - jnp.mean(values, axis=-1, keepdims=True)
    spread = jnp.mean(centre * centre, axis=-1, keepdims=True)
    return centre * lax.rsqrt(spread + 1e-06) * gain_row + bias_row


def norm_back(values, gain_row, bias_row, cotangent):
    _, pullback = jax.vjp(layer_norm, values, gain_row, bias_row)
    return pullback(cotangent)


def gelu(values):
    return 0.5 * values * (1.0 + lax.erf(values * math.sqrt(0.5)))


def gelu_slope(values):
    return 0.5 * (1.0 + lax.erf(values * math.sqrt(0.5))) + values * (
        math.sqrt(0.5 / math.pi) * jnp.exp(-0.5 * values * values)
    )


def as_rows(value, width):
    flat = value.reshape(1, -1)
    return jnp.pad(flat, ((0, 7), (0, width - flat.shape[1])))


def from_rows(cells, shape):
    rows, columns = shape
    flat = cells[:, 0, : rows * columns].reshape(-1, rows, columns)
    return flat.transpose(1, 0, 2).reshape(rows, -1)


def mm(spec, left, right):
    return jnp.einsum(spec, left, right, preferred_element_type=F32)


def column_sum(rows):
    return jnp.sum(rows.astype(F32), axis=0)


def hmul(left, right):
    return jnp.dot(left, right, precision=NS_PREC, preferred_element_type=F32)


def ortho(columns):
    gram_mat = pack_sum(
        lax.dot_general(columns, columns, (TN, ((), ())), precision=NS_PREC, preferred_element_type=F32)
    )
    scale = 1.0 / (jnp.sqrt(jnp.trace(gram_mat)) + 1e-07)
    iterate = columns * scale
    gram_mat = gram_mat * scale * scale
    eye = jnp.eye(gram_mat.shape[0], dtype=F32)
    for step in range(NS_STEPS):
        if step < NS_STEPS - 1:
            square = hmul(gram_mat, gram_mat)
            poly = COEF_ONE * eye + COEF_TWO * gram_mat + COEF_THREE * square
            poly_gram = COEF_ONE * gram_mat + COEF_TWO * square + COEF_THREE * hmul(square, gram_mat)
            iterate = hmul(iterate, poly)
            gram_mat = hmul(poly, poly_gram)
        else:
            first_pass = hmul(iterate, gram_mat)
            iterate = COEF_ONE * iterate + COEF_TWO * first_pass + COEF_THREE * hmul(first_pass, gram_mat)
    return iterate


def to_planes(shards):
    seq_count, seq_place = lax.axis_size("seq"), lax.axis_index("seq")
    most = max(m.shape[0] for m in shards)
    filled = [jnp.pad(m, ((0, most - m.shape[0]), (0, 0))) for m in shards]
    filled += [jnp.zeros_like(filled[0])] * (seq_count - len(shards))
    stacked = jnp.stack(filled)
    parts = [pick(stacked, seq_place)]
    parts += [swap(pick(stacked, seq_place ^ k), "seq", k) for k in range(1, seq_count)]
    return jnp.stack(parts)


def from_planes(value, counts):
    back = [value[0]] + [swap(value[k], "seq", k) for k in range(1, lax.axis_size("seq"))]
    return [_choose(back, lax.axis_index("seq"), m)[:count] for m, count in enumerate(counts)]


def muon_update(weight, iterate):
    col_ratio = math.sqrt(
        max(1.0, iterate.shape[1] * lax.axis_size(("pack", "seq")) / weight.shape[0])
    )
    return weight * (1.0 - MUON_RATE * DECAY) - MUON_RATE * col_ratio * iterate


def adam_update(weight, first_moment, second_moment, gradient, factor, count_float):
    scaled = factor * gradient
    new_first = BETA_ONE * first_moment + (1.0 - BETA_ONE) * scaled
    new_second = BETA_TWO * second_moment + (1.0 - BETA_TWO) * scaled * scaled
    first_hat = new_first / (1.0 - jnp.power(BETA_ONE, count_float))
    second_hat = new_second / (1.0 - jnp.power(BETA_TWO, count_float))
    new_weight = weight - ADAM_RATE * (first_hat / (jnp.sqrt(second_hat) + 1e-08) + DECAY * weight)
    return (new_weight, new_first, new_second)


def deal_rows(lengths, keep_mask, shard_len):
    packs, images = lengths.shape
    seq_count, seq_place = lax.axis_size("seq"), lax.axis_index("seq")
    image_range = jnp.arange(images, dtype=jnp.int32)
    upto = image_range[None, :] <= image_range[:, None]
    ends = jnp.sum(jnp.where(upto[None], lengths[:, None, :], 0), axis=2, dtype=jnp.int32)
    starts = ends - lengths
    cuts = jnp.arange(1, seq_count, dtype=jnp.int32) * shard_len
    straddles = (starts[:, None, :] < cuts[None, :, None]) & (ends[:, None, :] > cuts[None, :, None])
    behind = jnp.sum(jnp.where(straddles, cuts[None, :, None] - starts[:, None, :], 0), axis=2, dtype=jnp.int32)
    ahead = jnp.sum(jnp.where(straddles, ends[:, None, :] - cuts[None, :, None], 0), axis=2, dtype=jnp.int32)
    excess = jnp.zeros_like(cuts)
    moves = []
    for pack in range(packs):
        more, less = excess + ahead[pack], excess - behind[pack]
        forward = jnp.abs(more) <= jnp.abs(less)
        excess = jnp.where(forward, more, less)
        moves.append(jnp.where(forward, ahead[pack], -behind[pack]))
    borders = jnp.concatenate(
        [
            jnp.zeros((packs, 1), jnp.int32),
            cuts[None, :] + jnp.stack(moves),
            jnp.full((packs, 1), PACK_LEN, jnp.int32),
        ],
        axis=1,
    )
    first = lax.dynamic_index_in_dim(borders, seq_place, 1, keepdims=False)
    held = lax.dynamic_index_in_dim(borders, seq_place + 1, 1, keepdims=False) - first
    pack_range = jnp.arange(packs, dtype=jnp.int32)
    before = jnp.sum(jnp.where(pack_range[None, :] < pack_range[:, None], held[None, :], 0), axis=1, dtype=jnp.int32)
    row = jnp.arange(packs * shard_len + MAXLEN, dtype=jnp.int32)
    in_pack = (row[:, None] >= before[None, :]) & (row[:, None] < (before + held)[None, :])
    valid = jnp.any(in_pack, axis=1)

    def of_pack(values):
        return jnp.sum(jnp.where(in_pack, values, 0), axis=1, dtype=jnp.int32)

    pack_of = of_pack(pack_range[None, :])
    place = of_pack(row[:, None] - before[None, :] + first[None, :])
    window = shard_len + 2 * MAXLEN
    source = jnp.where(valid, pack_of * window + place - (seq_place * shard_len - MAXLEN), -1)
    row_ends = jnp.sum(jnp.where(in_pack[:, :, None], ends[None], 0), axis=1, dtype=jnp.int32)
    row_starts = jnp.sum(jnp.where(in_pack[:, :, None], starts[None], 0), axis=1, dtype=jnp.int32)
    image_of = jnp.sum((place[:, None] >= row_ends).astype(jnp.int32), axis=1, dtype=jnp.int32)
    is_first = jnp.any(place[:, None] == row_starts, axis=1)
    keep_rows = mm("rp,pj->rj", in_pack.astype(LOW), (keep_mask > 0).astype(LOW))
    spot = jnp.arange(PACK_LEN, dtype=jnp.int32)
    kept = jnp.any((place[:, None] == spot[None, :]) & (keep_rows > 0.5), axis=1)
    live = valid & (kept | is_first)
    group = jnp.where(valid, pack_of * images + image_of, -1)

    spots = jnp.arange(PACK_LEN, dtype=jnp.int32)[None, None, :]
    inside = (spots >= starts[:, :, None]) & (spots < ends[:, :, None])
    counted = inside & ((keep_mask > 0)[:, None, :] | (spots == starts[:, :, None]))
    counts = jnp.sum(counted.astype(F32), axis=2)
    return source, group, live, counts.reshape(-1)


def body(
    patches,
    lengths,
    keep_mask,
    labels,
    step_count,
    embed_weight,
    embed_first,
    embed_second,
    qkv_weight,
    qkv_moment,
    output_weight,
    output_moment,
    up_weight,
    up_moment,
    down_weight,
    down_moment,
    small_params,
    small_first,
    small_second,
    head_weight,
    head_first,
    head_second,
    head_bias,
    bias_first,
    bias_second,
):
    packs, shard_len, patch_in = patches.shape
    images = lengths.shape[1]
    width = qkv_weight.shape[0]
    seq_count, seq_place = lax.axis_size("seq"), lax.axis_index("seq")
    pack_count, pack_place = lax.axis_size("pack"), lax.axis_index("pack")
    small_rows = small_params.shape[0]

    bundle = [embed_weight.T, qkv_weight.T, as_rows(small_params, width), as_rows(head_bias, width)]
    spots = [0]
    for piece in bundle:
        spots.append(spots[-1] + piece.shape[0])
    first = Gather(jnp.concatenate([piece.astype(LOW) for piece in bundle]))
    first_block = first.along_seq()
    patches, first_there = hold(patches, first_block)
    first_plane = first.in_plane()
    second_shard, _ = hold(
        jnp.concatenate([up_weight.T.astype(LOW), output_weight.T.astype(LOW)]), first_there
    )
    second = Gather(second_shard)
    second.along_seq()
    second.block, _ = hold(second.block, first_plane)
    cells = first.whole()
    embed_full, qkv_full, small_full, bias_full = (
        cells[:, here:there] for here, there in zip(spots[:-1], spots[1:])
    )
    embed_full, qkv_full = embed_full.reshape(-1, width), qkv_full.reshape(-1, width)
    gain_bias = from_rows(small_full, small_params.shape).astype(F32)
    bias_full = lax.dynamic_slice_in_dim(bias_full, pack_place * seq_count, seq_count, 0)
    bias_full = bias_full[:, 0, : head_bias.shape[0]].reshape(-1)
    third_shard, _ = hold(down_weight.T.astype(LOW), second.block)
    third = Gather(third_shard)
    third_block = third.along_seq()
    second_plane = second.in_plane()
    third.block, _ = hold(third.block, second_plane)
    head_shard, _ = hold(head_weight.astype(LOW), third_block)
    head_full = lax.all_gather(head_shard, "seq", axis=0, tiled=True)
    hidden = up_weight.shape[1]
    own, other = second.halves()
    up_full = [half[:, :, :hidden].reshape(-1, width) for half in (own, other)]
    by_chip = by_index([own[k, :, hidden:] for k in range(own.shape[0])], pack_place >> 1)
    other_chip = by_index([other[k, :, hidden:] for k in range(own.shape[0])], pack_place >> 1)
    output_full = by_core(by_chip, other_chip, 1).reshape(-1, width)
    third.in_plane()
    down_full = [half.reshape(-1, width) for half in third.halves()]

    ends = seq_count - 1
    from_left = lax.ppermute(patches[:, shard_len - MAXLEN :], "seq", [(i, i + 1) for i in range(ends)])
    from_right = lax.ppermute(patches[:, :MAXLEN], "seq", [(i + 1, i) for i in range(ends)])
    window = jnp.concatenate([from_left, patches, from_right], axis=1).reshape(-1, patch_in)
    source, group, live, counts = deal_rows(lengths, keep_mask, shard_len)
    chosen = (source[:, None] == jnp.arange(window.shape[0], dtype=jnp.int32)[None, :]).astype(LOW)
    tokens = mm("rw,wi->ri", chosen, window).astype(LOW)
    rows = tokens.shape[0]
    query_id = group.reshape(rows // BLOCK, 1, BLOCK)
    key_id = jnp.pad(jnp.where(live, group, -2), (BLOCK, BLOCK), constant_values=-2)[:, None]
    group_count = packs * images
    member = (
        (group[None, :] == jnp.arange(group_count, dtype=jnp.int32)[:, None]) & live[None, :]
    ).astype(F32)

    embedded = mm("ri,di->rd", tokens, embed_full) + gain_bias[6]
    normed_one = layer_norm(embedded, gain_bias[0], gain_bias[1]).astype(LOW)
    qkv_bias = jnp.concatenate([gain_bias[7], jnp.zeros_like(gain_bias[7]), gain_bias[8]])
    qkv_rows = (mm("rd,ed->re", normed_one, qkv_full) + qkv_bias).astype(LOW)
    attn_low, log_total = attend(qkv_rows, query_id, key_id)
    after_attn = embedded + mm("re,de->rd", attn_low, output_full) + gain_bias[9]
    normed_two = layer_norm(after_attn, gain_bias[2], gain_bias[3]).astype(LOW)
    up_bias = jnp.take(
        gain_bias[11:15].reshape(pack_count, -1), relative_packs() ^ pack_place, axis=0
    ).reshape(2, -1)
    up_rows = [mm("rd,fd->rf", normed_two, up_full[half]) + up_bias[half] for half in range(2)]
    active = [gelu(rows).astype(LOW) for rows in up_rows]
    after_mlp = (
        after_attn
        + (mm("rf,fd->rd", active[0], down_full[0]) + mm("rf,fd->rd", active[1], down_full[1]))
        + gain_bias[10]
    )
    final_rows = layer_norm(after_mlp, gain_bias[4], gain_bias[5])
    pool_sums = jnp.dot(member, final_rows, precision=HIGHEST_PREC, preferred_element_type=F32)
    pooled_mine = (pool_sums / counts[:, None]).astype(LOW)

    img_share = group_count // seq_count
    split = pooled_mine.reshape(seq_count, img_share, width)
    pooled_low = tree_sum(
        [pick(split, seq_place).astype(F32)]
        + [swap(pick(split, seq_place ^ k), "seq", k).astype(F32) for k in range(1, seq_count)]
    ).astype(LOW)
    pooled_rows = jnp.concatenate(gather_blocks(pooled_low), axis=0).reshape(-1, width)
    depth = head_weight.shape[0]
    label_cols = head_full.shape[1]
    logits = mm("nd,dc->nc", pooled_rows, head_full) + bias_full.astype(F32)
    label_rows = jnp.take(
        pick(labels.reshape(pack_count, seq_count, img_share), seq_place, 1),
        relative_packs() ^ pack_place,
        axis=0,
    ).reshape(-1)
    class_ids = pack_place * label_cols + jnp.arange(label_cols, dtype=jnp.int32)
    valid = (class_ids < LABELS).astype(F32)
    target = (label_rows[:, None] == class_ids[None, :]).astype(F32)
    image_total = labels.shape[0] * labels.shape[1]
    loss_part = jnp.sum(valid[None, :] * (jax.nn.softplus(logits) - target * logits)) / image_total
    grad_logits = (valid[None, :] * (jax.nn.sigmoid(logits) - target) / image_total).astype(LOW)
    pooled_part = mm("nc,dc->nd", grad_logits, head_full).reshape(pack_count, img_share, width)
    pooled_grad = pack_scatter(pooled_part)
    pooled_grad = jnp.concatenate(absolute(relative(pooled_grad, "seq"), seq_place), axis=0)
    pooled_grad = pooled_grad / counts[:, None]

    traded, pooled_grad = hold(jnp.concatenate([pooled_rows, grad_logits], axis=1), pooled_grad)
    traded = lax.all_gather(traded, "seq", axis=0, tiled=True)

    grad_final = lax.dot_general(
        member, pooled_grad, (TN, ((), ())), precision=HIGHEST_PREC, preferred_element_type=F32
    )
    grad_mlp, grad_gain_f, grad_bias_f = norm_back(after_mlp, gain_bias[4], gain_bias[5], grad_final)
    grad_mlp_low = grad_mlp.astype(LOW)
    down_sum, up_sum = Scatter(0, width, True), Scatter(1, width, True)
    half = width // 2
    late_sums = [Scatter(0, half), Scatter(1, half)]
    last_sum = Scatter(0, width)
    down_out = mm("rf,rd->fd", active[1], grad_mlp_low)
    down_keep = mm("rf,rd->fd", active[0], grad_mlp_low)
    grad_mlp_low, down_out, down_keep = hold(grad_mlp_low, down_out, down_keep)
    down_out = down_sum.start_halves(down_keep, down_out)
    grad_upper = [
        (mm("rd,fd->rf", grad_mlp_low, down_full[side]) * gelu_slope(up_rows[side])).astype(LOW)
        for side in range(2)
    ]
    up_out = mm("rf,rd->fd", grad_upper[1], normed_two)
    up_keep = mm("rf,rd->fd", grad_upper[0], normed_two)
    grad_upper[0], grad_upper[1], up_out, up_keep = hold(*grad_upper, up_out, up_keep)
    up_out = up_sum.start_halves(up_keep, up_out)
    grad_normed = mm("rf,fd->rd", grad_upper[0], up_full[0]) + mm("rf,fd->rd", grad_upper[1], up_full[1])
    down_out = down_sum.step(down_out)
    grad_normed, down_out = hold(grad_normed, down_out)
    grad_two, grad_gain_2, grad_bias_2 = norm_back(after_attn, gain_bias[2], gain_bias[3], grad_normed)
    grad_attn = grad_mlp + grad_two
    grad_attn_low = grad_attn.astype(LOW)
    grad_mixed = mm("rd,de->re", grad_attn_low, output_full).astype(LOW)
    output_grad = mm("rd,re->de", grad_attn_low, attn_low)
    up_out = up_sum.step(up_out)
    muon_moments = [m.T for m in (qkv_moment, output_moment, up_moment, down_moment)]
    grad_mixed, up_out, *muon_moments = hold(grad_mixed, up_out, *muon_moments)
    old_columns = to_planes(muon_moments)
    grad_qkv = attend_back(qkv_rows, grad_mixed, log_total, query_id, key_id)
    grad_qkv, traded, old_columns = hold(grad_qkv, traded, old_columns)
    late_keep, late_out = late_halves(mm("re,rd->ed", grad_qkv, normed_one), output_grad)
    down_out, up_out = down_sum.step(down_out), up_sum.step(up_out)
    grad_qkv, late_out, down_out, up_out = hold(grad_qkv, late_out, down_out, up_out)
    qkv_bias_grad = column_sum(grad_qkv)
    grad_normed = mm("re,ed->rd", grad_qkv, qkv_full)
    late = late_keep + swap(late_out, "pack", 1)
    late_outs = [
        each.start_joined(part) for each, part in zip(late_sums, (late[..., :half], late[..., half:]))
    ]
    grad_normed, *late_outs = hold(grad_normed, *late_outs)
    grad_one, grad_gain_1, grad_bias_1 = norm_back(embedded, gain_bias[0], gain_bias[1], grad_normed)
    grad_embed_rows = (grad_attn + grad_one).astype(LOW)
    small_grad = jnp.concatenate(
        [
            jnp.stack(
                [
                    grad_gain_1,
                    grad_bias_1,
                    grad_gain_2,
                    grad_bias_2,
                    grad_gain_f,
                    grad_bias_f,
                    column_sum(grad_embed_rows),
                    qkv_bias_grad[:width],
                    qkv_bias_grad[2 * width :],
                    column_sum(grad_attn_low),
                    column_sum(grad_mlp_low),
                ]
            ),
            jnp.take(
                jnp.concatenate([column_sum(half) for half in grad_upper]).reshape(pack_count, -1),
                relative_slots(),
                axis=0,
            ).reshape(-1, width),
        ],
        axis=0,
    )
    devices = pack_count * seq_count
    small_cells = small_grad.reshape(small_rows, devices, -1).transpose(1, 0, 2).reshape(devices, 1, -1)
    last_cells = jnp.concatenate(
        [
            mm("rd,ri->di", grad_embed_rows, tokens).reshape(devices, -1, width),
            jnp.pad(small_cells, ((0, 0), (0, 7), (0, width - small_cells.shape[2]))),
        ],
        axis=1,
    )
    all_pooled = pick(traded[:, :width].reshape(-1, seq_count, head_weight.shape[0]), seq_place, 1)
    all_logits = traded[:, width:]
    head_grad = mm("nd,nc->dc", all_pooled, all_logits)
    bias_grad = pick(column_sum(all_logits).reshape(seq_count, -1), seq_place)
    going = [
        (down_sum, down_out),
        (up_sum, up_out),
        (late_sums[0], late_outs[0]),
        (late_sums[1], late_outs[1]),
        (last_sum, last_sum.start(last_cells)),
    ]
    while going:
        going = [(each, each.step(sent)) for each, sent in going]
        going = [(each, sent) for each, sent in going if sent is not None]
    down_share, up_share = down_sum.finish(), up_sum.finish()
    late_share = jnp.concatenate([each.finish() for each in late_sums], axis=1)
    qkv_share, output_share = late_share[: qkv_weight.shape[1]], late_share[qkv_weight.shape[1] :]
    last_share = last_sum.finish()
    embed_share = last_share[: embed_weight.shape[1]].T
    small_share = last_share[embed_weight.shape[1], : small_params.size].reshape(small_params.shape)

    shares = (qkv_share, output_share, up_share, down_share, embed_share, small_share, head_grad, bias_grad)
    square_sum = sum((jnp.sum(piece * piece) for piece in shares))
    sums = jnp.broadcast_to(jnp.stack([loss_part, square_sum])[:, None], (2, BLOCK))
    sums = sum_all(sums)
    loss_value, square_total = sums[0, 0], sums[1, 0]
    grad_norm = jnp.sqrt(square_total)
    factor = jnp.minimum(1.0, CLIP_NORM / (grad_norm + 1e-06))
    muon_shares = (qkv_share, output_share, up_share, down_share)
    columns = MUON_MU * old_columns + factor * to_planes(muon_shares)
    iterates = ortho(columns.reshape(-1, width)).reshape(columns.shape)
    iterates = [iterate.T for iterate in from_planes(iterates, [m.shape[0] for m in muon_moments])]
    moments = [
        (MUON_MU * moment + factor * share).T for moment, share in zip(muon_moments, muon_shares)
    ]
    new_qkv = muon_update(qkv_weight, iterates[0])
    new_output = muon_update(output_weight, iterates[1])
    new_up = muon_update(up_weight, iterates[2])
    new_down = muon_update(down_weight, iterates[3])
    count_float = step_count[0].astype(F32)
    new_embed, new_embed_first, new_embed_second = adam_update(
        embed_weight, embed_first, embed_second, embed_share, factor, count_float
    )
    new_small, new_small_first, new_small_second = adam_update(
        small_params, small_first, small_second, small_share, factor, count_float
    )
    new_head, new_head_first, new_head_second = adam_update(
        head_weight, head_first, head_second, head_grad, factor, count_float
    )
    new_bias, new_bias_first, new_bias_second = adam_update(
        head_bias, bias_first, bias_second, bias_grad, factor, count_float
    )
    return (
        loss_value,
        grad_norm,
        new_embed,
        new_embed_first,
        new_embed_second,
        new_qkv,
        moments[0],
        new_output,
        moments[1],
        new_up,
        moments[2],
        new_down,
        moments[3],
        new_small,
        new_small_first,
        new_small_second,
        new_head,
        new_head_first,
        new_head_second,
        new_bias,
        new_bias_first,
        new_bias_second,
    )


def solution(mesh):
    both = P(None, ("pack", "seq"))
    head = P("seq", "pack")
    line = P(("pack", "seq"))
    return jax.shard_map(
        body,
        mesh=mesh,
        in_specs=(P("pack", "seq", None), P("pack", None), P("pack", None), P(), P())
        + (both,) * 14
        + (head,) * 3
        + (line,) * 3,
        out_specs=(P(), P()) + (both,) * 14 + (head,) * 3 + (line,) * 3,
        check_vma=False,
    )
```

```python
import math

import jax
import jax.numpy as jnp
from jax import lax
from jax.experimental import pallas as pl
from jax.experimental.pallas import tpu as pltpu
from jax.sharding import PartitionSpec as P

HEAD_DIM = 64
LABELS = 21843
PACK_LEN = 1024
MAXLEN = 128
NS_STEPS = 2
BLOCK = 128
PAIR = 2 * HEAD_DIM

HIGHEST_PREC = lax.Precision.HIGHEST
NS_PREC = lax.Precision.HIGH
CLIP_NORM = 1.0
MUON_MU = 0.95
MUON_RATE = 1.0
ADAM_RATE = 0.02
BETA_ONE = 0.9
BETA_TWO = 0.95
DECAY = 0.01
COEF_ONE = 3.4445
COEF_TWO = -4.775
COEF_THREE = 2.0315
SCALE = HEAD_DIM ** (-0.5)
LOW = jnp.bfloat16
F32 = jnp.float32
NEG = -1e30
NO_COST = pl.CostEstimate(flops=0, bytes_accessed=0, transcendentals=0)


def swap(value, axis, bit):
    return lax.ppermute(value, axis, [(i, i ^ bit) for i in range(lax.axis_size(axis))])


def pick(value, index, dim=0):
    return lax.dynamic_index_in_dim(value, index, dim, keepdims=False)


def tree_sum(parts):
    while len(parts) > 1:
        parts = [parts[i] + parts[i + 1] for i in range(0, len(parts), 2)]
    return parts[0]


def relative(value, axis):
    return [value] + [swap(value, axis, k) for k in range(1, lax.axis_size(axis))]


def absolute(parts, place):
    return [_choose(parts, place, j) for j in range(len(parts))]


def _choose(parts, place, j):
    out = parts[j]
    for other in range(1, len(parts)):
        out = jnp.where(place == other, parts[j ^ other], out)
    return out


def all_sum(value, axis):
    return tree_sum(relative(value, axis))


def hold(*values):
    return lax.optimization_barrier(values)


def other_chips():
    return list(range(2, lax.axis_size("pack"), 2))


def relative_packs():
    same = [0] + other_chips()
    return jnp.array(same + [k + 1 for k in same], jnp.int32)


def relative_slots():
    count = lax.axis_size("pack")
    offset = lax.axis_index("pack") ^ jnp.arange(count, dtype=jnp.int32)
    return (offset >> 1) + (offset & 1) * (count // 2)


def gather_blocks(block):
    own = jnp.stack([block] + [swap(block, "pack", k) for k in other_chips()])
    return own, swap(own, "pack", 1)


def by_index(parts, place):
    if len(parts) <= 8:
        return jnp.stack(absolute(parts, place))
    value = jnp.stack(parts)
    shape, bit = value.shape, 1
    while bit < len(parts):
        value = value.reshape((-1, 2, bit) + shape[1:])
        turned = jnp.concatenate([value[:, 1:], value[:, :1]], axis=1)
        value = jnp.where((place & bit) == 0, value, turned)
        bit *= 2
    return value.reshape(shape)


def by_core(own, other, dim):
    return jnp.where(
        (lax.axis_index("pack") & 1) == 0, jnp.stack([own, other], axis=dim), jnp.stack([other, own], axis=dim)
    )


class Gather:
    def __init__(self, shard):
        self.shard = shard

    def along_seq(self):
        self.block = by_index(relative(self.shard, "seq"), lax.axis_index("seq"))
        return self.block

    def in_plane(self):
        self.parts = [self.block] + [swap(self.block, "pack", k) for k in other_chips()]

    def pieces(self, spots):
        own = jnp.stack(self.parts)
        other = swap(own, "pack", 1)
        chip = lax.axis_index("pack") >> 1
        found = []
        for here, there in zip(spots[:-1], spots[1:]):
            both = [
                by_index([half[k, :, here:there] for k in range(half.shape[0])], chip) for half in (own, other)
            ]
            found.append(by_core(*both, 1).reshape(-1, there - here, own.shape[-1]))
        return found

    def halves(self):
        own = jnp.stack(self.parts)
        return own, swap(own, "pack", 1)


class Scatter:
    def __init__(self, order, width, relative=False):
        self.left = [1 << b for b in reversed(range(lax.axis_size("pack").bit_length() - 1))]
        chips = [b for b in self.left if b > 1]
        self.order = [1] + (chips if order == 0 else chips[::-1])
        self.relative, self.width = relative, width

    def start_halves(self, keep, send):
        self.left.remove(1)
        self.bit = self.order.pop(0)
        shape = (2,) * len(self.left) + (lax.axis_size("seq"), -1, self.width)
        self.keep = keep.reshape(shape)
        return send.reshape(shape)

    def start_joined(self, value):
        self.left.remove(1)
        self.order.pop(0)
        self.value = value
        return self.send()

    def send(self):
        self.bit = bit = self.order.pop(0)
        dim = self.left.index(bit)
        self.left.remove(bit)
        if self.relative:
            self.keep = lax.index_in_dim(self.value, 0, dim, keepdims=False)
            return lax.index_in_dim(self.value, 1, dim, keepdims=False)
        mine = (lax.axis_index("pack") & bit) // bit
        self.keep = pick(self.value, mine, dim)
        return pick(self.value, 1 - mine, dim)

    def step(self, sent):
        self.value = self.keep + swap(sent, "pack", self.bit)
        return self.send() if self.order else None

    def finish(self, sent):
        while sent is not None:
            sent = self.step(sent)


class SeqScatter:
    def __init__(self, value):
        self.value, self.bit = value, 1

    def send(self):
        tail = self.value.shape[-2:]
        split = self.value.reshape((-1, 2) + tail)
        mine = (lax.axis_index("seq") & self.bit) // self.bit
        self.keep = pick(split, mine, 1)
        return pick(split, 1 - mine, 1)

    def step(self, sent):
        self.value = self.keep + swap(sent, "seq", self.bit)
        self.bit *= 2
        return self.send() if self.bit < lax.axis_size("seq") else None

    def result(self):
        return self.value.reshape(self.value.shape[-2:])


def late_halves(*grads):
    seq_count, pack_count = lax.axis_size("seq"), lax.axis_size("pack")
    chips = (2,) * (pack_count.bit_length() - 2)
    core = lax.axis_index("pack") & 1

    def half(which):
        pieces = [
            pick(grad.reshape(chips + (2, seq_count, -1, grad.shape[1])), which, len(chips)) for grad in grads
        ]
        return jnp.concatenate(pieces, axis=-2)

    return half(core), half(1 - core)


def pack_scatter(value):
    half = value.shape[0] // 2
    mine = value[:half] + swap(value[half:], "pack", 1)
    parts = [mine[0]] + [swap(mine[k // 2], "pack", k) for k in other_chips()]
    return tree_sum(parts)


def pack_sum(value):
    pack_place, count = lax.axis_index("pack"), lax.axis_size("pack")
    core = pack_place & 1
    split = value.reshape(count // 2, 2, -1, value.shape[1])
    mine = pick(split, core, 1) + swap(pick(split, 1 - core, 1), "pack", 1)
    chip = pack_place >> 1
    parts = [pick(mine, chip)] + [swap(pick(mine, chip ^ (k // 2)), "pack", k) for k in other_chips()]
    total = tree_sum(parts)
    mine = by_index([total] + [swap(total, "pack", k) for k in other_chips()], chip)
    return by_core(mine, swap(mine, "pack", 1), 1).reshape(value.shape)


def sum_plane(value):
    value = value + swap(value, "pack", 1)
    return tree_sum([value] + [swap(value, "pack", k) for k in other_chips()])


def _dot(left, right, dims):
    return lax.dot_general(left, right, (dims, ((), ())), preferred_element_type=F32)


NT = ((1,), (1,))
TN = ((0,), (0,))
NN = ((1,), (0,))


def _window(ref, block, blocks, column):
    places = (jnp.maximum(block - 1, 0), block, jnp.minimum(block + 1, blocks - 1))
    return jnp.concatenate(
        [ref[pl.ds(pl.multiple_of(place * BLOCK, BLOCK), BLOCK), column : column + PAIR] for place in places],
        axis=0,
    )


def _halves(value):
    lane = lax.broadcasted_iota(jnp.int32, value.shape, 1)
    zero = jnp.zeros_like(value)
    return jnp.concatenate(
        [jnp.where(lane < HEAD_DIM, value, zero), jnp.where(lane < HEAD_DIM, zero, value)], axis=0
    )


def _merge(value):
    return jnp.concatenate([value[:HEAD_DIM, :BLOCK], value[HEAD_DIM:, BLOCK:]], axis=0).T


def attend_kernel(width, blocks, rows_ref, query_id_ref, key_id_ref, out_ref, log_ref):
    block = pl.program_id(0)
    here = pl.ds(pl.multiple_of(block * BLOCK, BLOCK), BLOCK)
    allowed = key_id_ref[pl.ds(pl.multiple_of(block * BLOCK, BLOCK), 3 * BLOCK), :] == query_id_ref[0]
    for pair in range(width // PAIR):
        column = pair * PAIR
        queries = _halves(rows_ref[here, column : column + PAIR] * SCALE)
        keys = _window(rows_ref, block, blocks, width + column)
        values = _window(rows_ref, block, blocks, 2 * width + column)
        mixed = []
        for lanes in (slice(0, BLOCK), slice(BLOCK, 2 * BLOCK)):
            scores = jnp.where(allowed, _dot(keys, queries[lanes], NT), NEG)
            top = jnp.max(scores, axis=0, keepdims=True)
            raised = jnp.exp(scores - top)
            total = jnp.sum(raised, axis=0, keepdims=True)
            probs = (raised * (1.0 / total)).astype(LOW)
            log_ref[0, pair : pair + 1, lanes] = top + jnp.log(total)
            mixed.append(_dot(values, probs, TN))
        out_ref[:, column : column + PAIR] = _merge(jnp.concatenate(mixed, axis=1)).astype(LOW)


def attend_back_kernel(
    width, blocks, rows_ref, grad_ref, log_ref, query_id_ref, key_id_ref, out_ref, key_sum, value_sum
):
    block = pl.program_id(0)

    @pl.when(block == 0)
    def _():
        key_sum[...] = jnp.zeros_like(key_sum)
        value_sum[...] = jnp.zeros_like(value_sum)

    span = pl.ds(pl.multiple_of(block * BLOCK, BLOCK), 3 * BLOCK)
    here = pl.ds(pl.multiple_of(block * BLOCK, BLOCK), BLOCK)
    allowed = key_id_ref[span, :] == query_id_ref[0]
    allowed = jnp.concatenate([allowed, allowed], axis=1)
    for pair in range(width // PAIR):
        column = pair * PAIR
        lanes = slice(column, column + PAIR)
        queries = _halves(rows_ref[here, lanes] * SCALE)
        grads = _halves(grad_ref[here, lanes])
        keys = _window(rows_ref, block, blocks, width + column)
        values = _window(rows_ref, block, blocks, 2 * width + column)
        scores = jnp.where(allowed, _dot(keys, queries, NT), NEG)
        probs = jnp.exp(scores - log_ref[0, pair : pair + 1, :])
        grad_probs = _dot(values, grads, NT)
        inner = jnp.sum(probs * grad_probs, axis=0, keepdims=True)
        grad_scores = (probs * (grad_probs - inner)).astype(LOW)
        out_ref[here, lanes] = (_merge(_dot(keys, grad_scores, TN)) * SCALE).astype(LOW)
        key_sum[span, lanes] += _dot(grad_scores, queries, NN)
        value_sum[span, lanes] += _dot(probs.astype(LOW), grads, NN)

    @pl.when(block == blocks - 1)
    def _():
        def write(place, carry):
            into = pl.ds(pl.multiple_of(place * BLOCK, BLOCK), BLOCK)
            source = pl.ds(pl.multiple_of((place + 1) * BLOCK, BLOCK), BLOCK)
            out_ref[into, width : 2 * width] = key_sum[source, :].astype(LOW)
            out_ref[into, 2 * width :] = value_sum[source, :].astype(LOW)
            return carry

        lax.fori_loop(0, blocks, write, 0)


def _params():
    return pltpu.CompilerParams(dimension_semantics=("arbitrary",), vmem_limit_bytes=56 << 20)


def attend(qkv_rows, query_id, key_id):
    rows, triple = qkv_rows.shape
    width, blocks = triple // 3, rows // BLOCK
    heads = width // HEAD_DIM
    return pl.pallas_call(
        lambda *refs: attend_kernel(width, blocks, *refs),
        grid=(blocks,),
        in_specs=[
            pl.BlockSpec((rows, triple), lambda i: (0, 0)),
            pl.BlockSpec((1, 1, BLOCK), lambda i: (i, 0, 0)),
            pl.BlockSpec((rows + 2 * BLOCK, 1), lambda i: (0, 0)),
        ],
        out_specs=[
            pl.BlockSpec((BLOCK, width), lambda i: (i, 0)),
            pl.BlockSpec((1, heads // 2, 2 * BLOCK), lambda i: (i, 0, 0)),
        ],
        out_shape=[
            jax.ShapeDtypeStruct((rows, width), LOW),
            jax.ShapeDtypeStruct((blocks, heads // 2, 2 * BLOCK), F32),
        ],
        compiler_params=_params(),
        cost_estimate=NO_COST,
    )(qkv_rows, query_id, key_id)


def attend_back(qkv_rows, grad_rows, log_total, query_id, key_id):
    rows, triple = qkv_rows.shape
    width, blocks = triple // 3, rows // BLOCK
    heads = width // HEAD_DIM
    return pl.pallas_call(
        lambda *refs: attend_back_kernel(width, blocks, *refs),
        grid=(blocks,),
        in_specs=[
            pl.BlockSpec((rows, triple), lambda i: (0, 0)),
            pl.BlockSpec((rows, width), lambda i: (0, 0)),
            pl.BlockSpec((1, heads // 2, 2 * BLOCK), lambda i: (i, 0, 0)),
            pl.BlockSpec((1, 1, BLOCK), lambda i: (i, 0, 0)),
            pl.BlockSpec((rows + 2 * BLOCK, 1), lambda i: (0, 0)),
        ],
        out_specs=pl.BlockSpec((rows, triple), lambda i: (0, 0)),
        out_shape=jax.ShapeDtypeStruct((rows, triple), LOW),
        scratch_shapes=[
            pltpu.VMEM((rows + 2 * BLOCK, width), F32),
            pltpu.VMEM((rows + 2 * BLOCK, width), F32),
        ],
        compiler_params=_params(),
        cost_estimate=NO_COST,
    )(qkv_rows, grad_rows, log_total, query_id, key_id)


def layer_norm(values, gain_row, bias_row):
    centre = values - jnp.mean(values, axis=-1, keepdims=True)
    spread = jnp.mean(centre * centre, axis=-1, keepdims=True)
    return centre * lax.rsqrt(spread + 1e-06) * gain_row + bias_row


def norm_back_kernel(
    groups, keep_sum, values_ref, cot_ref, more_ref, gain_ref, low_ref, sum_ref, out_ref=None
):
    @pl.when(pl.program_id(0) == 0)
    def _():
        sum_ref[...] = jnp.zeros_like(sum_ref)

    values = values_ref[...]
    if groups:
        group = lax.broadcasted_iota(jnp.int32, (values.shape[0], groups), 1)
        chosen = jnp.where(more_ref[...] == group, 1.0, 0.0)
        cot = jnp.dot(chosen, cot_ref[...], precision=HIGHEST_PREC, preferred_element_type=F32)
    else:
        cot = cot_ref[...]
    centre = values - jnp.mean(values, axis=-1, keepdims=True)
    scale = lax.rsqrt(jnp.mean(centre * centre, axis=-1, keepdims=True) + 1e-06)
    normed = centre * scale
    scaled = cot * gain_ref[...]
    grad = scale * (
        scaled
        - jnp.mean(scaled, axis=-1, keepdims=True)
        - normed * jnp.mean(scaled * normed, axis=-1, keepdims=True)
    )
    if not groups:
        grad = grad + more_ref[...]
    low = grad.astype(LOW)
    if keep_sum:
        out_ref[...] = grad
    low_ref[...] = low
    for row, value in enumerate((cot * normed, cot, low.astype(F32))):
        sum_ref[row : row + 1, :] += jnp.sum(value, axis=0, keepdims=True)


def norm_back(values, gain_row, cotangent, more, keep_sum=True):
    rows, width = values.shape
    groups = cotangent.shape[0] if more.shape[1] == 1 else 0
    tile = rows // 8
    block = pl.BlockSpec((tile, width), lambda i: (i, 0))
    line = pl.BlockSpec((1, width), lambda i: (0, 0))
    out_specs = [block, pl.BlockSpec((8, width), lambda i: (0, 0))]
    out_shape = [jax.ShapeDtypeStruct((rows, width), LOW), jax.ShapeDtypeStruct((8, width), F32)]
    if keep_sum:
        out_specs.append(block)
        out_shape.append(jax.ShapeDtypeStruct((rows, width), F32))
    return pl.pallas_call(
        lambda *refs: norm_back_kernel(groups, keep_sum, *refs),
        grid=(8,),
        in_specs=[
            block,
            pl.BlockSpec((groups, width), lambda i: (0, 0)) if groups else block,
            pl.BlockSpec((tile, 1), lambda i: (i, 0)) if groups else block,
            line,
        ],
        out_specs=out_specs,
        out_shape=out_shape,
        compiler_params=_params(),
        cost_estimate=NO_COST,
    )(values, cotangent, more, gain_row[None])


def small_kernel(spots_ref, first_ref, second_ref, last_ref, qkv_ref, up_ref, out_ref):
    width, slots = out_ref.shape[1], spots_ref.shape[0]
    out_ref[...] = jnp.zeros_like(out_ref)
    rows = [(first_ref, 0), (first_ref, 1), (second_ref, 0), (second_ref, 1), (last_ref, 0), (last_ref, 1)]
    rows += [(first_ref, 2), (qkv_ref, 0), (qkv_ref, 2), (second_ref, 2), (last_ref, 2)]
    for row, (ref, which) in enumerate(rows):
        if ref is qkv_ref:
            out_ref[row : row + 1, :] = ref[:, which * width : (which + 1) * width]
        else:
            out_ref[row : row + 1, :] = ref[which : which + 1, :]
    for slot in range(slots):
        out_ref[pl.ds(16 + spots_ref[slot], 1), :] = up_ref[slot : slot + 1, :]


def small_sums(first, second, last, qkv_sum, up_sums):
    width, count = first.shape[1], lax.axis_size("pack")
    spots = relative_packs() ^ lax.axis_index("pack")
    up_sum = jnp.concatenate(up_sums).reshape(count, -1)
    arrays = [first, second, last, qkv_sum[None], jnp.pad(up_sum, ((0, 0), (0, width - up_sum.shape[1])))]
    return pl.pallas_call(
        small_kernel,
        in_specs=[pl.BlockSpec(memory_space=pltpu.SMEM)] + [pl.BlockSpec(memory_space=pltpu.VMEM)] * len(arrays),
        out_specs=pl.BlockSpec(memory_space=pltpu.VMEM),
        out_shape=jax.ShapeDtypeStruct((16 + count, width), F32),
        compiler_params=pltpu.CompilerParams(vmem_limit_bytes=16 << 20),
        cost_estimate=NO_COST,
    )(spots, *arrays)


def gelu(values):
    return 0.5 * values * (1.0 + lax.erf(values * math.sqrt(0.5)))


def gelu_slope(values):
    return 0.5 * (1.0 + lax.erf(values * math.sqrt(0.5))) + values * (
        math.sqrt(0.5 / math.pi) * jnp.exp(-0.5 * values * values)
    )


def as_rows(value, width):
    flat = value.reshape(1, -1)
    return jnp.pad(flat, ((0, 7), (0, width - flat.shape[1])))


def from_rows(cells, shape):
    rows, columns = shape
    flat = cells[:, 0, : rows * columns].reshape(-1, rows, columns)
    return flat.transpose(1, 0, 2).reshape(rows, -1)


def mm(spec, left, right):
    return jnp.einsum(spec, left, right, preferred_element_type=F32)


def column_sum(rows):
    return jnp.sum(rows.astype(F32), axis=0)


def hmul(left, right):
    return jnp.dot(left, right, precision=NS_PREC, preferred_element_type=F32)


def ortho(columns):
    gram_mat = pack_sum(
        lax.dot_general(columns, columns, (TN, ((), ())), precision=NS_PREC, preferred_element_type=F32)
    )
    scale = 1.0 / (jnp.sqrt(jnp.trace(gram_mat)) + 1e-07)
    iterate = columns * scale
    gram_mat = gram_mat * scale * scale
    eye = jnp.eye(gram_mat.shape[0], dtype=F32)
    for step in range(NS_STEPS):
        if step < NS_STEPS - 1:
            square = hmul(gram_mat, gram_mat)
            poly = COEF_ONE * eye + COEF_TWO * gram_mat + COEF_THREE * square
            poly_gram = COEF_ONE * gram_mat + COEF_TWO * square + COEF_THREE * hmul(square, gram_mat)
            iterate = hmul(iterate, poly)
            gram_mat = hmul(poly, poly_gram)
        else:
            first_pass = hmul(iterate, gram_mat)
            iterate = COEF_ONE * iterate + COEF_TWO * first_pass + COEF_THREE * hmul(first_pass, gram_mat)
    return iterate


def to_planes(shards):
    seq_count, seq_place = lax.axis_size("seq"), lax.axis_index("seq")
    most = max(m.shape[0] for m in shards)
    filled = [jnp.pad(m, ((0, most - m.shape[0]), (0, 0))) for m in shards]
    filled += [jnp.zeros_like(filled[0])] * (seq_count - len(shards))
    stacked = jnp.stack(filled)
    parts = [pick(stacked, seq_place)]
    parts += [swap(pick(stacked, seq_place ^ k), "seq", k) for k in range(1, seq_count)]
    return jnp.stack(parts)


def from_planes(value, counts):
    back = [value[0]] + [swap(value[k], "seq", k) for k in range(1, lax.axis_size("seq"))]
    return [_choose(back, lax.axis_index("seq"), m)[:count] for m, count in enumerate(counts)]


def muon_update(weight, iterate):
    col_ratio = math.sqrt(
        max(1.0, iterate.shape[1] * lax.axis_size(("pack", "seq")) / weight.shape[0])
    )
    return weight * (1.0 - MUON_RATE * DECAY) - MUON_RATE * col_ratio * iterate


def adam_update(weight, first_moment, second_moment, gradient, factor, count_float):
    scaled = factor * gradient
    new_first = BETA_ONE * first_moment + (1.0 - BETA_ONE) * scaled
    new_second = BETA_TWO * second_moment + (1.0 - BETA_TWO) * scaled * scaled
    first_hat = new_first / (1.0 - jnp.power(BETA_ONE, count_float))
    second_hat = new_second / (1.0 - jnp.power(BETA_TWO, count_float))
    new_weight = weight - ADAM_RATE * (first_hat / (jnp.sqrt(second_hat) + 1e-08) + DECAY * weight)
    return (new_weight, new_first, new_second)


def deal_rows(lengths, keep_mask, shard_len):
    packs, images = lengths.shape
    seq_count, seq_place = lax.axis_size("seq"), lax.axis_index("seq")
    image_range = jnp.arange(images, dtype=jnp.int32)
    upto = image_range[None, :] <= image_range[:, None]
    ends = jnp.sum(jnp.where(upto[None], lengths[:, None, :], 0), axis=2, dtype=jnp.int32)
    starts = ends - lengths
    cuts = jnp.arange(1, seq_count, dtype=jnp.int32) * shard_len
    straddles = (starts[:, None, :] < cuts[None, :, None]) & (ends[:, None, :] > cuts[None, :, None])
    behind = jnp.sum(jnp.where(straddles, cuts[None, :, None] - starts[:, None, :], 0), axis=2, dtype=jnp.int32)
    ahead = jnp.sum(jnp.where(straddles, ends[:, None, :] - cuts[None, :, None], 0), axis=2, dtype=jnp.int32)
    excess = jnp.zeros_like(cuts)
    moves = []
    for pack in range(packs):
        more, less = excess + ahead[pack], excess - behind[pack]
        forward = jnp.abs(more) <= jnp.abs(less)
        excess = jnp.where(forward, more, less)
        moves.append(jnp.where(forward, ahead[pack], -behind[pack]))
    borders = jnp.concatenate(
        [
            jnp.zeros((packs, 1), jnp.int32),
            cuts[None, :] + jnp.stack(moves),
            jnp.full((packs, 1), PACK_LEN, jnp.int32),
        ],
        axis=1,
    )
    first = lax.dynamic_index_in_dim(borders, seq_place, 1, keepdims=False)
    held = lax.dynamic_index_in_dim(borders, seq_place + 1, 1, keepdims=False) - first
    pack_range = jnp.arange(packs, dtype=jnp.int32)
    before = jnp.sum(jnp.where(pack_range[None, :] < pack_range[:, None], held[None, :], 0), axis=1, dtype=jnp.int32)
    row = jnp.arange(packs * shard_len + MAXLEN, dtype=jnp.int32)
    in_pack = (row[:, None] >= before[None, :]) & (row[:, None] < (before + held)[None, :])
    valid = jnp.any(in_pack, axis=1)

    def of_pack(values):
        return jnp.sum(jnp.where(in_pack, values, 0), axis=1, dtype=jnp.int32)

    pack_of = of_pack(pack_range[None, :])
    place = of_pack(row[:, None] - before[None, :] + first[None, :])
    window = shard_len + 2 * MAXLEN
    source = jnp.where(valid, pack_of * window + place - (seq_place * shard_len - MAXLEN), -1)
    row_ends = jnp.sum(jnp.where(in_pack[:, :, None], ends[None], 0), axis=1, dtype=jnp.int32)
    row_starts = jnp.sum(jnp.where(in_pack[:, :, None], starts[None], 0), axis=1, dtype=jnp.int32)
    image_of = jnp.sum((place[:, None] >= row_ends).astype(jnp.int32), axis=1, dtype=jnp.int32)
    is_first = jnp.any(place[:, None] == row_starts, axis=1)
    keep_rows = mm("rp,pj->rj", in_pack.astype(LOW), (keep_mask > 0).astype(LOW))
    spot = jnp.arange(PACK_LEN, dtype=jnp.int32)
    kept = jnp.any((place[:, None] == spot[None, :]) & (keep_rows > 0.5), axis=1)
    live = valid & (kept | is_first)
    group = jnp.where(valid, pack_of * images + image_of, -1)

    spots = jnp.arange(PACK_LEN, dtype=jnp.int32)[None, None, :]
    inside = (spots >= starts[:, :, None]) & (spots < ends[:, :, None])
    counted = inside & ((keep_mask > 0)[:, None, :] | (spots == starts[:, :, None]))
    counts = jnp.sum(counted.astype(F32), axis=2)
    return source, group, live, counts.reshape(-1)


def body(
    patches,
    lengths,
    keep_mask,
    labels,
    step_count,
    embed_weight,
    embed_first,
    embed_second,
    qkv_weight,
    qkv_moment,
    output_weight,
    output_moment,
    up_weight,
    up_moment,
    down_weight,
    down_moment,
    small_params,
    small_first,
    small_second,
    head_weight,
    head_first,
    head_second,
    head_bias,
    bias_first,
    bias_second,
):
    packs, shard_len, patch_in = patches.shape
    images = lengths.shape[1]
    width = qkv_weight.shape[0]
    seq_count, seq_place = lax.axis_size("seq"), lax.axis_index("seq")
    pack_count, pack_place = lax.axis_size("pack"), lax.axis_index("pack")
    small_rows = small_params.shape[0]

    bundle = [
        embed_weight.T,
        qkv_weight.T,
        output_weight.T,
        as_rows(small_params, width),
        as_rows(head_bias, width),
    ]
    spots = [0]
    for piece in bundle:
        spots.append(spots[-1] + piece.shape[0])
    first = Gather(jnp.concatenate([piece.astype(LOW) for piece in bundle]))
    up_gather, down_gather = Gather(up_weight.T.astype(LOW)), Gather(down_weight.T.astype(LOW))
    first.along_seq()
    first.block, patches = hold(first.block, patches)
    first.in_plane()
    ends = seq_count - 1
    from_left = lax.ppermute(patches[:, shard_len - MAXLEN :], "seq", [(i, i + 1) for i in range(ends)])
    from_right = lax.ppermute(patches[:, :MAXLEN], "seq", [(i + 1, i) for i in range(ends)])
    from_left, from_right, up_gather.shard = hold(from_left, from_right, up_gather.shard)
    up_gather.along_seq()
    *first.parts, up_gather.block, down_gather.shard = hold(*first.parts, up_gather.block, down_gather.shard)
    embed_full, qkv_full, output_full, small_full, bias_full = first.pieces(spots)
    embed_full, qkv_full, output_full = (
        value.reshape(-1, width) for value in (embed_full, qkv_full, output_full)
    )
    (gain_bias,) = hold(from_rows(small_full, small_params.shape).astype(F32))
    bias_full = lax.dynamic_slice_in_dim(bias_full, pack_place * seq_count, seq_count, 0)
    bias_full = bias_full[:, 0, : head_bias.shape[0]].reshape(-1)
    up_gather.in_plane()
    down_gather.along_seq()

    window = jnp.concatenate([from_left, patches, from_right], axis=1).reshape(-1, patch_in)
    source, group, live, counts = deal_rows(lengths, keep_mask, shard_len)
    chosen = (source[:, None] == jnp.arange(window.shape[0], dtype=jnp.int32)[None, :]).astype(LOW)
    tokens = mm("rw,wi->ri", chosen, window).astype(LOW)
    rows = tokens.shape[0]
    query_id = group.reshape(rows // BLOCK, 1, BLOCK)
    key_id = jnp.pad(jnp.where(live, group, -2), (BLOCK, BLOCK), constant_values=-2)[:, None]
    group_count = packs * images
    member = (
        (group[None, :] == jnp.arange(group_count, dtype=jnp.int32)[:, None]) & live[None, :]
    ).astype(F32)

    embedded = mm("ri,di->rd", tokens, embed_full) + gain_bias[6]
    embedded, *up_gather.parts, down_gather.block, head_low = hold(
        embedded, *up_gather.parts, down_gather.block, head_weight.astype(LOW)
    )
    down_gather.in_plane()
    head_full = lax.all_gather(head_low, "seq", axis=0, tiled=True)
    up_full = [half.reshape(-1, width) for half in up_gather.halves()]
    normed_one = layer_norm(embedded, gain_bias[0], gain_bias[1]).astype(LOW)
    qkv_bias = jnp.concatenate([gain_bias[7], jnp.zeros_like(gain_bias[7]), gain_bias[8]])
    qkv_rows = (mm("rd,ed->re", normed_one, qkv_full) + qkv_bias).astype(LOW)
    attn_low, log_total = attend(qkv_rows, query_id, key_id)
    attn_low, *down_gather.parts = hold(attn_low, *down_gather.parts)
    down_full = [half.reshape(-1, width) for half in down_gather.halves()]
    after_attn = embedded + mm("re,de->rd", attn_low, output_full) + gain_bias[9]
    normed_two = layer_norm(after_attn, gain_bias[2], gain_bias[3]).astype(LOW)
    up_bias = jnp.take(
        gain_bias[11:15].reshape(pack_count, -1), relative_packs() ^ pack_place, axis=0
    ).reshape(2, -1)
    up_rows = [mm("rd,fd->rf", normed_two, up_full[half]) + up_bias[half] for half in range(2)]
    active = [gelu(rows).astype(LOW) for rows in up_rows]
    after_mlp = (
        after_attn
        + (mm("rf,fd->rd", active[0], down_full[0]) + mm("rf,fd->rd", active[1], down_full[1]))
        + gain_bias[10]
    )
    final_rows = layer_norm(after_mlp, gain_bias[4], gain_bias[5])
    pool_sums = jnp.dot(member, final_rows, precision=HIGHEST_PREC, preferred_element_type=F32)
    pooled_mine = (pool_sums / counts[:, None]).astype(LOW)

    img_share = group_count // seq_count
    split = pooled_mine.reshape(seq_count, img_share, width)
    pooled_low = tree_sum(
        [pick(split, seq_place).astype(F32)]
        + [swap(pick(split, seq_place ^ k), "seq", k).astype(F32) for k in range(1, seq_count)]
    ).astype(LOW)
    pooled_rows = jnp.concatenate(gather_blocks(pooled_low), axis=0).reshape(-1, width)
    depth = head_weight.shape[0]
    label_cols = head_full.shape[1]
    logits = mm("nd,dc->nc", pooled_rows, head_full) + bias_full.astype(F32)
    label_rows = jnp.take(
        pick(labels.reshape(pack_count, seq_count, img_share), seq_place, 1),
        relative_packs() ^ pack_place,
        axis=0,
    ).reshape(-1)
    class_ids = pack_place * label_cols + jnp.arange(label_cols, dtype=jnp.int32)
    valid = (class_ids < LABELS).astype(F32)
    target = (label_rows[:, None] == class_ids[None, :]).astype(F32)
    image_total = labels.shape[0] * labels.shape[1]
    loss_part = jnp.sum(valid[None, :] * (jax.nn.softplus(logits) - target * logits)) / image_total
    grad_logits = (valid[None, :] * (jax.nn.sigmoid(logits) - target) / image_total).astype(LOW)
    pooled_part = mm("nc,dc->nd", grad_logits, head_full).reshape(pack_count, img_share, width)
    pooled_grad = pack_scatter(pooled_part)
    pooled_grad = jnp.concatenate(absolute(relative(pooled_grad, "seq"), seq_place), axis=0)
    pooled_grad = pooled_grad / counts[:, None]

    traded, pooled_grad = hold(jnp.concatenate([pooled_rows, grad_logits], axis=1), pooled_grad)
    traded = lax.all_gather(traded, "seq", axis=0, tiled=True)

    grad_mlp_low, sums_last, grad_mlp = norm_back(
        after_mlp, gain_bias[4], pooled_grad, jnp.where(live, group, -1)[:, None]
    )
    down_sum, up_sum = Scatter(0, width, True), Scatter(1, width, True)
    half = width // 2
    late_sums = [Scatter(0, half), Scatter(1, half)]
    down_out = mm("rf,rd->fd", active[1], grad_mlp_low)
    down_keep = mm("rf,rd->fd", active[0], grad_mlp_low)
    grad_mlp_low, down_out, down_keep = hold(grad_mlp_low, down_out, down_keep)
    down_out = down_sum.start_halves(down_keep, down_out)
    grad_upper = [
        (mm("rd,fd->rf", grad_mlp_low, down_full[side]) * gelu_slope(up_rows[side])).astype(LOW)
        for side in range(2)
    ]
    up_out = mm("rf,rd->fd", grad_upper[1], normed_two)
    up_keep = mm("rf,rd->fd", grad_upper[0], normed_two)
    grad_upper[0], grad_upper[1], up_out, up_keep = hold(*grad_upper, up_out, up_keep)
    up_out = up_sum.start_halves(up_keep, up_out)
    grad_normed = mm("rf,fd->rd", grad_upper[0], up_full[0]) + mm("rf,fd->rd", grad_upper[1], up_full[1])
    down_out = down_sum.step(down_out)
    grad_normed, down_out = hold(grad_normed, down_out)
    grad_attn_low, sums_second, grad_attn = norm_back(
        after_attn, gain_bias[2], grad_normed, grad_mlp
    )
    grad_mixed = mm("rd,de->re", grad_attn_low, output_full).astype(LOW)
    up_out = up_sum.step(up_out)
    muon_moments = [m.T for m in (qkv_moment, output_moment, up_moment, down_moment)]
    grad_mixed, up_out, *muon_moments = hold(grad_mixed, up_out, *muon_moments)
    old_columns = to_planes(muon_moments)
    grad_qkv = attend_back(qkv_rows, grad_mixed, log_total, query_id, key_id)
    output_grad = mm("rd,re->de", grad_attn_low, attn_low)
    late_keep, late_out = late_halves(mm("re,rd->ed", grad_qkv, normed_one), output_grad)
    down_out, up_out = down_sum.step(down_out), up_sum.step(up_out)
    grad_qkv, late_out, down_out, up_out = hold(grad_qkv, late_out, down_out, up_out)
    grad_normed = mm("re,ed->rd", grad_qkv, qkv_full)
    late = late_keep + swap(late_out, "pack", 1)
    late_outs = [
        each.start_joined(part) for each, part in zip(late_sums, (late[..., :half], late[..., half:]))
    ]
    grad_normed, late_outs[0], late_outs[1], down_sum.keep, up_sum.keep = hold(
        grad_normed, *late_outs, down_sum.keep, up_sum.keep
    )
    grad_embed_rows, sums_first = norm_back(embedded, gain_bias[0], grad_normed, grad_attn, keep_sum=False)
    last_keep, last_out = late_halves(mm("rd,ri->di", grad_embed_rows, tokens))
    down_sum.finish(down_out)
    up_sum.finish(up_out)
    early_sum = SeqScatter(jnp.concatenate([down_sum.value, up_sum.value], axis=1))
    early_out = early_sum.send()
    last_out, early_out, late_sums[0].keep, late_sums[1].keep, grad_qkv, traded, old_columns = hold(
        last_out, early_out, late_sums[0].keep, late_sums[1].keep, grad_qkv, traded, old_columns
    )
    all_pooled = pick(traded[:, :width].reshape(-1, seq_count, head_weight.shape[0]), seq_place, 1)
    all_logits = traded[:, width:]
    head_grad = mm("nd,nc->dc", all_pooled, all_logits)
    bias_grad = pick(column_sum(all_logits).reshape(seq_count, -1), seq_place)
    qkv_sum = column_sum(grad_qkv)
    late_outs = [each.step(sent) for each, sent in zip(late_sums, late_outs)]
    last = last_keep + swap(last_out, "pack", 1)
    last = last.reshape((pack_count // 2,) + last.shape[-3:])
    last_outs = [pick(last, (pack_place ^ k) >> 1) for k in other_chips()]
    early_out = early_sum.step(early_out)
    head_grad, bias_grad, qkv_sum, early_out, grad_upper[0], grad_upper[1], *sends = hold(
        head_grad, bias_grad, qkv_sum, early_out, *grad_upper, *late_outs, *last_outs
    )
    small_mine = small_sums(
        sums_first, sums_second, sums_last, qkv_sum, [column_sum(side) for side in grad_upper]
    )
    for each, sent in zip(late_sums, sends[:2]):
        each.finish(sent)
    last_parts = [pick(last, pack_place >> 1)] + [
        swap(sent, "pack", k) for k, sent in zip(other_chips(), sends[2:])
    ]
    late_sum = SeqScatter(
        jnp.concatenate(
            [jnp.concatenate([each.value for each in late_sums], axis=2), tree_sum(last_parts)], axis=1
        )
    )
    late_out, small_mine = hold(late_sum.send(), small_mine)
    small_total = sum_plane(small_mine)
    while early_out is not None:
        early_out = early_sum.step(early_out)
    late_out = late_sum.step(late_out)
    while late_out is not None:
        late_out = late_sum.step(late_out)
    small_total = all_sum(small_total, "seq")
    down_share, up_share = jnp.split(early_sum.result(), 2)
    late_share = late_sum.result()
    widths = [qkv_weight.shape[1], output_weight.shape[1], embed_weight.shape[1]]
    qkv_share, output_share = late_share[: widths[0]], late_share[widths[0] : widths[0] + widths[1]]
    embed_share = late_share[widths[0] + widths[1] :].T
    hidden = down_weight.shape[1] * seq_count
    small_total = jnp.concatenate(
        [small_total[:11], small_total[16:, :hidden].reshape(small_rows - 11, width)], axis=0
    )
    place = pack_place * seq_count + seq_place
    small_share = pick(small_total.reshape(small_rows, pack_count * seq_count, -1), place, 1)

    shares = (early_sum.result(), late_share, head_grad, bias_grad)
    square_sum = sum((jnp.sum(piece * piece) for piece in shares))
    sums = jnp.broadcast_to(jnp.stack([loss_part, square_sum])[:, None], (2, BLOCK))
    sums = sum_plane(sums)
    muon_shares = (qkv_share, output_share, up_share, down_share)
    new_columns, sums = hold(to_planes(muon_shares), sums)
    sums = all_sum(sums, "seq")
    loss_value, square_total = sums[0, 0], sums[1, 0] + jnp.sum(small_total * small_total)
    grad_norm = jnp.sqrt(square_total)
    factor = jnp.minimum(1.0, CLIP_NORM / (grad_norm + 1e-06))
    columns = MUON_MU * old_columns + factor * new_columns
    iterates = ortho(columns.reshape(-1, width)).reshape(columns.shape)
    iterates = [iterate.T for iterate in from_planes(iterates, [m.shape[0] for m in muon_moments])]
    moments = [
        (MUON_MU * moment + factor * share).T for moment, share in zip(muon_moments, muon_shares)
    ]
    new_qkv = muon_update(qkv_weight, iterates[0])
    new_output = muon_update(output_weight, iterates[1])
    new_up = muon_update(up_weight, iterates[2])
    new_down = muon_update(down_weight, iterates[3])
    count_float = step_count[0].astype(F32)
    new_embed, new_embed_first, new_embed_second = adam_update(
        embed_weight, embed_first, embed_second, embed_share, factor, count_float
    )
    new_small, new_small_first, new_small_second = adam_update(
        small_params, small_first, small_second, small_share, factor, count_float
    )
    new_head, new_head_first, new_head_second = adam_update(
        head_weight, head_first, head_second, head_grad, factor, count_float
    )
    new_bias, new_bias_first, new_bias_second = adam_update(
        head_bias, bias_first, bias_second, bias_grad, factor, count_float
    )
    return (
        loss_value,
        grad_norm,
        new_embed,
        new_embed_first,
        new_embed_second,
        new_qkv,
        moments[0],
        new_output,
        moments[1],
        new_up,
        moments[2],
        new_down,
        moments[3],
        new_small,
        new_small_first,
        new_small_second,
        new_head,
        new_head_first,
        new_head_second,
        new_bias,
        new_bias_first,
        new_bias_second,
    )


def solution(mesh):
    both = P(None, ("pack", "seq"))
    head = P("seq", "pack")
    line = P(("pack", "seq"))
    return jax.shard_map(
        body,
        mesh=mesh,
        in_specs=(P("pack", "seq", None), P("pack", None), P("pack", None), P(), P())
        + (both,) * 14
        + (head,) * 3
        + (line,) * 3,
        out_specs=(P(), P()) + (both,) * 14 + (head,) * 3 + (line,) * 3,
        check_vma=False,
    )
```

```python
import math

import jax
import jax.numpy as jnp
from jax import lax
from jax.experimental import pallas as pl
from jax.experimental.pallas import tpu as pltpu
from jax.sharding import PartitionSpec as P

HEAD_DIM = 64
LABELS = 21843
PACK_LEN = 1024
MAXLEN = 128
NS_STEPS = 2
BLOCK = 128
PAIR = 2 * HEAD_DIM

HIGHEST_PREC = lax.Precision.HIGHEST
NS_PREC = lax.Precision.HIGH
CLIP_NORM = 1.0
MUON_MU = 0.95
MUON_RATE = 1.0
ADAM_RATE = 0.02
BETA_ONE = 0.9
BETA_TWO = 0.95
DECAY = 0.01
COEF_ONE = 3.4445
COEF_TWO = -4.775
COEF_THREE = 2.0315
SCALE = HEAD_DIM ** (-0.5)
LOW = jnp.bfloat16
F32 = jnp.float32
NEG = -1e30
NO_COST = pl.CostEstimate(flops=0, bytes_accessed=0, transcendentals=0)


def swap(value, axis, bit):
    return lax.ppermute(value, axis, [(i, i ^ bit) for i in range(lax.axis_size(axis))])


def pick(value, index, dim=0):
    return lax.dynamic_index_in_dim(value, index, dim, keepdims=False)


def tree_sum(parts):
    while len(parts) > 1:
        parts = [parts[i] + parts[i + 1] for i in range(0, len(parts), 2)]
    return parts[0]


def relative(value, axis):
    return [value] + [swap(value, axis, k) for k in range(1, lax.axis_size(axis))]


def absolute(parts, place):
    return [_choose(parts, place, j) for j in range(len(parts))]


def _choose(parts, place, j):
    out = parts[j]
    for other in range(1, len(parts)):
        out = jnp.where(place == other, parts[j ^ other], out)
    return out


def all_sum(value, axis):
    return tree_sum(relative(value, axis))


def hold(*values):
    return lax.optimization_barrier(values)


def other_chips():
    return list(range(2, lax.axis_size("pack"), 2))


def relative_packs():
    same = [0] + other_chips()
    return jnp.array(same + [k + 1 for k in same], jnp.int32)


def relative_slots():
    count = lax.axis_size("pack")
    offset = lax.axis_index("pack") ^ jnp.arange(count, dtype=jnp.int32)
    return (offset >> 1) + (offset & 1) * (count // 2)


def gather_blocks(block):
    own = jnp.stack([block] + [swap(block, "pack", k) for k in other_chips()])
    return own, swap(own, "pack", 1)


def by_index(parts, place):
    if len(parts) <= 8:
        return jnp.stack(absolute(parts, place))
    value = jnp.stack(parts)
    shape, bit = value.shape, 1
    while bit < len(parts):
        value = value.reshape((-1, 2, bit) + shape[1:])
        turned = jnp.concatenate([value[:, 1:], value[:, :1]], axis=1)
        value = jnp.where((place & bit) == 0, value, turned)
        bit *= 2
    return value.reshape(shape)


def by_core(own, other, dim):
    return jnp.where(
        (lax.axis_index("pack") & 1) == 0, jnp.stack([own, other], axis=dim), jnp.stack([other, own], axis=dim)
    )


class Gather:
    def __init__(self, shard):
        self.shard = shard

    def along_seq(self):
        self.block = by_index(relative(self.shard, "seq"), lax.axis_index("seq"))
        return self.block

    def doubling(self):
        place, count, bit = lax.axis_index("seq"), lax.axis_size("seq"), 1
        block = self.shard[None]
        while bit < count:
            other = swap(block, "seq", bit)
            block = jnp.where(
                (place & bit) == 0,
                jnp.concatenate([block, other], axis=0),
                jnp.concatenate([other, block], axis=0),
            )
            bit *= 2
        self.block = block
        return block

    def in_plane(self):
        self.parts = [self.block] + [swap(self.block, "pack", k) for k in other_chips()]

    def pieces(self, spots):
        mine = by_index(self.parts, lax.axis_index("pack") >> 1)
        other = swap(mine, "pack", 1)
        return [
            by_core(mine[:, :, here:there], other[:, :, here:there], 1).reshape(-1, there - here, mine.shape[-1])
            for here, there in zip(spots[:-1], spots[1:])
        ]

    def halves(self):
        own = jnp.stack(self.parts)
        return own, swap(own, "pack", 1)


class Scatter:
    def __init__(self, order, width, relative=False):
        self.left = [1 << b for b in reversed(range(lax.axis_size("pack").bit_length() - 1))]
        chips = [b for b in self.left if b > 1]
        self.order = [1] + (chips if order == 0 else chips[::-1])
        self.relative, self.width = relative, width

    def start_halves(self, keep, send):
        self.left.remove(1)
        self.bit = self.order.pop(0)
        shape = (2,) * len(self.left) + (lax.axis_size("seq"), -1, self.width)
        self.keep = keep.reshape(shape)
        return send.reshape(shape)

    def start_joined(self, value):
        self.left.remove(1)
        self.order.pop(0)
        self.value = value
        return self.send()

    def send(self):
        self.bit = bit = self.order.pop(0)
        dim = self.left.index(bit)
        self.left.remove(bit)
        if self.relative:
            self.keep = lax.index_in_dim(self.value, 0, dim, keepdims=False)
            return lax.index_in_dim(self.value, 1, dim, keepdims=False)
        mine = (lax.axis_index("pack") & bit) // bit
        self.keep = pick(self.value, mine, dim)
        return pick(self.value, 1 - mine, dim)

    def step(self, sent):
        self.value = self.keep + swap(sent, "pack", self.bit)
        return self.send() if self.order else None

    def finish(self, sent):
        while sent is not None:
            sent = self.step(sent)


class SeqScatter:
    def __init__(self, value):
        self.value, self.bit = value, 1

    def send(self):
        tail = self.value.shape[-2:]
        split = self.value.reshape((-1, 2) + tail)
        mine = (lax.axis_index("seq") & self.bit) // self.bit
        self.keep = pick(split, mine, 1)
        return pick(split, 1 - mine, 1)

    def step(self, sent):
        self.value = self.keep + swap(sent, "seq", self.bit)
        self.bit *= 2
        return self.send() if self.bit < lax.axis_size("seq") else None

    def result(self):
        return self.value.reshape(self.value.shape[-2:])


def late_halves(*grads):
    seq_count, pack_count = lax.axis_size("seq"), lax.axis_size("pack")
    chips = (2,) * (pack_count.bit_length() - 2)
    core = lax.axis_index("pack") & 1

    def half(which):
        pieces = [
            pick(grad.reshape(chips + (2, seq_count, -1, grad.shape[1])), which, len(chips)) for grad in grads
        ]
        return jnp.concatenate(pieces, axis=-2)

    return half(core), half(1 - core)


def pack_scatter(value):
    half = value.shape[0] // 2
    mine = value[:half] + swap(value[half:], "pack", 1)
    parts = [mine[0]] + [swap(mine[k // 2], "pack", k) for k in other_chips()]
    return tree_sum(parts)


def pack_sum(value):
    pack_place, count = lax.axis_index("pack"), lax.axis_size("pack")
    core = pack_place & 1
    split = value.reshape(count // 2, 2, -1, value.shape[1])
    mine = pick(split, core, 1) + swap(pick(split, 1 - core, 1), "pack", 1)
    chip = pack_place >> 1
    parts = [pick(mine, chip)] + [swap(pick(mine, chip ^ (k // 2)), "pack", k) for k in other_chips()]
    total = tree_sum(parts)
    mine = by_index([total] + [swap(total, "pack", k) for k in other_chips()], chip)
    return by_core(mine, swap(mine, "pack", 1), 1).reshape(value.shape)


def sum_plane(value):
    return sum_chips(value + swap(value, "pack", 1))


def sum_chips(value):
    return tree_sum([value] + [swap(value, "pack", k) for k in other_chips()])


def _dot(left, right, dims):
    return lax.dot_general(left, right, (dims, ((), ())), preferred_element_type=F32)


NT = ((1,), (1,))
TN = ((0,), (0,))
NN = ((1,), (0,))


def _window(ref, block, blocks, column):
    places = (jnp.maximum(block - 1, 0), block, jnp.minimum(block + 1, blocks - 1))
    return jnp.concatenate(
        [ref[pl.ds(pl.multiple_of(place * BLOCK, BLOCK), BLOCK), column : column + PAIR] for place in places],
        axis=0,
    )


def _halves(value):
    lane = lax.broadcasted_iota(jnp.int32, value.shape, 1)
    zero = jnp.zeros_like(value)
    return jnp.concatenate(
        [jnp.where(lane < HEAD_DIM, value, zero), jnp.where(lane < HEAD_DIM, zero, value)], axis=0
    )


def _merge(value):
    return jnp.concatenate([value[:HEAD_DIM, :BLOCK], value[HEAD_DIM:, BLOCK:]], axis=0).T


def attend_kernel(width, blocks, rows_ref, query_id_ref, key_id_ref, out_ref, log_ref):
    block = pl.program_id(0)
    here = pl.ds(pl.multiple_of(block * BLOCK, BLOCK), BLOCK)
    allowed = key_id_ref[pl.ds(pl.multiple_of(block * BLOCK, BLOCK), 3 * BLOCK), :] == query_id_ref[0]
    for pair in range(width // PAIR):
        column = pair * PAIR
        queries = _halves(rows_ref[here, column : column + PAIR] * SCALE)
        keys = _window(rows_ref, block, blocks, width + column)
        values = _window(rows_ref, block, blocks, 2 * width + column)
        mixed = []
        for lanes in (slice(0, BLOCK), slice(BLOCK, 2 * BLOCK)):
            scores = jnp.where(allowed, _dot(keys, queries[lanes], NT), NEG)
            top = jnp.max(scores, axis=0, keepdims=True)
            raised = jnp.exp(scores - top)
            total = jnp.sum(raised, axis=0, keepdims=True)
            probs = (raised * (1.0 / total)).astype(LOW)
            log_ref[0, pair : pair + 1, lanes] = top + jnp.log(total)
            mixed.append(_dot(values, probs, TN))
        out_ref[:, column : column + PAIR] = _merge(jnp.concatenate(mixed, axis=1)).astype(LOW)


def attend_back_kernel(
    width, blocks, rows_ref, grad_ref, log_ref, query_id_ref, key_id_ref, out_ref, key_sum, value_sum
):
    block = pl.program_id(0)

    @pl.when(block == 0)
    def _():
        key_sum[...] = jnp.zeros_like(key_sum)
        value_sum[...] = jnp.zeros_like(value_sum)

    span = pl.ds(pl.multiple_of(block * BLOCK, BLOCK), 3 * BLOCK)
    here = pl.ds(pl.multiple_of(block * BLOCK, BLOCK), BLOCK)
    allowed = key_id_ref[span, :] == query_id_ref[0]
    allowed = jnp.concatenate([allowed, allowed], axis=1)
    for pair in range(width // PAIR):
        column = pair * PAIR
        lanes = slice(column, column + PAIR)
        queries = _halves(rows_ref[here, lanes] * SCALE)
        grads = _halves(grad_ref[here, lanes])
        keys = _window(rows_ref, block, blocks, width + column)
        values = _window(rows_ref, block, blocks, 2 * width + column)
        scores = jnp.where(allowed, _dot(keys, queries, NT), NEG)
        probs = jnp.exp(scores - log_ref[0, pair : pair + 1, :])
        grad_probs = _dot(values, grads, NT)
        inner = jnp.sum(probs * grad_probs, axis=0, keepdims=True)
        grad_scores = (probs * (grad_probs - inner)).astype(LOW)
        out_ref[here, lanes] = (_merge(_dot(keys, grad_scores, TN)) * SCALE).astype(LOW)
        key_sum[span, lanes] += _dot(grad_scores, queries, NN)
        value_sum[span, lanes] += _dot(probs.astype(LOW), grads, NN)

    @pl.when(block == blocks - 1)
    def _():
        def write(place, carry):
            into = pl.ds(pl.multiple_of(place * BLOCK, BLOCK), BLOCK)
            source = pl.ds(pl.multiple_of((place + 1) * BLOCK, BLOCK), BLOCK)
            out_ref[into, width : 2 * width] = key_sum[source, :].astype(LOW)
            out_ref[into, 2 * width :] = value_sum[source, :].astype(LOW)
            return carry

        lax.fori_loop(0, blocks, write, 0)


def _params():
    return pltpu.CompilerParams(dimension_semantics=("arbitrary",), vmem_limit_bytes=56 << 20)


def attend(qkv_rows, query_id, key_id):
    rows, triple = qkv_rows.shape
    width, blocks = triple // 3, rows // BLOCK
    heads = width // HEAD_DIM
    return pl.pallas_call(
        lambda *refs: attend_kernel(width, blocks, *refs),
        grid=(blocks,),
        in_specs=[
            pl.BlockSpec((rows, triple), lambda i: (0, 0)),
            pl.BlockSpec((1, 1, BLOCK), lambda i: (i, 0, 0)),
            pl.BlockSpec((rows + 2 * BLOCK, 1), lambda i: (0, 0)),
        ],
        out_specs=[
            pl.BlockSpec((BLOCK, width), lambda i: (i, 0)),
            pl.BlockSpec((1, heads // 2, 2 * BLOCK), lambda i: (i, 0, 0)),
        ],
        out_shape=[
            jax.ShapeDtypeStruct((rows, width), LOW),
            jax.ShapeDtypeStruct((blocks, heads // 2, 2 * BLOCK), F32),
        ],
        compiler_params=_params(),
        cost_estimate=NO_COST,
    )(qkv_rows, query_id, key_id)


def attend_back(qkv_rows, grad_rows, log_total, query_id, key_id):
    rows, triple = qkv_rows.shape
    width, blocks = triple // 3, rows // BLOCK
    heads = width // HEAD_DIM
    return pl.pallas_call(
        lambda *refs: attend_back_kernel(width, blocks, *refs),
        grid=(blocks,),
        in_specs=[
            pl.BlockSpec((rows, triple), lambda i: (0, 0)),
            pl.BlockSpec((rows, width), lambda i: (0, 0)),
            pl.BlockSpec((1, heads // 2, 2 * BLOCK), lambda i: (i, 0, 0)),
            pl.BlockSpec((1, 1, BLOCK), lambda i: (i, 0, 0)),
            pl.BlockSpec((rows + 2 * BLOCK, 1), lambda i: (0, 0)),
        ],
        out_specs=pl.BlockSpec((rows, triple), lambda i: (0, 0)),
        out_shape=jax.ShapeDtypeStruct((rows, triple), LOW),
        scratch_shapes=[
            pltpu.VMEM((rows + 2 * BLOCK, width), F32),
            pltpu.VMEM((rows + 2 * BLOCK, width), F32),
        ],
        compiler_params=_params(),
        cost_estimate=NO_COST,
    )(qkv_rows, grad_rows, log_total, query_id, key_id)


def layer_norm(values, gain_row, bias_row):
    centre = values - jnp.mean(values, axis=-1, keepdims=True)
    spread = jnp.mean(centre * centre, axis=-1, keepdims=True)
    return centre * lax.rsqrt(spread + 1e-06) * gain_row + bias_row


def norm_back_kernel(
    groups, keep_sum, values_ref, cot_ref, more_ref, gain_ref, low_ref, sum_ref, out_ref=None
):
    @pl.when(pl.program_id(0) == 0)
    def _():
        sum_ref[...] = jnp.zeros_like(sum_ref)

    values = values_ref[...]
    if groups:
        group = lax.broadcasted_iota(jnp.int32, (values.shape[0], groups), 1)
        chosen = jnp.where(more_ref[...] == group, 1.0, 0.0)
        cot = jnp.dot(chosen, cot_ref[...], precision=HIGHEST_PREC, preferred_element_type=F32)
    else:
        cot = cot_ref[...]
    centre = values - jnp.mean(values, axis=-1, keepdims=True)
    scale = lax.rsqrt(jnp.mean(centre * centre, axis=-1, keepdims=True) + 1e-06)
    normed = centre * scale
    scaled = cot * gain_ref[...]
    grad = scale * (
        scaled
        - jnp.mean(scaled, axis=-1, keepdims=True)
        - normed * jnp.mean(scaled * normed, axis=-1, keepdims=True)
    )
    if not groups:
        grad = grad + more_ref[...]
    low = grad.astype(LOW)
    if keep_sum:
        out_ref[...] = grad
    low_ref[...] = low
    for row, value in enumerate((cot * normed, cot, low.astype(F32))):
        sum_ref[row : row + 1, :] += jnp.sum(value, axis=0, keepdims=True)


def norm_back(values, gain_row, cotangent, more, keep_sum=True):
    rows, width = values.shape
    groups = cotangent.shape[0] if more.shape[1] == 1 else 0
    tile = rows // 8
    block = pl.BlockSpec((tile, width), lambda i: (i, 0))
    line = pl.BlockSpec((1, width), lambda i: (0, 0))
    out_specs = [block, pl.BlockSpec((8, width), lambda i: (0, 0))]
    out_shape = [jax.ShapeDtypeStruct((rows, width), LOW), jax.ShapeDtypeStruct((8, width), F32)]
    if keep_sum:
        out_specs.append(block)
        out_shape.append(jax.ShapeDtypeStruct((rows, width), F32))
    return pl.pallas_call(
        lambda *refs: norm_back_kernel(groups, keep_sum, *refs),
        grid=(8,),
        in_specs=[
            block,
            pl.BlockSpec((groups, width), lambda i: (0, 0)) if groups else block,
            pl.BlockSpec((tile, 1), lambda i: (i, 0)) if groups else block,
            line,
        ],
        out_specs=out_specs,
        out_shape=out_shape,
        compiler_params=_params(),
        cost_estimate=NO_COST,
    )(values, cotangent, more, gain_row[None])


def small_kernel(spots_ref, first_ref, second_ref, last_ref, qkv_ref, up_ref, out_ref):
    width, slots = out_ref.shape[1], spots_ref.shape[0]
    out_ref[...] = jnp.zeros_like(out_ref)
    rows = [(first_ref, 0), (first_ref, 1), (second_ref, 0), (second_ref, 1), (last_ref, 0), (last_ref, 1)]
    rows += [(first_ref, 2), (qkv_ref, 0), (qkv_ref, 2), (second_ref, 2), (last_ref, 2)]
    for row, (ref, which) in enumerate(rows):
        if ref is qkv_ref:
            out_ref[row : row + 1, :] = ref[:, which * width : (which + 1) * width]
        else:
            out_ref[row : row + 1, :] = ref[which : which + 1, :]
    for slot in range(slots):
        out_ref[pl.ds(16 + spots_ref[slot], 1), :] = up_ref[slot : slot + 1, :]


def small_sums(first, second, last, qkv_sum, up_sums):
    width, count = first.shape[1], lax.axis_size("pack")
    spots = relative_packs() ^ lax.axis_index("pack")
    up_sum = jnp.concatenate(up_sums).reshape(count, -1)
    arrays = [first, second, last, qkv_sum[None], jnp.pad(up_sum, ((0, 0), (0, width - up_sum.shape[1])))]
    return pl.pallas_call(
        small_kernel,
        in_specs=[pl.BlockSpec(memory_space=pltpu.SMEM)] + [pl.BlockSpec(memory_space=pltpu.VMEM)] * len(arrays),
        out_specs=pl.BlockSpec(memory_space=pltpu.VMEM),
        out_shape=jax.ShapeDtypeStruct((16 + count, width), F32),
        compiler_params=pltpu.CompilerParams(vmem_limit_bytes=16 << 20),
        cost_estimate=NO_COST,
    )(spots, *arrays)


def gelu(values):
    return 0.5 * values * (1.0 + lax.erf(values * math.sqrt(0.5)))


def gelu_slope(values):
    return 0.5 * (1.0 + lax.erf(values * math.sqrt(0.5))) + values * (
        math.sqrt(0.5 / math.pi) * jnp.exp(-0.5 * values * values)
    )


def as_rows(value, width):
    flat = value.reshape(1, -1)
    return jnp.pad(flat, ((0, 7), (0, width - flat.shape[1])))


def from_rows(cells, shape):
    rows, columns = shape
    flat = cells[:, 0, : rows * columns].reshape(-1, rows, columns)
    return flat.transpose(1, 0, 2).reshape(rows, -1)


def mm(spec, left, right):
    return jnp.einsum(spec, left, right, preferred_element_type=F32)


def column_sum(rows):
    return jnp.sum(rows.astype(F32), axis=0)


def hmul(left, right):
    return jnp.dot(left, right, precision=NS_PREC, preferred_element_type=F32)


def ortho(columns):
    gram_mat = pack_sum(
        lax.dot_general(columns, columns, (TN, ((), ())), precision=NS_PREC, preferred_element_type=F32)
    )
    scale = 1.0 / (jnp.sqrt(jnp.trace(gram_mat)) + 1e-07)
    iterate = columns * scale
    gram_mat = gram_mat * scale * scale
    eye = jnp.eye(gram_mat.shape[0], dtype=F32)
    for step in range(NS_STEPS):
        if step < NS_STEPS - 1:
            square = hmul(gram_mat, gram_mat)
            poly = COEF_ONE * eye + COEF_TWO * gram_mat + COEF_THREE * square
            poly_gram = COEF_ONE * gram_mat + COEF_TWO * square + COEF_THREE * hmul(square, gram_mat)
            iterate = hmul(iterate, poly)
            gram_mat = hmul(poly, poly_gram)
        else:
            first_pass = hmul(iterate, gram_mat)
            iterate = COEF_ONE * iterate + COEF_TWO * first_pass + COEF_THREE * hmul(first_pass, gram_mat)
    return iterate


def to_planes(shards):
    seq_count, seq_place = lax.axis_size("seq"), lax.axis_index("seq")
    most = max(m.shape[0] for m in shards)
    filled = [jnp.pad(m, ((0, most - m.shape[0]), (0, 0))) for m in shards]
    filled += [jnp.zeros_like(filled[0])] * (seq_count - len(shards))
    stacked = jnp.stack(filled)
    parts = [pick(stacked, seq_place)]
    parts += [swap(pick(stacked, seq_place ^ k), "seq", k) for k in range(1, seq_count)]
    return jnp.stack(parts)


def from_planes(value, counts):
    back = [value[0]] + [swap(value[k], "seq", k) for k in range(1, lax.axis_size("seq"))]
    return [_choose(back, lax.axis_index("seq"), m)[:count] for m, count in enumerate(counts)]


def muon_update(weight, iterate):
    col_ratio = math.sqrt(
        max(1.0, iterate.shape[1] * lax.axis_size(("pack", "seq")) / weight.shape[0])
    )
    return weight * (1.0 - MUON_RATE * DECAY) - MUON_RATE * col_ratio * iterate


def adam_update(weight, first_moment, second_moment, gradient, factor, count_float):
    scaled = factor * gradient
    new_first = BETA_ONE * first_moment + (1.0 - BETA_ONE) * scaled
    new_second = BETA_TWO * second_moment + (1.0 - BETA_TWO) * scaled * scaled
    first_hat = new_first / (1.0 - jnp.power(BETA_ONE, count_float))
    second_hat = new_second / (1.0 - jnp.power(BETA_TWO, count_float))
    new_weight = weight - ADAM_RATE * (first_hat / (jnp.sqrt(second_hat) + 1e-08) + DECAY * weight)
    return (new_weight, new_first, new_second)


def deal_rows(lengths, keep_mask, shard_len):
    packs, images = lengths.shape
    seq_count, seq_place = lax.axis_size("seq"), lax.axis_index("seq")
    image_range = jnp.arange(images, dtype=jnp.int32)
    upto = image_range[None, :] <= image_range[:, None]
    ends = jnp.sum(jnp.where(upto[None], lengths[:, None, :], 0), axis=2, dtype=jnp.int32)
    starts = ends - lengths
    cuts = jnp.arange(1, seq_count, dtype=jnp.int32) * shard_len
    straddles = (starts[:, None, :] < cuts[None, :, None]) & (ends[:, None, :] > cuts[None, :, None])
    behind = jnp.sum(jnp.where(straddles, cuts[None, :, None] - starts[:, None, :], 0), axis=2, dtype=jnp.int32)
    ahead = jnp.sum(jnp.where(straddles, ends[:, None, :] - cuts[None, :, None], 0), axis=2, dtype=jnp.int32)
    excess = jnp.zeros_like(cuts)
    moves = []
    for pack in range(packs):
        more, less = excess + ahead[pack], excess - behind[pack]
        forward = jnp.abs(more) <= jnp.abs(less)
        excess = jnp.where(forward, more, less)
        moves.append(jnp.where(forward, ahead[pack], -behind[pack]))
    borders = jnp.concatenate(
        [
            jnp.zeros((packs, 1), jnp.int32),
            cuts[None, :] + jnp.stack(moves),
            jnp.full((packs, 1), PACK_LEN, jnp.int32),
        ],
        axis=1,
    )
    first = lax.dynamic_index_in_dim(borders, seq_place, 1, keepdims=False)
    held = lax.dynamic_index_in_dim(borders, seq_place + 1, 1, keepdims=False) - first
    pack_range = jnp.arange(packs, dtype=jnp.int32)
    before = jnp.sum(jnp.where(pack_range[None, :] < pack_range[:, None], held[None, :], 0), axis=1, dtype=jnp.int32)
    row = jnp.arange(packs * shard_len + MAXLEN, dtype=jnp.int32)
    in_pack = (row[:, None] >= before[None, :]) & (row[:, None] < (before + held)[None, :])
    valid = jnp.any(in_pack, axis=1)

    def of_pack(values):
        return jnp.sum(jnp.where(in_pack, values, 0), axis=1, dtype=jnp.int32)

    pack_of = of_pack(pack_range[None, :])
    place = of_pack(row[:, None] - before[None, :] + first[None, :])
    window = shard_len + 2 * MAXLEN
    source = jnp.where(valid, pack_of * window + place - (seq_place * shard_len - MAXLEN), -1)
    row_ends = jnp.sum(jnp.where(in_pack[:, :, None], ends[None], 0), axis=1, dtype=jnp.int32)
    row_starts = jnp.sum(jnp.where(in_pack[:, :, None], starts[None], 0), axis=1, dtype=jnp.int32)
    image_of = jnp.sum((place[:, None] >= row_ends).astype(jnp.int32), axis=1, dtype=jnp.int32)
    is_first = jnp.any(place[:, None] == row_starts, axis=1)
    keep_rows = mm("rp,pj->rj", in_pack.astype(LOW), (keep_mask > 0).astype(LOW))
    spot = jnp.arange(PACK_LEN, dtype=jnp.int32)
    kept = jnp.any((place[:, None] == spot[None, :]) & (keep_rows > 0.5), axis=1)
    live = valid & (kept | is_first)
    group = jnp.where(valid, pack_of * images + image_of, -1)

    spots = jnp.arange(PACK_LEN, dtype=jnp.int32)[None, None, :]
    inside = (spots >= starts[:, :, None]) & (spots < ends[:, :, None])
    counted = inside & ((keep_mask > 0)[:, None, :] | (spots == starts[:, :, None]))
    counts = jnp.sum(counted.astype(F32), axis=2)
    return source, group, live, counts.reshape(-1)


def body(
    patches,
    lengths,
    keep_mask,
    labels,
    step_count,
    embed_weight,
    embed_first,
    embed_second,
    qkv_weight,
    qkv_moment,
    output_weight,
    output_moment,
    up_weight,
    up_moment,
    down_weight,
    down_moment,
    small_params,
    small_first,
    small_second,
    head_weight,
    head_first,
    head_second,
    head_bias,
    bias_first,
    bias_second,
):
    packs, shard_len, patch_in = patches.shape
    images = lengths.shape[1]
    width = qkv_weight.shape[0]
    seq_count, seq_place = lax.axis_size("seq"), lax.axis_index("seq")
    pack_count, pack_place = lax.axis_size("pack"), lax.axis_index("pack")
    small_rows = small_params.shape[0]

    bundle = [
        embed_weight.T,
        qkv_weight.T,
        output_weight.T,
        as_rows(small_params, width),
        as_rows(head_bias, width),
    ]
    spots = [0]
    for piece in bundle:
        spots.append(spots[-1] + piece.shape[0])
    first = Gather(jnp.concatenate([piece.astype(LOW) for piece in bundle]))
    up_gather, down_gather = Gather(up_weight.T.astype(LOW)), Gather(down_weight.T.astype(LOW))
    first.along_seq()
    first.block, patches = hold(first.block, patches)
    first.in_plane()
    ends = seq_count - 1
    from_left = lax.ppermute(patches[:, shard_len - MAXLEN :], "seq", [(i, i + 1) for i in range(ends)])
    from_right = lax.ppermute(patches[:, :MAXLEN], "seq", [(i + 1, i) for i in range(ends)])
    window = jnp.concatenate([from_left, patches, from_right], axis=1).reshape(-1, patch_in)
    source, group, live, counts = deal_rows(lengths, keep_mask, shard_len)
    chosen = (source[:, None] == jnp.arange(window.shape[0], dtype=jnp.int32)[None, :]).astype(LOW)
    tokens = mm("rw,wi->ri", chosen, window).astype(LOW)
    tokens, up_gather.shard, *first.parts = hold(tokens, up_gather.shard, *first.parts)
    up_gather.along_seq()
    embed_full, qkv_full, output_full, small_full, bias_full = first.pieces(spots)
    embed_full, qkv_full, output_full = (
        value.reshape(-1, width) for value in (embed_full, qkv_full, output_full)
    )
    (gain_bias,) = hold(from_rows(small_full, small_params.shape).astype(F32))
    bias_full = lax.dynamic_slice_in_dim(bias_full, pack_place * seq_count, seq_count, 0)
    bias_full = bias_full[:, 0, : head_bias.shape[0]].reshape(-1)

    rows = tokens.shape[0]
    query_id = group.reshape(rows // BLOCK, 1, BLOCK)
    key_id = jnp.pad(jnp.where(live, group, -2), (BLOCK, BLOCK), constant_values=-2)[:, None]
    group_count = packs * images
    member = (
        (group[None, :] == jnp.arange(group_count, dtype=jnp.int32)[:, None]) & live[None, :]
    ).astype(F32)

    embedded = mm("ri,di->rd", tokens, embed_full) + gain_bias[6]
    embedded, up_gather.block, down_gather.shard = hold(embedded, up_gather.block, down_gather.shard)
    up_gather.in_plane()
    down_gather.doubling()
    normed_one = layer_norm(embedded, gain_bias[0], gain_bias[1]).astype(LOW)
    qkv_bias = jnp.concatenate([gain_bias[7], jnp.zeros_like(gain_bias[7]), gain_bias[8]])
    qkv_rows = (mm("rd,ed->re", normed_one, qkv_full) + qkv_bias).astype(LOW)
    qkv_rows, down_gather.block, head_low, *up_gather.parts = hold(
        qkv_rows, down_gather.block, head_weight.astype(LOW), *up_gather.parts
    )
    head_full = lax.all_gather(head_low, "seq", axis=0, tiled=True)
    down_gather.in_plane()
    up_full = [half.reshape(-1, width) for half in up_gather.halves()]
    attn_low, log_total = attend(qkv_rows, query_id, key_id)
    attn_low, *down_gather.parts = hold(attn_low, *down_gather.parts)
    down_full = [half.reshape(-1, width) for half in down_gather.halves()]
    after_attn = embedded + mm("re,de->rd", attn_low, output_full) + gain_bias[9]
    normed_two = layer_norm(after_attn, gain_bias[2], gain_bias[3]).astype(LOW)
    up_bias = jnp.take(
        gain_bias[11:15].reshape(pack_count, -1), relative_packs() ^ pack_place, axis=0
    ).reshape(2, -1)
    up_rows = [mm("rd,fd->rf", normed_two, up_full[half]) + up_bias[half] for half in range(2)]
    active = [gelu(rows).astype(LOW) for rows in up_rows]
    after_mlp = (
        after_attn
        + (mm("rf,fd->rd", active[0], down_full[0]) + mm("rf,fd->rd", active[1], down_full[1]))
        + gain_bias[10]
    )
    final_rows = layer_norm(after_mlp, gain_bias[4], gain_bias[5])
    pool_sums = jnp.dot(member, final_rows, precision=HIGHEST_PREC, preferred_element_type=F32)
    pooled_mine = (pool_sums / counts[:, None]).astype(LOW)

    img_share = group_count // seq_count
    split = pooled_mine.reshape(seq_count, img_share, width)
    pooled_low = tree_sum(
        [pick(split, seq_place).astype(F32)]
        + [swap(pick(split, seq_place ^ k), "seq", k).astype(F32) for k in range(1, seq_count)]
    ).astype(LOW)
    pooled_rows = jnp.concatenate(gather_blocks(pooled_low), axis=0).reshape(-1, width)
    depth = head_weight.shape[0]
    label_cols = head_full.shape[1]
    logits = mm("nd,dc->nc", pooled_rows, head_full) + bias_full.astype(F32)
    label_rows = jnp.take(
        pick(labels.reshape(pack_count, seq_count, img_share), seq_place, 1),
        relative_packs() ^ pack_place,
        axis=0,
    ).reshape(-1)
    class_ids = pack_place * label_cols + jnp.arange(label_cols, dtype=jnp.int32)
    valid = (class_ids < LABELS).astype(F32)
    target = (label_rows[:, None] == class_ids[None, :]).astype(F32)
    image_total = labels.shape[0] * labels.shape[1]
    loss_part = jnp.sum(valid[None, :] * (jax.nn.softplus(logits) - target * logits)) / image_total
    grad_logits = (valid[None, :] * (jax.nn.sigmoid(logits) - target) / image_total).astype(LOW)
    pooled_part = mm("nc,dc->nd", grad_logits, head_full).reshape(pack_count, img_share, width)
    pooled_grad = pack_scatter(pooled_part)
    pooled_grad = jnp.concatenate(absolute(relative(pooled_grad, "seq"), seq_place), axis=0)
    pooled_grad = pooled_grad / counts[:, None]

    traded, pooled_grad = hold(jnp.concatenate([pooled_rows, grad_logits], axis=1), pooled_grad)
    traded = lax.all_gather(traded, "seq", axis=0, tiled=True)

    grad_mlp_low, sums_last, grad_mlp = norm_back(
        after_mlp, gain_bias[4], pooled_grad, jnp.where(live, group, -1)[:, None]
    )
    down_sum, up_sum = Scatter(0, width, True), Scatter(1, width, True)
    half = width // 2
    late_sums = [Scatter(0, half), Scatter(1, half)]
    down_out = mm("rf,rd->fd", active[1], grad_mlp_low)
    down_keep = mm("rf,rd->fd", active[0], grad_mlp_low)
    grad_mlp_low, down_out, down_keep = hold(grad_mlp_low, down_out, down_keep)
    down_out = down_sum.start_halves(down_keep, down_out)
    grad_upper = [
        (mm("rd,fd->rf", grad_mlp_low, down_full[side]) * gelu_slope(up_rows[side])).astype(LOW)
        for side in range(2)
    ]
    up_out = mm("rf,rd->fd", grad_upper[1], normed_two)
    up_keep = mm("rf,rd->fd", grad_upper[0], normed_two)
    grad_upper[0], grad_upper[1], up_out, up_keep = hold(*grad_upper, up_out, up_keep)
    up_out = up_sum.start_halves(up_keep, up_out)
    grad_normed = mm("rf,fd->rd", grad_upper[0], up_full[0]) + mm("rf,fd->rd", grad_upper[1], up_full[1])
    down_out = down_sum.step(down_out)
    grad_normed, down_out = hold(grad_normed, down_out)
    grad_attn_low, sums_second, grad_attn = norm_back(
        after_attn, gain_bias[2], grad_normed, grad_mlp
    )
    grad_mixed = mm("rd,de->re", grad_attn_low, output_full).astype(LOW)
    up_out = up_sum.step(up_out)
    grad_mixed, up_out = hold(grad_mixed, up_out)
    grad_qkv = attend_back(qkv_rows, grad_mixed, log_total, query_id, key_id)
    down_out, up_out = down_sum.step(down_out), up_sum.step(up_out)
    grad_qkv, down_out, up_out = hold(grad_qkv, down_out, up_out)
    grad_normed = mm("re,ed->rd", grad_qkv, qkv_full)
    grad_embed_rows, sums_first = norm_back(embedded, gain_bias[0], grad_normed, grad_attn, keep_sum=False)
    output_grad = mm("rd,re->de", grad_attn_low, attn_low)
    embed_grad = mm("rd,ri->di", grad_embed_rows, tokens)
    down_sum.finish(down_out)
    up_sum.finish(up_out)
    early_sum = SeqScatter(jnp.concatenate([down_sum.value, up_sum.value], axis=1))
    early_out = early_sum.send()
    grad_qkv, output_grad, embed_grad, early_out = hold(grad_qkv, output_grad, embed_grad, early_out)
    late_keep, late_out = late_halves(mm("re,rd->ed", grad_qkv, normed_one), output_grad, embed_grad)
    late_out, early_sum.keep, grad_qkv, traded = hold(late_out, early_sum.keep, grad_qkv, traded)
    all_pooled = pick(traded[:, :width].reshape(-1, seq_count, head_weight.shape[0]), seq_place, 1)
    all_logits = traded[:, width:]
    head_grad = mm("nd,nc->dc", all_pooled, all_logits)
    bias_grad = pick(column_sum(all_logits).reshape(seq_count, -1), seq_place)
    late = late_keep + swap(late_out, "pack", 1)
    late_outs = [
        each.start_joined(part) for each, part in zip(late_sums, (late[..., :half], late[..., half:]))
    ]
    head_grad, bias_grad, grad_qkv, early_sum.keep, grad_upper[0], grad_upper[1], *late_outs = hold(
        head_grad, bias_grad, grad_qkv, early_sum.keep, *grad_upper, *late_outs
    )
    small_mine = small_sums(
        sums_first, sums_second, sums_last, column_sum(grad_qkv), [column_sum(side) for side in grad_upper]
    )
    late_outs = [each.step(sent) for each, sent in zip(late_sums, late_outs)]
    early_out = early_sum.step(early_out)
    small_mine, early_out, *late_outs = hold(small_mine, early_out, *late_outs)
    small_total = small_mine + swap(small_mine, "pack", 1)
    for each, sent in zip(late_sums, late_outs):
        each.finish(sent)
    late_sum = SeqScatter(jnp.concatenate([each.value for each in late_sums], axis=2))
    late_out, small_total, early_sum.keep = hold(late_sum.send(), small_total, early_sum.keep)
    small_total = sum_chips(small_total)
    while early_out is not None:
        early_out = early_sum.step(early_out)
    late_out = late_sum.step(late_out)
    late_out, small_total, early_sum.value = hold(late_out, small_total, early_sum.value)
    small_total = all_sum(small_total, "seq")
    while late_out is not None:
        late_out = late_sum.step(late_out)
    down_share, up_share = jnp.split(early_sum.result(), 2)
    late_share = late_sum.result()
    widths = [qkv_weight.shape[1], output_weight.shape[1], embed_weight.shape[1]]
    qkv_share, output_share = late_share[: widths[0]], late_share[widths[0] : widths[0] + widths[1]]
    embed_share = late_share[widths[0] + widths[1] :].T
    hidden = down_weight.shape[1] * seq_count
    small_total = jnp.concatenate(
        [small_total[:11], small_total[16:, :hidden].reshape(small_rows - 11, width)], axis=0
    )
    place = pack_place * seq_count + seq_place
    small_share = pick(small_total.reshape(small_rows, pack_count * seq_count, -1), place, 1)

    shares = (early_sum.result(), late_share, head_grad, bias_grad)
    square_sum = sum((jnp.sum(piece * piece) for piece in shares))
    sums = jnp.broadcast_to(jnp.stack([loss_part, square_sum])[:, None], (2, BLOCK))
    sums = sum_plane(all_sum(sums, "seq"))
    loss_value, square_total = sums[0, 0], sums[1, 0] + jnp.sum(small_total * small_total)
    grad_norm = jnp.sqrt(square_total)
    factor = jnp.minimum(1.0, CLIP_NORM / (grad_norm + 1e-06))
    muon_shares = (qkv_share, output_share, up_share, down_share)
    moments = [
        MUON_MU * moment.T + factor * share
        for moment, share in zip((qkv_moment, output_moment, up_moment, down_moment), muon_shares)
    ]
    columns = to_planes(moments)
    iterates = ortho(columns.reshape(-1, width)).reshape(columns.shape)
    iterates = [iterate.T for iterate in from_planes(iterates, [m.shape[0] for m in moments])]
    moments = [moment.T for moment in moments]
    new_qkv = muon_update(qkv_weight, iterates[0])
    new_output = muon_update(output_weight, iterates[1])
    new_up = muon_update(up_weight, iterates[2])
    new_down = muon_update(down_weight, iterates[3])
    count_float = step_count[0].astype(F32)
    new_embed, new_embed_first, new_embed_second = adam_update(
        embed_weight, embed_first, embed_second, embed_share, factor, count_float
    )
    new_small, new_small_first, new_small_second = adam_update(
        small_params, small_first, small_second, small_share, factor, count_float
    )
    new_head, new_head_first, new_head_second = adam_update(
        head_weight, head_first, head_second, head_grad, factor, count_float
    )
    new_bias, new_bias_first, new_bias_second = adam_update(
        head_bias, bias_first, bias_second, bias_grad, factor, count_float
    )
    return (
        loss_value,
        grad_norm,
        new_embed,
        new_embed_first,
        new_embed_second,
        new_qkv,
        moments[0],
        new_output,
        moments[1],
        new_up,
        moments[2],
        new_down,
        moments[3],
        new_small,
        new_small_first,
        new_small_second,
        new_head,
        new_head_first,
        new_head_second,
        new_bias,
        new_bias_first,
        new_bias_second,
    )


def solution(mesh):
    both = P(None, ("pack", "seq"))
    head = P("seq", "pack")
    line = P(("pack", "seq"))
    return jax.shard_map(
        body,
        mesh=mesh,
        in_specs=(P("pack", "seq", None), P("pack", None), P("pack", None), P(), P())
        + (both,) * 14
        + (head,) * 3
        + (line,) * 3,
        out_specs=(P(), P()) + (both,) * 14 + (head,) * 3 + (line,) * 3,
        check_vma=False,
    )
```

```python
import math

import jax
import jax.numpy as jnp
from jax import lax
from jax.experimental import pallas as pl
from jax.experimental.pallas import tpu as pltpu
from jax.sharding import PartitionSpec as P

HEAD_DIM = 64
LABELS = 21843
PACK_LEN = 1024
MAXLEN = 128
NS_STEPS = 2
BLOCK = 128
PAIR = 2 * HEAD_DIM

HIGHEST_PREC = lax.Precision.HIGHEST
NS_PREC = lax.Precision.HIGH
CLIP_NORM = 1.0
MUON_MU = 0.95
MUON_RATE = 1.0
ADAM_RATE = 0.02
BETA_ONE = 0.9
BETA_TWO = 0.95
DECAY = 0.01
COEF_ONE = 3.4445
COEF_TWO = -4.775
COEF_THREE = 2.0315
SCALE = HEAD_DIM ** (-0.5)
LOW = jnp.bfloat16
F32 = jnp.float32
NEG = -1e30
NO_COST = pl.CostEstimate(flops=0, bytes_accessed=0, transcendentals=0)


def swap(value, axis, bit):
    return lax.ppermute(value, axis, [(i, i ^ bit) for i in range(lax.axis_size(axis))])


def pick(value, index, dim=0):
    return lax.dynamic_index_in_dim(value, index, dim, keepdims=False)


def tree_sum(parts):
    while len(parts) > 1:
        parts = [parts[i] + parts[i + 1] for i in range(0, len(parts), 2)]
    return parts[0]


def relative(value, axis):
    return [value] + [swap(value, axis, k) for k in range(1, lax.axis_size(axis))]


def absolute(parts, place):
    return [_choose(parts, place, j) for j in range(len(parts))]


def _choose(parts, place, j):
    out = parts[j]
    for other in range(1, len(parts)):
        out = jnp.where(place == other, parts[j ^ other], out)
    return out


def all_sum(value, axis):
    return tree_sum(relative(value, axis))


def hold(*values):
    return lax.optimization_barrier(values)


def other_chips():
    return list(range(2, lax.axis_size("pack"), 2))


def relative_packs():
    same = [0] + other_chips()
    return jnp.array(same + [k + 1 for k in same], jnp.int32)


def relative_slots():
    count = lax.axis_size("pack")
    offset = lax.axis_index("pack") ^ jnp.arange(count, dtype=jnp.int32)
    return (offset >> 1) + (offset & 1) * (count // 2)


def gather_blocks(block):
    own = jnp.stack([block] + [swap(block, "pack", k) for k in other_chips()])
    return own, swap(own, "pack", 1)


def by_index(parts, place):
    if len(parts) <= 8:
        return jnp.stack(absolute(parts, place))
    value = jnp.stack(parts)
    shape, bit = value.shape, 1
    while bit < len(parts):
        value = value.reshape((-1, 2, bit) + shape[1:])
        turned = jnp.concatenate([value[:, 1:], value[:, :1]], axis=1)
        value = jnp.where((place & bit) == 0, value, turned)
        bit *= 2
    return value.reshape(shape)


def by_core(own, other, dim):
    return jnp.where(
        (lax.axis_index("pack") & 1) == 0, jnp.stack([own, other], axis=dim), jnp.stack([other, own], axis=dim)
    )


class Gather:
    def __init__(self, shard):
        self.shard = shard

    def along_seq(self):
        self.block = by_index(relative(self.shard, "seq"), lax.axis_index("seq"))

    def send_seq(self):
        self.parts = relative(self.shard, "seq")

    def join_seq(self):
        self.block = by_index(self.parts, lax.axis_index("seq"))

    def doubling(self):
        place, count, bit = lax.axis_index("seq"), lax.axis_size("seq"), 1
        block = self.shard[None]
        while bit < count:
            other = swap(block, "seq", bit)
            block = jnp.where(
                (place & bit) == 0,
                jnp.concatenate([block, other], axis=0),
                jnp.concatenate([other, block], axis=0),
            )
            bit *= 2
        self.block = block
        return block

    def in_plane(self):
        self.parts = [self.block] + [swap(self.block, "pack", k) for k in other_chips()]

    def pieces(self, spots):
        mine = by_index(self.parts, lax.axis_index("pack") >> 1)
        other = swap(mine, "pack", 1)
        return [
            by_core(mine[:, :, here:there], other[:, :, here:there], 1).reshape(-1, there - here, mine.shape[-1])
            for here, there in zip(spots[:-1], spots[1:])
        ]

    def halves(self):
        own = jnp.stack(self.parts)
        return own, swap(own, "pack", 1)


class Scatter:
    def __init__(self, order, width, relative=False):
        self.left = [1 << b for b in reversed(range(lax.axis_size("pack").bit_length() - 1))]
        chips = [b for b in self.left if b > 1]
        self.order = [1] + (chips if order == 0 else chips[::-1])
        self.relative, self.width = relative, width

    def start_halves(self, keep, send):
        self.left.remove(1)
        self.bit = self.order.pop(0)
        shape = (2,) * len(self.left) + (lax.axis_size("seq"), -1, self.width)
        self.keep = keep.reshape(shape)
        return send.reshape(shape)

    def start_joined(self, value):
        self.left.remove(1)
        self.order.pop(0)
        self.value = value
        return self.send()

    def send(self):
        self.bit = bit = self.order.pop(0)
        dim = self.left.index(bit)
        self.left.remove(bit)
        if self.relative:
            self.keep = lax.index_in_dim(self.value, 0, dim, keepdims=False)
            return lax.index_in_dim(self.value, 1, dim, keepdims=False)
        mine = (lax.axis_index("pack") & bit) // bit
        self.keep = pick(self.value, mine, dim)
        return pick(self.value, 1 - mine, dim)

    def step(self, sent):
        self.value = self.keep + swap(sent, "pack", self.bit)
        return self.send() if self.order else None

    def finish(self, sent):
        while sent is not None:
            sent = self.step(sent)


class SeqScatter:
    def __init__(self, value):
        self.value, self.bit = value, 1

    def send(self):
        tail = self.value.shape[-2:]
        split = self.value.reshape((-1, 2) + tail)
        mine = (lax.axis_index("seq") & self.bit) // self.bit
        self.keep = pick(split, mine, 1)
        return pick(split, 1 - mine, 1)

    def step(self, sent):
        self.value = self.keep + swap(sent, "seq", self.bit)
        self.bit *= 2
        return self.send() if self.bit < lax.axis_size("seq") else None

    def result(self):
        return self.value.reshape(self.value.shape[-2:])


def late_halves(*grads):
    seq_count, pack_count = lax.axis_size("seq"), lax.axis_size("pack")
    chips = (2,) * (pack_count.bit_length() - 2)
    core = lax.axis_index("pack") & 1

    def half(which):
        pieces = [
            pick(grad.reshape(chips + (2, seq_count, -1, grad.shape[1])), which, len(chips)) for grad in grads
        ]
        return jnp.concatenate(pieces, axis=-2)

    return half(core), half(1 - core)


def pack_scatter(value):
    half = value.shape[0] // 2
    mine = value[:half] + swap(value[half:], "pack", 1)
    parts = [mine[0]] + [swap(mine[k // 2], "pack", k) for k in other_chips()]
    return tree_sum(parts)


def pack_sum(value):
    pack_place, count = lax.axis_index("pack"), lax.axis_size("pack")
    core = pack_place & 1
    split = value.reshape(count // 2, 2, -1, value.shape[1])
    mine = pick(split, core, 1) + swap(pick(split, 1 - core, 1), "pack", 1)
    chip = pack_place >> 1
    parts = [pick(mine, chip)] + [swap(pick(mine, chip ^ (k // 2)), "pack", k) for k in other_chips()]
    total = tree_sum(parts)
    mine = by_index([total] + [swap(total, "pack", k) for k in other_chips()], chip)
    return by_core(mine, swap(mine, "pack", 1), 1).reshape(value.shape)


def sum_plane(value):
    return sum_chips(value + swap(value, "pack", 1))


def sum_chips(value):
    return tree_sum([value] + [swap(value, "pack", k) for k in other_chips()])


def _dot(left, right, dims):
    return lax.dot_general(left, right, (dims, ((), ())), preferred_element_type=F32)


NT = ((1,), (1,))
TN = ((0,), (0,))
NN = ((1,), (0,))


def _window(ref, block, blocks, column):
    places = (jnp.maximum(block - 1, 0), block, jnp.minimum(block + 1, blocks - 1))
    return jnp.concatenate(
        [ref[pl.ds(pl.multiple_of(place * BLOCK, BLOCK), BLOCK), column : column + PAIR] for place in places],
        axis=0,
    )


def _halves(value):
    lane = lax.broadcasted_iota(jnp.int32, value.shape, 1)
    zero = jnp.zeros_like(value)
    return jnp.concatenate(
        [jnp.where(lane < HEAD_DIM, value, zero), jnp.where(lane < HEAD_DIM, zero, value)], axis=0
    )


def _merge(value):
    return jnp.concatenate([value[:HEAD_DIM, :BLOCK], value[HEAD_DIM:, BLOCK:]], axis=0).T


def attend_kernel(width, blocks, rows_ref, query_id_ref, key_id_ref, out_ref, log_ref):
    block = pl.program_id(0)
    here = pl.ds(pl.multiple_of(block * BLOCK, BLOCK), BLOCK)
    allowed = key_id_ref[pl.ds(pl.multiple_of(block * BLOCK, BLOCK), 3 * BLOCK), :] == query_id_ref[0]
    for pair in range(width // PAIR):
        column = pair * PAIR
        queries = _halves(rows_ref[here, column : column + PAIR] * SCALE)
        keys = _window(rows_ref, block, blocks, width + column)
        values = _window(rows_ref, block, blocks, 2 * width + column)
        mixed = []
        for lanes in (slice(0, BLOCK), slice(BLOCK, 2 * BLOCK)):
            scores = jnp.where(allowed, _dot(keys, queries[lanes], NT), NEG)
            top = jnp.max(scores, axis=0, keepdims=True)
            raised = jnp.exp(scores - top)
            total = jnp.sum(raised, axis=0, keepdims=True)
            probs = (raised * (1.0 / total)).astype(LOW)
            log_ref[0, pair : pair + 1, lanes] = top + jnp.log(total)
            mixed.append(_dot(values, probs, TN))
        out_ref[:, column : column + PAIR] = _merge(jnp.concatenate(mixed, axis=1)).astype(LOW)


def attend_back_kernel(
    width, blocks, rows_ref, grad_ref, log_ref, query_id_ref, key_id_ref, out_ref, key_sum, value_sum
):
    block = pl.program_id(0)

    @pl.when(block == 0)
    def _():
        key_sum[...] = jnp.zeros_like(key_sum)
        value_sum[...] = jnp.zeros_like(value_sum)

    span = pl.ds(pl.multiple_of(block * BLOCK, BLOCK), 3 * BLOCK)
    here = pl.ds(pl.multiple_of(block * BLOCK, BLOCK), BLOCK)
    allowed = key_id_ref[span, :] == query_id_ref[0]
    allowed = jnp.concatenate([allowed, allowed], axis=1)
    for pair in range(width // PAIR):
        column = pair * PAIR
        lanes = slice(column, column + PAIR)
        queries = _halves(rows_ref[here, lanes] * SCALE)
        grads = _halves(grad_ref[here, lanes])
        keys = _window(rows_ref, block, blocks, width + column)
        values = _window(rows_ref, block, blocks, 2 * width + column)
        scores = jnp.where(allowed, _dot(keys, queries, NT), NEG)
        probs = jnp.exp(scores - log_ref[0, pair : pair + 1, :])
        grad_probs = _dot(values, grads, NT)
        inner = jnp.sum(probs * grad_probs, axis=0, keepdims=True)
        grad_scores = (probs * (grad_probs - inner)).astype(LOW)
        out_ref[here, lanes] = (_merge(_dot(keys, grad_scores, TN)) * SCALE).astype(LOW)
        key_sum[span, lanes] += _dot(grad_scores, queries, NN)
        value_sum[span, lanes] += _dot(probs.astype(LOW), grads, NN)

    @pl.when(block == blocks - 1)
    def _():
        def write(place, carry):
            into = pl.ds(pl.multiple_of(place * BLOCK, BLOCK), BLOCK)
            source = pl.ds(pl.multiple_of((place + 1) * BLOCK, BLOCK), BLOCK)
            out_ref[into, width : 2 * width] = key_sum[source, :].astype(LOW)
            out_ref[into, 2 * width :] = value_sum[source, :].astype(LOW)
            return carry

        lax.fori_loop(0, blocks, write, 0)


def _params():
    return pltpu.CompilerParams(dimension_semantics=("arbitrary",), vmem_limit_bytes=56 << 20)


def attend(qkv_rows, query_id, key_id):
    rows, triple = qkv_rows.shape
    width, blocks = triple // 3, rows // BLOCK
    heads = width // HEAD_DIM
    return pl.pallas_call(
        lambda *refs: attend_kernel(width, blocks, *refs),
        grid=(blocks,),
        in_specs=[
            pl.BlockSpec((rows, triple), lambda i: (0, 0)),
            pl.BlockSpec((1, 1, BLOCK), lambda i: (i, 0, 0)),
            pl.BlockSpec((rows + 2 * BLOCK, 1), lambda i: (0, 0)),
        ],
        out_specs=[
            pl.BlockSpec((BLOCK, width), lambda i: (i, 0)),
            pl.BlockSpec((1, heads // 2, 2 * BLOCK), lambda i: (i, 0, 0)),
        ],
        out_shape=[
            jax.ShapeDtypeStruct((rows, width), LOW),
            jax.ShapeDtypeStruct((blocks, heads // 2, 2 * BLOCK), F32),
        ],
        compiler_params=_params(),
        cost_estimate=NO_COST,
    )(qkv_rows, query_id, key_id)


def attend_back(qkv_rows, grad_rows, log_total, query_id, key_id):
    rows, triple = qkv_rows.shape
    width, blocks = triple // 3, rows // BLOCK
    heads = width // HEAD_DIM
    return pl.pallas_call(
        lambda *refs: attend_back_kernel(width, blocks, *refs),
        grid=(blocks,),
        in_specs=[
            pl.BlockSpec((rows, triple), lambda i: (0, 0)),
            pl.BlockSpec((rows, width), lambda i: (0, 0)),
            pl.BlockSpec((1, heads // 2, 2 * BLOCK), lambda i: (i, 0, 0)),
            pl.BlockSpec((1, 1, BLOCK), lambda i: (i, 0, 0)),
            pl.BlockSpec((rows + 2 * BLOCK, 1), lambda i: (0, 0)),
        ],
        out_specs=pl.BlockSpec((rows, triple), lambda i: (0, 0)),
        out_shape=jax.ShapeDtypeStruct((rows, triple), LOW),
        scratch_shapes=[
            pltpu.VMEM((rows + 2 * BLOCK, width), F32),
            pltpu.VMEM((rows + 2 * BLOCK, width), F32),
        ],
        compiler_params=_params(),
        cost_estimate=NO_COST,
    )(qkv_rows, grad_rows, log_total, query_id, key_id)


def layer_norm(values, gain_row, bias_row):
    centre = values - jnp.mean(values, axis=-1, keepdims=True)
    spread = jnp.mean(centre * centre, axis=-1, keepdims=True)
    return centre * lax.rsqrt(spread + 1e-06) * gain_row + bias_row


def norm_back_kernel(
    groups, keep_sum, values_ref, cot_ref, more_ref, gain_ref, low_ref, sum_ref, out_ref=None
):
    @pl.when(pl.program_id(0) == 0)
    def _():
        sum_ref[...] = jnp.zeros_like(sum_ref)

    values = values_ref[...]
    if groups:
        group = lax.broadcasted_iota(jnp.int32, (values.shape[0], groups), 1)
        chosen = jnp.where(more_ref[...] == group, 1.0, 0.0)
        cot = jnp.dot(chosen, cot_ref[...], precision=HIGHEST_PREC, preferred_element_type=F32)
    else:
        cot = cot_ref[...]
    centre = values - jnp.mean(values, axis=-1, keepdims=True)
    scale = lax.rsqrt(jnp.mean(centre * centre, axis=-1, keepdims=True) + 1e-06)
    normed = centre * scale
    scaled = cot * gain_ref[...]
    grad = scale * (
        scaled
        - jnp.mean(scaled, axis=-1, keepdims=True)
        - normed * jnp.mean(scaled * normed, axis=-1, keepdims=True)
    )
    if not groups:
        grad = grad + more_ref[...]
    low = grad.astype(LOW)
    if keep_sum:
        out_ref[...] = grad
    low_ref[...] = low
    for row, value in enumerate((cot * normed, cot, low.astype(F32))):
        sum_ref[row : row + 1, :] += jnp.sum(value, axis=0, keepdims=True)


def norm_back(values, gain_row, cotangent, more, keep_sum=True):
    rows, width = values.shape
    groups = cotangent.shape[0] if more.shape[1] == 1 else 0
    tile = rows // 8
    block = pl.BlockSpec((tile, width), lambda i: (i, 0))
    line = pl.BlockSpec((1, width), lambda i: (0, 0))
    out_specs = [block, pl.BlockSpec((8, width), lambda i: (0, 0))]
    out_shape = [jax.ShapeDtypeStruct((rows, width), LOW), jax.ShapeDtypeStruct((8, width), F32)]
    if keep_sum:
        out_specs.append(block)
        out_shape.append(jax.ShapeDtypeStruct((rows, width), F32))
    return pl.pallas_call(
        lambda *refs: norm_back_kernel(groups, keep_sum, *refs),
        grid=(8,),
        in_specs=[
            block,
            pl.BlockSpec((groups, width), lambda i: (0, 0)) if groups else block,
            pl.BlockSpec((tile, 1), lambda i: (i, 0)) if groups else block,
            line,
        ],
        out_specs=out_specs,
        out_shape=out_shape,
        compiler_params=_params(),
        cost_estimate=NO_COST,
    )(values, cotangent, more, gain_row[None])


def small_kernel(spots_ref, first_ref, second_ref, last_ref, qkv_ref, up_ref, out_ref):
    width, slots = out_ref.shape[1], spots_ref.shape[0]
    out_ref[...] = jnp.zeros_like(out_ref)
    rows = [(first_ref, 0), (first_ref, 1), (second_ref, 0), (second_ref, 1), (last_ref, 0), (last_ref, 1)]
    rows += [(first_ref, 2), (qkv_ref, 0), (qkv_ref, 2), (second_ref, 2), (last_ref, 2)]
    for row, (ref, which) in enumerate(rows):
        if ref is qkv_ref:
            out_ref[row : row + 1, :] = ref[:, which * width : (which + 1) * width]
        else:
            out_ref[row : row + 1, :] = ref[which : which + 1, :]
    for slot in range(slots):
        out_ref[pl.ds(16 + spots_ref[slot], 1), :] = up_ref[slot : slot + 1, :]


def small_sums(first, second, last, qkv_sum, up_sums):
    width, count = first.shape[1], lax.axis_size("pack")
    spots = relative_packs() ^ lax.axis_index("pack")
    up_sum = jnp.concatenate(up_sums).reshape(count, -1)
    arrays = [first, second, last, qkv_sum[None], jnp.pad(up_sum, ((0, 0), (0, width - up_sum.shape[1])))]
    return pl.pallas_call(
        small_kernel,
        in_specs=[pl.BlockSpec(memory_space=pltpu.SMEM)] + [pl.BlockSpec(memory_space=pltpu.VMEM)] * len(arrays),
        out_specs=pl.BlockSpec(memory_space=pltpu.VMEM),
        out_shape=jax.ShapeDtypeStruct((16 + count, width), F32),
        compiler_params=pltpu.CompilerParams(vmem_limit_bytes=16 << 20),
        cost_estimate=NO_COST,
    )(spots, *arrays)


def gelu(values):
    return 0.5 * values * (1.0 + lax.erf(values * math.sqrt(0.5)))


def gelu_slope(values):
    return 0.5 * (1.0 + lax.erf(values * math.sqrt(0.5))) + values * (
        math.sqrt(0.5 / math.pi) * jnp.exp(-0.5 * values * values)
    )


def as_rows(value, width):
    flat = value.reshape(1, -1)
    return jnp.pad(flat, ((0, 7), (0, width - flat.shape[1])))


def from_rows(cells, shape):
    rows, columns = shape
    flat = cells[:, 0, : rows * columns].reshape(-1, rows, columns)
    return flat.transpose(1, 0, 2).reshape(rows, -1)


def mm(spec, left, right):
    return jnp.einsum(spec, left, right, preferred_element_type=F32)


def column_sum(rows):
    return jnp.sum(rows.astype(F32), axis=0)


def hmul(left, right):
    return jnp.dot(left, right, precision=NS_PREC, preferred_element_type=F32)


def ortho(columns):
    gram_mat = pack_sum(
        lax.dot_general(columns, columns, (TN, ((), ())), precision=NS_PREC, preferred_element_type=F32)
    )
    scale = 1.0 / (jnp.sqrt(jnp.trace(gram_mat)) + 1e-07)
    iterate = columns * scale
    gram_mat = gram_mat * scale * scale
    eye = jnp.eye(gram_mat.shape[0], dtype=F32)
    for step in range(NS_STEPS):
        if step < NS_STEPS - 1:
            square = hmul(gram_mat, gram_mat)
            poly = COEF_ONE * eye + COEF_TWO * gram_mat + COEF_THREE * square
            poly_gram = COEF_ONE * gram_mat + COEF_TWO * square + COEF_THREE * hmul(square, gram_mat)
            iterate = hmul(iterate, poly)
            gram_mat = hmul(poly, poly_gram)
        else:
            first_pass = hmul(iterate, gram_mat)
            iterate = COEF_ONE * iterate + COEF_TWO * first_pass + COEF_THREE * hmul(first_pass, gram_mat)
    return iterate


def to_planes(shards):
    seq_count, seq_place = lax.axis_size("seq"), lax.axis_index("seq")
    most = max(m.shape[0] for m in shards)
    filled = [jnp.pad(m, ((0, most - m.shape[0]), (0, 0))) for m in shards]
    filled += [jnp.zeros_like(filled[0])] * (seq_count - len(shards))
    stacked = jnp.stack(filled)
    parts = [pick(stacked, seq_place)]
    parts += [swap(pick(stacked, seq_place ^ k), "seq", k) for k in range(1, seq_count)]
    return jnp.stack(parts)


def from_planes(value, counts):
    back = [value[0]] + [swap(value[k], "seq", k) for k in range(1, lax.axis_size("seq"))]
    return [_choose(back, lax.axis_index("seq"), m)[:count] for m, count in enumerate(counts)]


def muon_update(weight, iterate):
    col_ratio = math.sqrt(
        max(1.0, iterate.shape[1] * lax.axis_size(("pack", "seq")) / weight.shape[0])
    )
    return weight * (1.0 - MUON_RATE * DECAY) - MUON_RATE * col_ratio * iterate


def adam_update(weight, first_moment, second_moment, gradient, factor, count_float):
    scaled = factor * gradient
    new_first = BETA_ONE * first_moment + (1.0 - BETA_ONE) * scaled
    new_second = BETA_TWO * second_moment + (1.0 - BETA_TWO) * scaled * scaled
    first_hat = new_first / (1.0 - jnp.power(BETA_ONE, count_float))
    second_hat = new_second / (1.0 - jnp.power(BETA_TWO, count_float))
    new_weight = weight - ADAM_RATE * (first_hat / (jnp.sqrt(second_hat) + 1e-08) + DECAY * weight)
    return (new_weight, new_first, new_second)


def deal_rows(lengths, keep_mask, shard_len):
    packs, images = lengths.shape
    seq_count, seq_place = lax.axis_size("seq"), lax.axis_index("seq")
    image_range = jnp.arange(images, dtype=jnp.int32)
    upto = image_range[None, :] <= image_range[:, None]
    ends = jnp.sum(jnp.where(upto[None], lengths[:, None, :], 0), axis=2, dtype=jnp.int32)
    starts = ends - lengths
    cuts = jnp.arange(1, seq_count, dtype=jnp.int32) * shard_len
    straddles = (starts[:, None, :] < cuts[None, :, None]) & (ends[:, None, :] > cuts[None, :, None])
    behind = jnp.sum(jnp.where(straddles, cuts[None, :, None] - starts[:, None, :], 0), axis=2, dtype=jnp.int32)
    ahead = jnp.sum(jnp.where(straddles, ends[:, None, :] - cuts[None, :, None], 0), axis=2, dtype=jnp.int32)
    excess = jnp.zeros_like(cuts)
    moves = []
    for pack in range(packs):
        more, less = excess + ahead[pack], excess - behind[pack]
        forward = jnp.abs(more) <= jnp.abs(less)
        excess = jnp.where(forward, more, less)
        moves.append(jnp.where(forward, ahead[pack], -behind[pack]))
    borders = jnp.concatenate(
        [
            jnp.zeros((packs, 1), jnp.int32),
            cuts[None, :] + jnp.stack(moves),
            jnp.full((packs, 1), PACK_LEN, jnp.int32),
        ],
        axis=1,
    )
    first = lax.dynamic_index_in_dim(borders, seq_place, 1, keepdims=False)
    held = lax.dynamic_index_in_dim(borders, seq_place + 1, 1, keepdims=False) - first
    pack_range = jnp.arange(packs, dtype=jnp.int32)
    before = jnp.sum(jnp.where(pack_range[None, :] < pack_range[:, None], held[None, :], 0), axis=1, dtype=jnp.int32)
    row = jnp.arange(packs * shard_len + MAXLEN, dtype=jnp.int32)
    in_pack = (row[:, None] >= before[None, :]) & (row[:, None] < (before + held)[None, :])
    valid = jnp.any(in_pack, axis=1)

    def of_pack(values):
        return jnp.sum(jnp.where(in_pack, values, 0), axis=1, dtype=jnp.int32)

    pack_of = of_pack(pack_range[None, :])
    place = of_pack(row[:, None] - before[None, :] + first[None, :])
    window = shard_len + 2 * MAXLEN
    source = jnp.where(valid, pack_of * window + place - (seq_place * shard_len - MAXLEN), -1)
    row_ends = jnp.sum(jnp.where(in_pack[:, :, None], ends[None], 0), axis=1, dtype=jnp.int32)
    row_starts = jnp.sum(jnp.where(in_pack[:, :, None], starts[None], 0), axis=1, dtype=jnp.int32)
    image_of = jnp.sum((place[:, None] >= row_ends).astype(jnp.int32), axis=1, dtype=jnp.int32)
    is_first = jnp.any(place[:, None] == row_starts, axis=1)
    keep_rows = mm("rp,pj->rj", in_pack.astype(LOW), (keep_mask > 0).astype(LOW))
    spot = jnp.arange(PACK_LEN, dtype=jnp.int32)
    kept = jnp.any((place[:, None] == spot[None, :]) & (keep_rows > 0.5), axis=1)
    live = valid & (kept | is_first)
    group = jnp.where(valid, pack_of * images + image_of, -1)

    spots = jnp.arange(PACK_LEN, dtype=jnp.int32)[None, None, :]
    inside = (spots >= starts[:, :, None]) & (spots < ends[:, :, None])
    counted = inside & ((keep_mask > 0)[:, None, :] | (spots == starts[:, :, None]))
    counts = jnp.sum(counted.astype(F32), axis=2)
    return source, group, live, counts.reshape(-1)


def body(
    patches,
    lengths,
    keep_mask,
    labels,
    step_count,
    embed_weight,
    embed_first,
    embed_second,
    qkv_weight,
    qkv_moment,
    output_weight,
    output_moment,
    up_weight,
    up_moment,
    down_weight,
    down_moment,
    small_params,
    small_first,
    small_second,
    head_weight,
    head_first,
    head_second,
    head_bias,
    bias_first,
    bias_second,
):
    packs, shard_len, patch_in = patches.shape
    images = lengths.shape[1]
    width = qkv_weight.shape[0]
    seq_count, seq_place = lax.axis_size("seq"), lax.axis_index("seq")
    pack_count, pack_place = lax.axis_size("pack"), lax.axis_index("pack")
    small_rows = small_params.shape[0]

    bundle = [
        embed_weight.T,
        qkv_weight.T,
        output_weight.T,
        as_rows(small_params, width),
        as_rows(head_bias, width),
    ]
    spots = [0]
    for piece in bundle:
        spots.append(spots[-1] + piece.shape[0])
    first = Gather(jnp.concatenate([piece.astype(LOW) for piece in bundle]))
    up_gather, down_gather = Gather(up_weight.T.astype(LOW)), Gather(down_weight.T.astype(LOW))
    first.along_seq()
    first.block, patches = hold(first.block, patches)
    first.in_plane()
    ends = seq_count - 1
    from_left = lax.ppermute(patches[:, shard_len - MAXLEN :], "seq", [(i, i + 1) for i in range(ends)])
    from_right = lax.ppermute(patches[:, :MAXLEN], "seq", [(i + 1, i) for i in range(ends)])
    window = jnp.concatenate([from_left, patches, from_right], axis=1).reshape(-1, patch_in)
    source, group, live, counts = deal_rows(lengths, keep_mask, shard_len)
    chosen = (source[:, None] == jnp.arange(window.shape[0], dtype=jnp.int32)[None, :]).astype(LOW)
    tokens = mm("rw,wi->ri", chosen, window).astype(LOW)
    tokens, up_gather.shard, *first.parts = hold(tokens, up_gather.shard, *first.parts)
    up_gather.send_seq()
    embed_full, qkv_full, output_full, small_full, bias_full = first.pieces(spots)
    embed_full, qkv_full, output_full = (
        value.reshape(-1, width) for value in (embed_full, qkv_full, output_full)
    )
    (gain_bias,) = hold(from_rows(small_full, small_params.shape).astype(F32))
    bias_full = lax.dynamic_slice_in_dim(bias_full, pack_place * seq_count, seq_count, 0)
    bias_full = bias_full[:, 0, : head_bias.shape[0]].reshape(-1)

    rows = tokens.shape[0]
    query_id = group.reshape(rows // BLOCK, 1, BLOCK)
    key_id = jnp.pad(jnp.where(live, group, -2), (BLOCK, BLOCK), constant_values=-2)[:, None]
    group_count = packs * images
    member = (
        (group[None, :] == jnp.arange(group_count, dtype=jnp.int32)[:, None]) & live[None, :]
    ).astype(F32)

    embedded = mm("ri,di->rd", tokens, embed_full) + gain_bias[6]
    embedded, up_gather.parts[0], down_gather.shard = hold(embedded, up_gather.parts[0], down_gather.shard)
    up_gather.join_seq()
    up_gather.in_plane()
    down_gather.doubling()
    normed_one = layer_norm(embedded, gain_bias[0], gain_bias[1]).astype(LOW)
    qkv_bias = jnp.concatenate([gain_bias[7], jnp.zeros_like(gain_bias[7]), gain_bias[8]])
    qkv_rows = (mm("rd,ed->re", normed_one, qkv_full) + qkv_bias).astype(LOW)
    qkv_rows, down_gather.block, head_low, *up_gather.parts = hold(
        qkv_rows, down_gather.block, head_weight.astype(LOW), *up_gather.parts
    )
    head_full = lax.all_gather(head_low, "seq", axis=0, tiled=True)
    down_gather.in_plane()
    up_full = [half.reshape(-1, width) for half in up_gather.halves()]
    attn_low, log_total = attend(qkv_rows, query_id, key_id)
    attn_low, *down_gather.parts = hold(attn_low, *down_gather.parts)
    down_full = [half.reshape(-1, width) for half in down_gather.halves()]
    after_attn = embedded + mm("re,de->rd", attn_low, output_full) + gain_bias[9]
    normed_two = layer_norm(after_attn, gain_bias[2], gain_bias[3]).astype(LOW)
    up_bias = jnp.take(
        gain_bias[11:15].reshape(pack_count, -1), relative_packs() ^ pack_place, axis=0
    ).reshape(2, -1)
    up_rows = [mm("rd,fd->rf", normed_two, up_full[half]) + up_bias[half] for half in range(2)]
    active = [gelu(rows).astype(LOW) for rows in up_rows]
    after_mlp = (
        after_attn
        + (mm("rf,fd->rd", active[0], down_full[0]) + mm("rf,fd->rd", active[1], down_full[1]))
        + gain_bias[10]
    )
    final_rows = layer_norm(after_mlp, gain_bias[4], gain_bias[5])
    pool_sums = jnp.dot(member, final_rows, precision=HIGHEST_PREC, preferred_element_type=F32)
    pooled_mine = (pool_sums / counts[:, None]).astype(LOW)

    img_share = group_count // seq_count
    split = pooled_mine.reshape(seq_count, img_share, width)
    pooled_low = tree_sum(
        [pick(split, seq_place).astype(F32)]
        + [swap(pick(split, seq_place ^ k), "seq", k).astype(F32) for k in range(1, seq_count)]
    ).astype(LOW)
    pooled_rows = jnp.concatenate(gather_blocks(pooled_low), axis=0).reshape(-1, width)
    depth = head_weight.shape[0]
    label_cols = head_full.shape[1]
    logits = mm("nd,dc->nc", pooled_rows, head_full) + bias_full.astype(F32)
    label_rows = jnp.take(
        pick(labels.reshape(pack_count, seq_count, img_share), seq_place, 1),
        relative_packs() ^ pack_place,
        axis=0,
    ).reshape(-1)
    class_ids = pack_place * label_cols + jnp.arange(label_cols, dtype=jnp.int32)
    valid = (class_ids < LABELS).astype(F32)
    target = (label_rows[:, None] == class_ids[None, :]).astype(F32)
    image_total = labels.shape[0] * labels.shape[1]
    loss_part = jnp.sum(valid[None, :] * (jax.nn.softplus(logits) - target * logits)) / image_total
    grad_logits = (valid[None, :] * (jax.nn.sigmoid(logits) - target) / image_total).astype(LOW)
    pooled_part = mm("nc,dc->nd", grad_logits, head_full).reshape(pack_count, img_share, width)
    pooled_grad = pack_scatter(pooled_part)
    pooled_grad = jnp.concatenate(absolute(relative(pooled_grad, "seq"), seq_place), axis=0)
    pooled_grad = pooled_grad / counts[:, None]

    traded, pooled_grad = hold(jnp.concatenate([pooled_rows, grad_logits], axis=1), pooled_grad)
    traded = lax.all_gather(traded, "seq", axis=0, tiled=True)

    grad_mlp_low, sums_last, grad_mlp = norm_back(
        after_mlp, gain_bias[4], pooled_grad, jnp.where(live, group, -1)[:, None]
    )
    down_sum, up_sum = Scatter(0, width, True), Scatter(1, width, True)
    half = width // 2
    late_sums = [Scatter(0, half), Scatter(1, half)]
    pair_sums = [Scatter(0, half), Scatter(1, half)]
    down_out = mm("rf,rd->fd", active[1], grad_mlp_low)
    down_keep = mm("rf,rd->fd", active[0], grad_mlp_low)
    grad_mlp_low, down_out, down_keep = hold(grad_mlp_low, down_out, down_keep)
    down_out = down_sum.start_halves(down_keep, down_out)
    grad_upper = [
        (mm("rd,fd->rf", grad_mlp_low, down_full[side]) * gelu_slope(up_rows[side])).astype(LOW)
        for side in range(2)
    ]
    up_out = mm("rf,rd->fd", grad_upper[1], normed_two)
    up_keep = mm("rf,rd->fd", grad_upper[0], normed_two)
    grad_upper[0], grad_upper[1], up_out, up_keep = hold(*grad_upper, up_out, up_keep)
    up_out = up_sum.start_halves(up_keep, up_out)
    grad_normed = mm("rf,fd->rd", grad_upper[0], up_full[0]) + mm("rf,fd->rd", grad_upper[1], up_full[1])
    down_out = down_sum.step(down_out)
    grad_normed, down_out = hold(grad_normed, down_out)
    grad_attn_low, sums_second, grad_attn = norm_back(
        after_attn, gain_bias[2], grad_normed, grad_mlp
    )
    grad_mixed = mm("rd,de->re", grad_attn_low, output_full).astype(LOW)
    up_out = up_sum.step(up_out)
    grad_mixed, up_out = hold(grad_mixed, up_out)
    grad_qkv = attend_back(qkv_rows, grad_mixed, log_total, query_id, key_id)
    down_out, up_out = down_sum.step(down_out), up_sum.step(up_out)
    grad_qkv, down_out, up_out = hold(grad_qkv, down_out, up_out)
    grad_normed = mm("re,ed->rd", grad_qkv, qkv_full)
    grad_embed_rows, sums_first = norm_back(embedded, gain_bias[0], grad_normed, grad_attn, keep_sum=False)
    output_grad = mm("rd,re->de", grad_attn_low, attn_low)
    embed_grad = mm("rd,ri->di", grad_embed_rows, tokens)
    down_sum.finish(down_out)
    up_sum.finish(up_out)
    early = jnp.concatenate([down_sum.value, up_sum.value], axis=1)
    pair_keep, pair_out = late_halves(output_grad, embed_grad)
    grad_qkv, pair_out, early = hold(grad_qkv, pair_out, early)
    early = lax.psum_scatter(early, "seq", scatter_dimension=0)
    late_keep, late_out = late_halves(mm("re,rd->ed", grad_qkv, normed_one))
    pair = pair_keep + swap(pair_out, "pack", 1)
    pair_outs = [
        each.start_joined(part) for each, part in zip(pair_sums, (pair[..., :half], pair[..., half:]))
    ]
    late_out, grad_qkv, traded, *pair_outs = hold(late_out, grad_qkv, traded, *pair_outs)
    all_logits = traded[:, width:]
    bias_grad = pick(column_sum(all_logits).reshape(seq_count, -1), seq_place)
    late = late_keep + swap(late_out, "pack", 1)
    late_outs = [
        each.start_joined(part) for each, part in zip(late_sums, (late[..., :half], late[..., half:]))
    ]
    bias_grad, grad_qkv, traded, grad_upper[0], grad_upper[1], *held = hold(
        bias_grad, grad_qkv, traded, *grad_upper, *late_outs, *[each.keep for each in pair_sums]
    )
    late_outs = held[:2]
    pair_sums[0].keep, pair_sums[1].keep = held[2:]
    all_pooled = pick(traded[:, :width].reshape(-1, seq_count, head_weight.shape[0]), seq_place, 1)
    head_grad = mm("nd,nc->dc", all_pooled, traded[:, width:])
    small_mine = small_sums(
        sums_first, sums_second, sums_last, column_sum(grad_qkv), [column_sum(side) for side in grad_upper]
    )
    for each, sent in zip(pair_sums, pair_outs):
        each.finish(sent)
    pair = jnp.concatenate([each.value for each in pair_sums], axis=2)
    late_outs = [each.step(sent) for each, sent in zip(late_sums, late_outs)]
    small_mine, head_grad, pair, *late_outs = hold(small_mine, head_grad, pair, *late_outs)
    small_total = small_mine + swap(small_mine, "pack", 1)
    for each, sent in zip(late_sums, late_outs):
        each.finish(sent)
    late_sum = SeqScatter(
        jnp.concatenate([jnp.concatenate([each.value for each in late_sums], axis=2), pair], axis=1)
    )
    late_out, small_total, early = hold(late_sum.send(), small_total, early)
    small_total = sum_chips(small_total)
    late_out = late_sum.step(late_out)
    late_out, small_total = hold(late_out, small_total)
    small_total = all_sum(small_total, "seq")
    while late_out is not None:
        late_out = late_sum.step(late_out)
    late_sum.value, small_total = hold(late_sum.value, small_total)
    down_share, up_share = jnp.split(early, 2)
    late_share = late_sum.result()
    widths = [qkv_weight.shape[1], output_weight.shape[1], embed_weight.shape[1]]
    qkv_share, output_share = late_share[: widths[0]], late_share[widths[0] : widths[0] + widths[1]]
    embed_share = late_share[widths[0] + widths[1] :].T
    hidden = down_weight.shape[1] * seq_count
    small_total = jnp.concatenate(
        [small_total[:11], small_total[16:, :hidden].reshape(small_rows - 11, width)], axis=0
    )
    place = pack_place * seq_count + seq_place
    small_share = pick(small_total.reshape(small_rows, pack_count * seq_count, -1), place, 1)

    shares = (early, late_share, head_grad, bias_grad)
    square_sum = sum((jnp.sum(piece * piece) for piece in shares))
    sums = jnp.broadcast_to(jnp.stack([loss_part, square_sum])[:, None], (2, BLOCK))
    sums = sum_plane(all_sum(sums, "seq"))
    loss_value, square_total = sums[0, 0], sums[1, 0] + jnp.sum(small_total * small_total)
    grad_norm = jnp.sqrt(square_total)
    factor = jnp.minimum(1.0, CLIP_NORM / (grad_norm + 1e-06))
    muon_shares = (qkv_share, output_share, up_share, down_share)
    moments = [
        MUON_MU * moment.T + factor * share
        for moment, share in zip((qkv_moment, output_moment, up_moment, down_moment), muon_shares)
    ]
    columns = to_planes(moments)
    iterates = ortho(columns.reshape(-1, width)).reshape(columns.shape)
    iterates = [iterate.T for iterate in from_planes(iterates, [m.shape[0] for m in moments])]
    moments = [moment.T for moment in moments]
    new_qkv = muon_update(qkv_weight, iterates[0])
    new_output = muon_update(output_weight, iterates[1])
    new_up = muon_update(up_weight, iterates[2])
    new_down = muon_update(down_weight, iterates[3])
    count_float = step_count[0].astype(F32)
    new_embed, new_embed_first, new_embed_second = adam_update(
        embed_weight, embed_first, embed_second, embed_share, factor, count_float
    )
    new_small, new_small_first, new_small_second = adam_update(
        small_params, small_first, small_second, small_share, factor, count_float
    )
    new_head, new_head_first, new_head_second = adam_update(
        head_weight, head_first, head_second, head_grad, factor, count_float
    )
    new_bias, new_bias_first, new_bias_second = adam_update(
        head_bias, bias_first, bias_second, bias_grad, factor, count_float
    )
    return (
        loss_value,
        grad_norm,
        new_embed,
        new_embed_first,
        new_embed_second,
        new_qkv,
        moments[0],
        new_output,
        moments[1],
        new_up,
        moments[2],
        new_down,
        moments[3],
        new_small,
        new_small_first,
        new_small_second,
        new_head,
        new_head_first,
        new_head_second,
        new_bias,
        new_bias_first,
        new_bias_second,
    )


def solution(mesh):
    both = P(None, ("pack", "seq"))
    head = P("seq", "pack")
    line = P(("pack", "seq"))
    return jax.shard_map(
        body,
        mesh=mesh,
        in_specs=(P("pack", "seq", None), P("pack", None), P("pack", None), P(), P())
        + (both,) * 14
        + (head,) * 3
        + (line,) * 3,
        out_specs=(P(), P()) + (both,) * 14 + (head,) * 3 + (line,) * 3,
        check_vma=False,
    )
```

```python
import math

import jax
import jax.numpy as jnp
from jax import lax
from jax.experimental import pallas as pl
from jax.experimental.pallas import tpu as pltpu
from jax.sharding import PartitionSpec as P

HEAD_DIM = 64
LABELS = 21843
PACK_LEN = 1024
MAXLEN = 128
NS_STEPS = 2
BLOCK = 128
PAIR = 2 * HEAD_DIM

HIGHEST_PREC = lax.Precision.HIGHEST
NS_PREC = lax.Precision.HIGH
CLIP_NORM = 1.0
MUON_MU = 0.95
MUON_RATE = 1.0
ADAM_RATE = 0.02
BETA_ONE = 0.9
BETA_TWO = 0.95
DECAY = 0.01
COEF_ONE = 3.4445
COEF_TWO = -4.775
COEF_THREE = 2.0315
SCALE = HEAD_DIM ** (-0.5)
LOW = jnp.bfloat16
F32 = jnp.float32
NEG = -1e30
NO_COST = pl.CostEstimate(flops=0, bytes_accessed=0, transcendentals=0)


def swap(value, axis, bit):
    return lax.ppermute(value, axis, [(i, i ^ bit) for i in range(lax.axis_size(axis))])


def pick(value, index, dim=0):
    return lax.dynamic_index_in_dim(value, index, dim, keepdims=False)


def tree_sum(parts):
    while len(parts) > 1:
        parts = [parts[i] + parts[i + 1] for i in range(0, len(parts), 2)]
    return parts[0]


def relative(value, axis):
    return [value] + [swap(value, axis, k) for k in range(1, lax.axis_size(axis))]


def absolute(parts, place):
    return [_choose(parts, place, j) for j in range(len(parts))]


def _choose(parts, place, j):
    out = parts[j]
    for other in range(1, len(parts)):
        out = jnp.where(place == other, parts[j ^ other], out)
    return out


def all_sum(value, axis):
    return tree_sum(relative(value, axis))


def hold(*values):
    return lax.optimization_barrier(values)


def other_chips():
    return list(range(2, lax.axis_size("pack"), 2))


def relative_packs():
    same = [0] + other_chips()
    return jnp.array(same + [k + 1 for k in same], jnp.int32)


def relative_slots():
    count = lax.axis_size("pack")
    offset = lax.axis_index("pack") ^ jnp.arange(count, dtype=jnp.int32)
    return (offset >> 1) + (offset & 1) * (count // 2)


def gather_blocks(block):
    own = jnp.stack([block] + [swap(block, "pack", k) for k in other_chips()])
    return own, swap(own, "pack", 1)


def by_index(parts, place):
    if len(parts) <= 8:
        return jnp.stack(absolute(parts, place))
    value = jnp.stack(parts)
    shape, bit = value.shape, 1
    while bit < len(parts):
        value = value.reshape((-1, 2, bit) + shape[1:])
        turned = jnp.concatenate([value[:, 1:], value[:, :1]], axis=1)
        value = jnp.where((place & bit) == 0, value, turned)
        bit *= 2
    return value.reshape(shape)


def by_core(own, other, dim):
    return jnp.where(
        (lax.axis_index("pack") & 1) == 0, jnp.stack([own, other], axis=dim), jnp.stack([other, own], axis=dim)
    )


class Gather:
    def __init__(self, shard):
        self.shard = shard

    def along_seq(self):
        self.block = by_index(relative(self.shard, "seq"), lax.axis_index("seq"))

    def send_seq(self):
        self.parts = relative(self.shard, "seq")

    def join_seq(self):
        self.block = by_index(self.parts, lax.axis_index("seq"))

    def doubling(self):
        place, count, bit = lax.axis_index("seq"), lax.axis_size("seq"), 1
        block = self.shard[None]
        while bit < count:
            other = swap(block, "seq", bit)
            block = jnp.where(
                (place & bit) == 0,
                jnp.concatenate([block, other], axis=0),
                jnp.concatenate([other, block], axis=0),
            )
            bit *= 2
        self.block = block
        return block

    def in_plane(self):
        self.parts = [self.block] + [swap(self.block, "pack", k) for k in other_chips()]

    def pieces(self, spots):
        mine = by_index(self.parts, lax.axis_index("pack") >> 1)
        other = swap(mine, "pack", 1)
        return [
            by_core(mine[:, :, here:there], other[:, :, here:there], 1).reshape(-1, there - here, mine.shape[-1])
            for here, there in zip(spots[:-1], spots[1:])
        ]

    def halves(self):
        own = jnp.stack(self.parts)
        return own, swap(own, "pack", 1)


class Scatter:
    def __init__(self, order, width, relative=False):
        self.left = [1 << b for b in reversed(range(lax.axis_size("pack").bit_length() - 1))]
        chips = [b for b in self.left if b > 1]
        self.order = [1] + (chips if order == 0 else chips[::-1])
        self.relative, self.width = relative, width

    def start_halves(self, keep, send):
        self.left.remove(1)
        self.bit = self.order.pop(0)
        shape = (2,) * len(self.left) + (lax.axis_size("seq"), -1, self.width)
        self.keep = keep.reshape(shape)
        return send.reshape(shape)

    def start_joined(self, value):
        self.left.remove(1)
        self.order.pop(0)
        self.value = value
        return self.send()

    def send(self):
        self.bit = bit = self.order.pop(0)
        dim = self.left.index(bit)
        self.left.remove(bit)
        if self.relative:
            self.keep = lax.index_in_dim(self.value, 0, dim, keepdims=False)
            return lax.index_in_dim(self.value, 1, dim, keepdims=False)
        mine = (lax.axis_index("pack") & bit) // bit
        self.keep = pick(self.value, mine, dim)
        return pick(self.value, 1 - mine, dim)

    def step(self, sent):
        self.value = self.keep + swap(sent, "pack", self.bit)
        return self.send() if self.order else None

    def finish(self, sent):
        while sent is not None:
            sent = self.step(sent)


class SeqScatter:
    def __init__(self, value):
        self.value, self.bit = value, 1

    def send(self):
        tail = self.value.shape[-2:]
        split = self.value.reshape((-1, 2) + tail)
        mine = (lax.axis_index("seq") & self.bit) // self.bit
        self.keep = pick(split, mine, 1)
        return pick(split, 1 - mine, 1)

    def step(self, sent):
        self.value = self.keep + swap(sent, "seq", self.bit)
        self.bit *= 2
        return self.send() if self.bit < lax.axis_size("seq") else None

    def result(self):
        return self.value.reshape(self.value.shape[-2:])


def late_halves(*grads):
    seq_count, pack_count = lax.axis_size("seq"), lax.axis_size("pack")
    chips = (2,) * (pack_count.bit_length() - 2)
    core = lax.axis_index("pack") & 1

    def half(which):
        pieces = [
            pick(grad.reshape(chips + (2, seq_count, -1, grad.shape[1])), which, len(chips)) for grad in grads
        ]
        return jnp.concatenate(pieces, axis=-2)

    return half(core), half(1 - core)


def pack_scatter(value):
    half = value.shape[0] // 2
    mine = value[:half] + swap(value[half:], "pack", 1)
    parts = [mine[0]] + [swap(mine[k // 2], "pack", k) for k in other_chips()]
    return tree_sum(parts)


def column_all_sum(value):
    seq_place, count = lax.axis_index("seq"), lax.axis_size("seq")
    core = lax.axis_index("pack") & 1
    split = value.reshape(2, count, -1, value.shape[1])
    mine = pick(split, core) + swap(pick(split, 1 - core), "pack", 1)
    parts = [pick(mine, seq_place)] + [swap(pick(mine, seq_place ^ k), "seq", k) for k in range(1, count)]
    mine = by_index(relative(tree_sum(parts), "seq"), seq_place)
    return by_core(mine, swap(mine, "pack", 1), 0).reshape(value.shape)


def fold(matrix):
    count, width = matrix.shape[0] // BLOCK, matrix.shape[0]

    def row(i):
        return matrix[i * BLOCK : (i + 1) * BLOCK, i * BLOCK :]

    return jnp.concatenate(
        [jnp.concatenate([row(i), row(count - 1 - i)], axis=1) for i in range(count // 2)], axis=0
    )


def unfold_kernel(folded_ref, out_ref, scale_ref):
    width = out_ref.shape[0]
    count = width // BLOCK

    def block(i, j):
        line = min(i, count - 1 - i)
        column = (j - i) * BLOCK + (0 if line == i else width - line * BLOCK)
        return folded_ref[line * BLOCK : (line + 1) * BLOCK, column : column + BLOCK]

    row = lax.broadcasted_iota(jnp.int32, (BLOCK, BLOCK), 0)
    column = lax.broadcasted_iota(jnp.int32, (BLOCK, BLOCK), 1)
    diagonal = jnp.zeros((BLOCK, BLOCK), F32)
    for i in range(count):
        diagonal += jnp.where(row == column, block(i, i), 0.0)
    trace = jnp.sum(jnp.sum(diagonal, axis=0, keepdims=True), axis=1, keepdims=True)
    scale = 1.0 / (jnp.sqrt(trace) + 1e-07)
    for i in range(count):
        for j in range(i, count):
            value = block(i, j) * scale * scale
            out_ref[i * BLOCK : (i + 1) * BLOCK, j * BLOCK : (j + 1) * BLOCK] = value
            if j > i:
                out_ref[j * BLOCK : (j + 1) * BLOCK, i * BLOCK : (i + 1) * BLOCK] = value.T
    scale_ref[...] = jnp.broadcast_to(scale, scale_ref.shape)


def unfold(folded, width):
    whole = pl.BlockSpec(memory_space=pltpu.VMEM)
    matrix, scale = pl.pallas_call(
        unfold_kernel,
        in_specs=[whole],
        out_specs=[whole, whole],
        out_shape=[jax.ShapeDtypeStruct((width, width), F32), jax.ShapeDtypeStruct((8, BLOCK), F32)],
        compiler_params=pltpu.CompilerParams(vmem_limit_bytes=32 << 20),
        cost_estimate=NO_COST,
    )(folded)
    return matrix, scale[0, 0]


def sum_plane(value):
    return sum_chips(value + swap(value, "pack", 1))


def sum_chips(value):
    return tree_sum([value] + [swap(value, "pack", k) for k in other_chips()])


def _dot(left, right, dims):
    return lax.dot_general(left, right, (dims, ((), ())), preferred_element_type=F32)


NT = ((1,), (1,))
TN = ((0,), (0,))
NN = ((1,), (0,))


def _window(ref, block, blocks, column):
    places = (jnp.maximum(block - 1, 0), block, jnp.minimum(block + 1, blocks - 1))
    return jnp.concatenate(
        [ref[pl.ds(pl.multiple_of(place * BLOCK, BLOCK), BLOCK), column : column + PAIR] for place in places],
        axis=0,
    )


def _halves(value):
    lane = lax.broadcasted_iota(jnp.int32, value.shape, 1)
    zero = jnp.zeros_like(value)
    return jnp.concatenate(
        [jnp.where(lane < HEAD_DIM, value, zero), jnp.where(lane < HEAD_DIM, zero, value)], axis=0
    )


def _merge(value):
    return jnp.concatenate([value[:HEAD_DIM, :BLOCK], value[HEAD_DIM:, BLOCK:]], axis=0).T


def attend_kernel(width, blocks, rows_ref, query_id_ref, key_id_ref, out_ref, log_ref):
    block = pl.program_id(0)
    here = pl.ds(pl.multiple_of(block * BLOCK, BLOCK), BLOCK)
    allowed = key_id_ref[pl.ds(pl.multiple_of(block * BLOCK, BLOCK), 3 * BLOCK), :] == query_id_ref[0]
    for pair in range(width // PAIR):
        column = pair * PAIR
        queries = _halves(rows_ref[here, column : column + PAIR] * SCALE)
        keys = _window(rows_ref, block, blocks, width + column)
        values = _window(rows_ref, block, blocks, 2 * width + column)
        mixed = []
        for lanes in (slice(0, BLOCK), slice(BLOCK, 2 * BLOCK)):
            scores = jnp.where(allowed, _dot(keys, queries[lanes], NT), NEG)
            top = jnp.max(scores, axis=0, keepdims=True)
            raised = jnp.exp(scores - top)
            total = jnp.sum(raised, axis=0, keepdims=True)
            probs = (raised * (1.0 / total)).astype(LOW)
            log_ref[0, pair : pair + 1, lanes] = top + jnp.log(total)
            mixed.append(_dot(values, probs, TN))
        out_ref[:, column : column + PAIR] = _merge(jnp.concatenate(mixed, axis=1)).astype(LOW)


def attend_back_kernel(
    width, blocks, rows_ref, grad_ref, log_ref, query_id_ref, key_id_ref, out_ref, key_sum, value_sum
):
    block = pl.program_id(0)

    @pl.when(block == 0)
    def _():
        key_sum[...] = jnp.zeros_like(key_sum)
        value_sum[...] = jnp.zeros_like(value_sum)

    span = pl.ds(pl.multiple_of(block * BLOCK, BLOCK), 3 * BLOCK)
    here = pl.ds(pl.multiple_of(block * BLOCK, BLOCK), BLOCK)
    allowed = key_id_ref[span, :] == query_id_ref[0]
    allowed = jnp.concatenate([allowed, allowed], axis=1)
    for pair in range(width // PAIR):
        column = pair * PAIR
        lanes = slice(column, column + PAIR)
        queries = _halves(rows_ref[here, lanes] * SCALE)
        grads = _halves(grad_ref[here, lanes])
        keys = _window(rows_ref, block, blocks, width + column)
        values = _window(rows_ref, block, blocks, 2 * width + column)
        scores = jnp.where(allowed, _dot(keys, queries, NT), NEG)
        probs = jnp.exp(scores - log_ref[0, pair : pair + 1, :])
        grad_probs = _dot(values, grads, NT)
        inner = jnp.sum(probs * grad_probs, axis=0, keepdims=True)
        grad_scores = (probs * (grad_probs - inner)).astype(LOW)
        out_ref[here, lanes] = (_merge(_dot(keys, grad_scores, TN)) * SCALE).astype(LOW)
        key_sum[span, lanes] += _dot(grad_scores, queries, NN)
        value_sum[span, lanes] += _dot(probs.astype(LOW), grads, NN)

    @pl.when(block == blocks - 1)
    def _():
        def write(place, carry):
            into = pl.ds(pl.multiple_of(place * BLOCK, BLOCK), BLOCK)
            source = pl.ds(pl.multiple_of((place + 1) * BLOCK, BLOCK), BLOCK)
            out_ref[into, width : 2 * width] = key_sum[source, :].astype(LOW)
            out_ref[into, 2 * width :] = value_sum[source, :].astype(LOW)
            return carry

        lax.fori_loop(0, blocks, write, 0)


def _params():
    return pltpu.CompilerParams(dimension_semantics=("arbitrary",), vmem_limit_bytes=56 << 20)


def attend(qkv_rows, query_id, key_id):
    rows, triple = qkv_rows.shape
    width, blocks = triple // 3, rows // BLOCK
    heads = width // HEAD_DIM
    return pl.pallas_call(
        lambda *refs: attend_kernel(width, blocks, *refs),
        grid=(blocks,),
        in_specs=[
            pl.BlockSpec((rows, triple), lambda i: (0, 0)),
            pl.BlockSpec((1, 1, BLOCK), lambda i: (i, 0, 0)),
            pl.BlockSpec((rows + 2 * BLOCK, 1), lambda i: (0, 0)),
        ],
        out_specs=[
            pl.BlockSpec((BLOCK, width), lambda i: (i, 0)),
            pl.BlockSpec((1, heads // 2, 2 * BLOCK), lambda i: (i, 0, 0)),
        ],
        out_shape=[
            jax.ShapeDtypeStruct((rows, width), LOW),
            jax.ShapeDtypeStruct((blocks, heads // 2, 2 * BLOCK), F32),
        ],
        compiler_params=_params(),
        cost_estimate=NO_COST,
    )(qkv_rows, query_id, key_id)


def attend_back(qkv_rows, grad_rows, log_total, query_id, key_id):
    rows, triple = qkv_rows.shape
    width, blocks = triple // 3, rows // BLOCK
    heads = width // HEAD_DIM
    return pl.pallas_call(
        lambda *refs: attend_back_kernel(width, blocks, *refs),
        grid=(blocks,),
        in_specs=[
            pl.BlockSpec((rows, triple), lambda i: (0, 0)),
            pl.BlockSpec((rows, width), lambda i: (0, 0)),
            pl.BlockSpec((1, heads // 2, 2 * BLOCK), lambda i: (i, 0, 0)),
            pl.BlockSpec((1, 1, BLOCK), lambda i: (i, 0, 0)),
            pl.BlockSpec((rows + 2 * BLOCK, 1), lambda i: (0, 0)),
        ],
        out_specs=pl.BlockSpec((rows, triple), lambda i: (0, 0)),
        out_shape=jax.ShapeDtypeStruct((rows, triple), LOW),
        scratch_shapes=[
            pltpu.VMEM((rows + 2 * BLOCK, width), F32),
            pltpu.VMEM((rows + 2 * BLOCK, width), F32),
        ],
        compiler_params=_params(),
        cost_estimate=NO_COST,
    )(qkv_rows, grad_rows, log_total, query_id, key_id)


def layer_norm(values, gain_row, bias_row):
    centre = values - jnp.mean(values, axis=-1, keepdims=True)
    spread = jnp.mean(centre * centre, axis=-1, keepdims=True)
    return centre * lax.rsqrt(spread + 1e-06) * gain_row + bias_row


def norm_back_kernel(
    groups, keep_sum, values_ref, cot_ref, more_ref, gain_ref, low_ref, sum_ref, out_ref=None
):
    @pl.when(pl.program_id(0) == 0)
    def _():
        sum_ref[...] = jnp.zeros_like(sum_ref)

    values = values_ref[...]
    if groups:
        group = lax.broadcasted_iota(jnp.int32, (values.shape[0], groups), 1)
        chosen = jnp.where(more_ref[...] == group, 1.0, 0.0)
        cot = jnp.dot(chosen, cot_ref[...], precision=HIGHEST_PREC, preferred_element_type=F32)
    else:
        cot = cot_ref[...]
    centre = values - jnp.mean(values, axis=-1, keepdims=True)
    scale = lax.rsqrt(jnp.mean(centre * centre, axis=-1, keepdims=True) + 1e-06)
    normed = centre * scale
    scaled = cot * gain_ref[...]
    grad = scale * (
        scaled
        - jnp.mean(scaled, axis=-1, keepdims=True)
        - normed * jnp.mean(scaled * normed, axis=-1, keepdims=True)
    )
    if not groups:
        grad = grad + more_ref[...]
    low = grad.astype(LOW)
    if keep_sum:
        out_ref[...] = grad
    low_ref[...] = low
    for row, value in enumerate((cot * normed, cot, low.astype(F32))):
        sum_ref[row : row + 1, :] += jnp.sum(value, axis=0, keepdims=True)


def norm_back(values, gain_row, cotangent, more, keep_sum=True):
    rows, width = values.shape
    groups = cotangent.shape[0] if more.shape[1] == 1 else 0
    tile = rows // 8
    block = pl.BlockSpec((tile, width), lambda i: (i, 0))
    line = pl.BlockSpec((1, width), lambda i: (0, 0))
    out_specs = [block, pl.BlockSpec((8, width), lambda i: (0, 0))]
    out_shape = [jax.ShapeDtypeStruct((rows, width), LOW), jax.ShapeDtypeStruct((8, width), F32)]
    if keep_sum:
        out_specs.append(block)
        out_shape.append(jax.ShapeDtypeStruct((rows, width), F32))
    return pl.pallas_call(
        lambda *refs: norm_back_kernel(groups, keep_sum, *refs),
        grid=(8,),
        in_specs=[
            block,
            pl.BlockSpec((groups, width), lambda i: (0, 0)) if groups else block,
            pl.BlockSpec((tile, 1), lambda i: (i, 0)) if groups else block,
            line,
        ],
        out_specs=out_specs,
        out_shape=out_shape,
        compiler_params=_params(),
        cost_estimate=NO_COST,
    )(values, cotangent, more, gain_row[None])


def small_kernel(spots_ref, first_ref, second_ref, last_ref, qkv_ref, up_ref, out_ref):
    width, slots = out_ref.shape[1], spots_ref.shape[0]
    out_ref[...] = jnp.zeros_like(out_ref)
    rows = [(first_ref, 0), (first_ref, 1), (second_ref, 0), (second_ref, 1), (last_ref, 0), (last_ref, 1)]
    rows += [(first_ref, 2), (qkv_ref, 0), (qkv_ref, 2), (second_ref, 2), (last_ref, 2)]
    for row, (ref, which) in enumerate(rows):
        if ref is qkv_ref:
            out_ref[row : row + 1, :] = ref[:, which * width : (which + 1) * width]
        else:
            out_ref[row : row + 1, :] = ref[which : which + 1, :]
    for slot in range(slots):
        out_ref[pl.ds(16 + spots_ref[slot], 1), :] = up_ref[slot : slot + 1, :]


def small_sums(first, second, last, qkv_sum, up_sums):
    width, count = first.shape[1], lax.axis_size("pack")
    spots = relative_packs() ^ lax.axis_index("pack")
    up_sum = jnp.concatenate(up_sums).reshape(count, -1)
    arrays = [first, second, last, qkv_sum[None], jnp.pad(up_sum, ((0, 0), (0, width - up_sum.shape[1])))]
    return pl.pallas_call(
        small_kernel,
        in_specs=[pl.BlockSpec(memory_space=pltpu.SMEM)] + [pl.BlockSpec(memory_space=pltpu.VMEM)] * len(arrays),
        out_specs=pl.BlockSpec(memory_space=pltpu.VMEM),
        out_shape=jax.ShapeDtypeStruct((16 + count, width), F32),
        compiler_params=pltpu.CompilerParams(vmem_limit_bytes=16 << 20),
        cost_estimate=NO_COST,
    )(spots, *arrays)


def gelu(values):
    return 0.5 * values * (1.0 + lax.erf(values * math.sqrt(0.5)))


def gelu_slope(values):
    return 0.5 * (1.0 + lax.erf(values * math.sqrt(0.5))) + values * (
        math.sqrt(0.5 / math.pi) * jnp.exp(-0.5 * values * values)
    )


def as_rows(value, width):
    flat = value.reshape(1, -1)
    return jnp.pad(flat, ((0, 7), (0, width - flat.shape[1])))


def from_rows(cells, shape):
    rows, columns = shape
    flat = cells[:, 0, : rows * columns].reshape(-1, rows, columns)
    return flat.transpose(1, 0, 2).reshape(rows, -1)


def mm(spec, left, right):
    return jnp.einsum(spec, left, right, preferred_element_type=F32)


def column_sum(rows):
    return jnp.sum(rows.astype(F32), axis=0)


def hmul(left, right):
    return jnp.dot(left, right, precision=NS_PREC, preferred_element_type=F32)


def ortho(columns):
    gram_part = lax.dot_general(columns, columns, (TN, ((), ())), precision=NS_PREC, preferred_element_type=F32)
    gram_mat, scale = unfold(column_all_sum(fold(gram_part)), columns.shape[1])
    iterate = columns * scale
    eye = jnp.eye(gram_mat.shape[0], dtype=F32)
    for step in range(NS_STEPS):
        if step < NS_STEPS - 1:
            square = hmul(gram_mat, gram_mat)
            poly = COEF_ONE * eye + COEF_TWO * gram_mat + COEF_THREE * square
            poly_gram = COEF_ONE * gram_mat + COEF_TWO * square + COEF_THREE * hmul(square, gram_mat)
            iterate = hmul(iterate, poly)
            gram_mat = hmul(poly, poly_gram)
        else:
            first_pass = hmul(iterate, gram_mat)
            iterate = COEF_ONE * iterate + COEF_TWO * first_pass + COEF_THREE * hmul(first_pass, gram_mat)
    return iterate


def to_columns(shards):
    chip = lax.axis_index("pack") >> 1
    most = max(m.shape[0] for m in shards)
    filled = [jnp.pad(m, ((0, most - m.shape[0]), (0, 0))) for m in shards]
    filled += [jnp.zeros_like(filled[0])] * (lax.axis_size("pack") // 2 - len(shards))
    stacked = jnp.stack(filled)
    parts = [pick(stacked, chip)]
    parts += [swap(pick(stacked, chip ^ (k // 2)), "pack", k) for k in other_chips()]
    return jnp.stack(parts)


def from_columns(value, counts):
    back = [value[0]] + [swap(value[k // 2], "pack", k) for k in other_chips()]
    return [_choose(back, lax.axis_index("pack") >> 1, m)[:count] for m, count in enumerate(counts)]


def muon_update(weight, iterate):
    col_ratio = math.sqrt(
        max(1.0, iterate.shape[1] * lax.axis_size(("pack", "seq")) / weight.shape[0])
    )
    return weight * (1.0 - MUON_RATE * DECAY) - MUON_RATE * col_ratio * iterate


def adam_update(weight, first_moment, second_moment, gradient, factor, count_float):
    scaled = factor * gradient
    new_first = BETA_ONE * first_moment + (1.0 - BETA_ONE) * scaled
    new_second = BETA_TWO * second_moment + (1.0 - BETA_TWO) * scaled * scaled
    first_hat = new_first / (1.0 - jnp.power(BETA_ONE, count_float))
    second_hat = new_second / (1.0 - jnp.power(BETA_TWO, count_float))
    new_weight = weight - ADAM_RATE * (first_hat / (jnp.sqrt(second_hat) + 1e-08) + DECAY * weight)
    return (new_weight, new_first, new_second)


def deal_rows(lengths, keep_mask, shard_len):
    packs, images = lengths.shape
    seq_count, seq_place = lax.axis_size("seq"), lax.axis_index("seq")
    image_range = jnp.arange(images, dtype=jnp.int32)
    upto = image_range[None, :] <= image_range[:, None]
    ends = jnp.sum(jnp.where(upto[None], lengths[:, None, :], 0), axis=2, dtype=jnp.int32)
    starts = ends - lengths
    cuts = jnp.arange(1, seq_count, dtype=jnp.int32) * shard_len
    straddles = (starts[:, None, :] < cuts[None, :, None]) & (ends[:, None, :] > cuts[None, :, None])
    behind = jnp.sum(jnp.where(straddles, cuts[None, :, None] - starts[:, None, :], 0), axis=2, dtype=jnp.int32)
    ahead = jnp.sum(jnp.where(straddles, ends[:, None, :] - cuts[None, :, None], 0), axis=2, dtype=jnp.int32)
    excess = jnp.zeros_like(cuts)
    moves = []
    for pack in range(packs):
        more, less = excess + ahead[pack], excess - behind[pack]
        forward = jnp.abs(more) <= jnp.abs(less)
        excess = jnp.where(forward, more, less)
        moves.append(jnp.where(forward, ahead[pack], -behind[pack]))
    borders = jnp.concatenate(
        [
            jnp.zeros((packs, 1), jnp.int32),
            cuts[None, :] + jnp.stack(moves),
            jnp.full((packs, 1), PACK_LEN, jnp.int32),
        ],
        axis=1,
    )
    first = lax.dynamic_index_in_dim(borders, seq_place, 1, keepdims=False)
    held = lax.dynamic_index_in_dim(borders, seq_place + 1, 1, keepdims=False) - first
    pack_range = jnp.arange(packs, dtype=jnp.int32)
    before = jnp.sum(jnp.where(pack_range[None, :] < pack_range[:, None], held[None, :], 0), axis=1, dtype=jnp.int32)
    row = jnp.arange(packs * shard_len + MAXLEN, dtype=jnp.int32)
    in_pack = (row[:, None] >= before[None, :]) & (row[:, None] < (before + held)[None, :])
    valid = jnp.any(in_pack, axis=1)

    def of_pack(values):
        return jnp.sum(jnp.where(in_pack, values, 0), axis=1, dtype=jnp.int32)

    pack_of = of_pack(pack_range[None, :])
    place = of_pack(row[:, None] - before[None, :] + first[None, :])
    window = shard_len + 2 * MAXLEN
    source = jnp.where(valid, pack_of * window + place - (seq_place * shard_len - MAXLEN), -1)
    row_ends = jnp.sum(jnp.where(in_pack[:, :, None], ends[None], 0), axis=1, dtype=jnp.int32)
    row_starts = jnp.sum(jnp.where(in_pack[:, :, None], starts[None], 0), axis=1, dtype=jnp.int32)
    image_of = jnp.sum((place[:, None] >= row_ends).astype(jnp.int32), axis=1, dtype=jnp.int32)
    is_first = jnp.any(place[:, None] == row_starts, axis=1)
    keep_rows = mm("rp,pj->rj", in_pack.astype(LOW), (keep_mask > 0).astype(LOW))
    spot = jnp.arange(PACK_LEN, dtype=jnp.int32)
    kept = jnp.any((place[:, None] == spot[None, :]) & (keep_rows > 0.5), axis=1)
    live = valid & (kept | is_first)
    group = jnp.where(valid, pack_of * images + image_of, -1)

    spots = jnp.arange(PACK_LEN, dtype=jnp.int32)[None, None, :]
    inside = (spots >= starts[:, :, None]) & (spots < ends[:, :, None])
    counted = inside & ((keep_mask > 0)[:, None, :] | (spots == starts[:, :, None]))
    counts = jnp.sum(counted.astype(F32), axis=2)
    return source, group, live, counts.reshape(-1)


def body(
    patches,
    lengths,
    keep_mask,
    labels,
    step_count,
    embed_weight,
    embed_first,
    embed_second,
    qkv_weight,
    qkv_moment,
    output_weight,
    output_moment,
    up_weight,
    up_moment,
    down_weight,
    down_moment,
    small_params,
    small_first,
    small_second,
    head_weight,
    head_first,
    head_second,
    head_bias,
    bias_first,
    bias_second,
):
    packs, shard_len, patch_in = patches.shape
    images = lengths.shape[1]
    width = qkv_weight.shape[0]
    seq_count, seq_place = lax.axis_size("seq"), lax.axis_index("seq")
    pack_count, pack_place = lax.axis_size("pack"), lax.axis_index("pack")
    small_rows = small_params.shape[0]

    bundle = [
        embed_weight.T,
        qkv_weight.T,
        output_weight.T,
        as_rows(small_params, width),
        as_rows(head_bias, width),
    ]
    spots = [0]
    for piece in bundle:
        spots.append(spots[-1] + piece.shape[0])
    first = Gather(jnp.concatenate([piece.astype(LOW) for piece in bundle]))
    up_gather, down_gather = Gather(up_weight.T.astype(LOW)), Gather(down_weight.T.astype(LOW))
    first.along_seq()
    first.block, patches = hold(first.block, patches)
    first.in_plane()
    ends = seq_count - 1
    from_left = lax.ppermute(patches[:, shard_len - MAXLEN :], "seq", [(i, i + 1) for i in range(ends)])
    from_right = lax.ppermute(patches[:, :MAXLEN], "seq", [(i + 1, i) for i in range(ends)])
    window = jnp.concatenate([from_left, patches, from_right], axis=1).reshape(-1, patch_in)
    source, group, live, counts = deal_rows(lengths, keep_mask, shard_len)
    chosen = (source[:, None] == jnp.arange(window.shape[0], dtype=jnp.int32)[None, :]).astype(LOW)
    tokens = mm("rw,wi->ri", chosen, window).astype(LOW)
    tokens, up_gather.shard, *first.parts = hold(tokens, up_gather.shard, *first.parts)
    up_gather.send_seq()
    embed_full, qkv_full, output_full, small_full, bias_full = first.pieces(spots)
    embed_full, qkv_full, output_full = (
        value.reshape(-1, width) for value in (embed_full, qkv_full, output_full)
    )
    (gain_bias,) = hold(from_rows(small_full, small_params.shape).astype(F32))
    bias_full = lax.dynamic_slice_in_dim(bias_full, pack_place * seq_count, seq_count, 0)
    bias_full = bias_full[:, 0, : head_bias.shape[0]].reshape(-1)

    rows = tokens.shape[0]
    query_id = group.reshape(rows // BLOCK, 1, BLOCK)
    key_id = jnp.pad(jnp.where(live, group, -2), (BLOCK, BLOCK), constant_values=-2)[:, None]
    group_count = packs * images
    member = (
        (group[None, :] == jnp.arange(group_count, dtype=jnp.int32)[:, None]) & live[None, :]
    ).astype(F32)

    embedded = mm("ri,di->rd", tokens, embed_full) + gain_bias[6]
    embedded, up_gather.parts[0], down_gather.shard = hold(embedded, up_gather.parts[0], down_gather.shard)
    up_gather.join_seq()
    up_gather.in_plane()
    down_gather.doubling()
    normed_one = layer_norm(embedded, gain_bias[0], gain_bias[1]).astype(LOW)
    qkv_bias = jnp.concatenate([gain_bias[7], jnp.zeros_like(gain_bias[7]), gain_bias[8]])
    qkv_rows = (mm("rd,ed->re", normed_one, qkv_full) + qkv_bias).astype(LOW)
    qkv_rows, down_gather.block, head_low, *up_gather.parts = hold(
        qkv_rows, down_gather.block, head_weight.astype(LOW), *up_gather.parts
    )
    head_full = lax.all_gather(head_low, "seq", axis=0, tiled=True)
    down_gather.in_plane()
    up_full = [half.reshape(-1, width) for half in up_gather.halves()]
    attn_low, log_total = attend(qkv_rows, query_id, key_id)
    attn_low, *down_gather.parts = hold(attn_low, *down_gather.parts)
    down_full = [half.reshape(-1, width) for half in down_gather.halves()]
    after_attn = embedded + mm("re,de->rd", attn_low, output_full) + gain_bias[9]
    normed_two = layer_norm(after_attn, gain_bias[2], gain_bias[3]).astype(LOW)
    up_bias = jnp.take(
        gain_bias[11:15].reshape(pack_count, -1), relative_packs() ^ pack_place, axis=0
    ).reshape(2, -1)
    up_rows = [mm("rd,fd->rf", normed_two, up_full[half]) + up_bias[half] for half in range(2)]
    active = [gelu(rows).astype(LOW) for rows in up_rows]
    after_mlp = (
        after_attn
        + (mm("rf,fd->rd", active[0], down_full[0]) + mm("rf,fd->rd", active[1], down_full[1]))
        + gain_bias[10]
    )
    final_rows = layer_norm(after_mlp, gain_bias[4], gain_bias[5])
    pool_sums = jnp.dot(member, final_rows, precision=HIGHEST_PREC, preferred_element_type=F32)
    pooled_mine = (pool_sums / counts[:, None]).astype(LOW)

    img_share = group_count // seq_count
    split = pooled_mine.reshape(seq_count, img_share, width)
    pooled_low = tree_sum(
        [pick(split, seq_place).astype(F32)]
        + [swap(pick(split, seq_place ^ k), "seq", k).astype(F32) for k in range(1, seq_count)]
    ).astype(LOW)
    pooled_rows = jnp.concatenate(gather_blocks(pooled_low), axis=0).reshape(-1, width)
    depth = head_weight.shape[0]
    label_cols = head_full.shape[1]
    logits = mm("nd,dc->nc", pooled_rows, head_full) + bias_full.astype(F32)
    label_rows = jnp.take(
        pick(labels.reshape(pack_count, seq_count, img_share), seq_place, 1),
        relative_packs() ^ pack_place,
        axis=0,
    ).reshape(-1)
    class_ids = pack_place * label_cols + jnp.arange(label_cols, dtype=jnp.int32)
    valid = (class_ids < LABELS).astype(F32)
    target = (label_rows[:, None] == class_ids[None, :]).astype(F32)
    image_total = labels.shape[0] * labels.shape[1]
    loss_part = jnp.sum(valid[None, :] * (jax.nn.softplus(logits) - target * logits)) / image_total
    grad_logits = (valid[None, :] * (jax.nn.sigmoid(logits) - target) / image_total).astype(LOW)
    pooled_part = mm("nc,dc->nd", grad_logits, head_full).reshape(pack_count, img_share, width)
    pooled_grad = pack_scatter(pooled_part)
    pooled_grad = jnp.concatenate(absolute(relative(pooled_grad, "seq"), seq_place), axis=0)
    pooled_grad = pooled_grad / counts[:, None]

    traded, pooled_grad = hold(jnp.concatenate([pooled_rows, grad_logits], axis=1), pooled_grad)
    traded = lax.all_gather(traded, "seq", axis=0, tiled=True)

    grad_mlp_low, sums_last, grad_mlp = norm_back(
        after_mlp, gain_bias[4], pooled_grad, jnp.where(live, group, -1)[:, None]
    )
    down_sum, up_sum = Scatter(0, width, True), Scatter(1, width, True)
    half = width // 2
    late_sums = [Scatter(0, half), Scatter(1, half)]
    pair_sums = [Scatter(0, half), Scatter(1, half)]
    down_out = mm("rf,rd->fd", active[1], grad_mlp_low)
    down_keep = mm("rf,rd->fd", active[0], grad_mlp_low)
    grad_mlp_low, down_out, down_keep = hold(grad_mlp_low, down_out, down_keep)
    down_out = down_sum.start_halves(down_keep, down_out)
    grad_upper = [
        (mm("rd,fd->rf", grad_mlp_low, down_full[side]) * gelu_slope(up_rows[side])).astype(LOW)
        for side in range(2)
    ]
    up_out = mm("rf,rd->fd", grad_upper[1], normed_two)
    up_keep = mm("rf,rd->fd", grad_upper[0], normed_two)
    grad_upper[0], grad_upper[1], up_out, up_keep = hold(*grad_upper, up_out, up_keep)
    up_out = up_sum.start_halves(up_keep, up_out)
    grad_normed = mm("rf,fd->rd", grad_upper[0], up_full[0]) + mm("rf,fd->rd", grad_upper[1], up_full[1])
    down_out = down_sum.step(down_out)
    grad_normed, down_out = hold(grad_normed, down_out)
    grad_attn_low, sums_second, grad_attn = norm_back(
        after_attn, gain_bias[2], grad_normed, grad_mlp
    )
    grad_mixed = mm("rd,de->re", grad_attn_low, output_full).astype(LOW)
    up_out = up_sum.step(up_out)
    grad_mixed, up_out = hold(grad_mixed, up_out)
    grad_qkv = attend_back(qkv_rows, grad_mixed, log_total, query_id, key_id)
    down_out, up_out = down_sum.step(down_out), up_sum.step(up_out)
    grad_qkv, down_out, up_out = hold(grad_qkv, down_out, up_out)
    grad_normed = mm("re,ed->rd", grad_qkv, qkv_full)
    grad_embed_rows, sums_first = norm_back(embedded, gain_bias[0], grad_normed, grad_attn, keep_sum=False)
    output_grad = mm("rd,re->de", grad_attn_low, attn_low)
    embed_grad = mm("rd,ri->di", grad_embed_rows, tokens)
    down_sum.finish(down_out)
    up_sum.finish(up_out)
    early = jnp.concatenate([down_sum.value, up_sum.value], axis=1)
    pair_keep, pair_out = late_halves(output_grad, embed_grad)
    grad_qkv, pair_out, early = hold(grad_qkv, pair_out, early)
    early = lax.psum_scatter(early, "seq", scatter_dimension=0)
    late_keep, late_out = late_halves(mm("re,rd->ed", grad_qkv, normed_one))
    pair = pair_keep + swap(pair_out, "pack", 1)
    pair_outs = [
        each.start_joined(part) for each, part in zip(pair_sums, (pair[..., :half], pair[..., half:]))
    ]
    late_out, grad_qkv, traded, *pair_outs = hold(late_out, grad_qkv, traded, *pair_outs)
    all_logits = traded[:, width:]
    bias_grad = pick(column_sum(all_logits).reshape(seq_count, -1), seq_place)
    late = late_keep + swap(late_out, "pack", 1)
    late_outs = [
        each.start_joined(part) for each, part in zip(late_sums, (late[..., :half], late[..., half:]))
    ]
    bias_grad, grad_qkv, traded, grad_upper[0], grad_upper[1], *held = hold(
        bias_grad, grad_qkv, traded, *grad_upper, *late_outs, *[each.keep for each in pair_sums]
    )
    late_outs = held[:2]
    pair_sums[0].keep, pair_sums[1].keep = held[2:]
    all_pooled = pick(traded[:, :width].reshape(-1, seq_count, head_weight.shape[0]), seq_place, 1)
    head_grad = mm("nd,nc->dc", all_pooled, traded[:, width:])
    small_mine = small_sums(
        sums_first, sums_second, sums_last, column_sum(grad_qkv), [column_sum(side) for side in grad_upper]
    )
    for each, sent in zip(pair_sums, pair_outs):
        each.finish(sent)
    pair = jnp.concatenate([each.value for each in pair_sums], axis=2)
    late_outs = [each.step(sent) for each, sent in zip(late_sums, late_outs)]
    small_mine, head_grad, pair, *late_outs = hold(small_mine, head_grad, pair, *late_outs)
    small_total = small_mine + swap(small_mine, "pack", 1)
    for each, sent in zip(late_sums, late_outs):
        each.finish(sent)
    late_sum = SeqScatter(
        jnp.concatenate([jnp.concatenate([each.value for each in late_sums], axis=2), pair], axis=1)
    )
    late_out, small_total, early = hold(late_sum.send(), small_total, early)
    small_total = sum_chips(small_total)
    late_out = late_sum.step(late_out)
    late_out, small_total = hold(late_out, small_total)
    small_total = all_sum(small_total, "seq")
    while late_out is not None:
        late_out = late_sum.step(late_out)
    late_sum.value, small_total = hold(late_sum.value, small_total)
    down_share, up_share = jnp.split(early, 2)
    late_share = late_sum.result()
    widths = [qkv_weight.shape[1], output_weight.shape[1], embed_weight.shape[1]]
    qkv_share, output_share = late_share[: widths[0]], late_share[widths[0] : widths[0] + widths[1]]
    embed_share = late_share[widths[0] + widths[1] :].T
    hidden = down_weight.shape[1] * seq_count
    small_total = jnp.concatenate(
        [small_total[:11], small_total[16:, :hidden].reshape(small_rows - 11, width)], axis=0
    )
    place = pack_place * seq_count + seq_place
    small_share = pick(small_total.reshape(small_rows, pack_count * seq_count, -1), place, 1)

    shares = (early, late_share, head_grad, bias_grad)
    square_sum = sum((jnp.sum(piece * piece) for piece in shares))
    sums = jnp.broadcast_to(jnp.stack([loss_part, square_sum])[:, None], (2, BLOCK))
    sums = sum_plane(all_sum(sums, "seq"))
    loss_value, square_total = sums[0, 0], sums[1, 0] + jnp.sum(small_total * small_total)
    grad_norm = jnp.sqrt(square_total)
    factor = jnp.minimum(1.0, CLIP_NORM / (grad_norm + 1e-06))
    muon_shares = (qkv_share, output_share, up_share, down_share)
    moments = [
        MUON_MU * moment.T + factor * share
        for moment, share in zip((qkv_moment, output_moment, up_moment, down_moment), muon_shares)
    ]
    columns = to_columns(moments)
    iterates = ortho(columns.reshape(-1, width)).reshape(columns.shape)
    iterates = [iterate.T for iterate in from_columns(iterates, [m.shape[0] for m in moments])]
    moments = [moment.T for moment in moments]
    new_qkv = muon_update(qkv_weight, iterates[0])
    new_output = muon_update(output_weight, iterates[1])
    new_up = muon_update(up_weight, iterates[2])
    new_down = muon_update(down_weight, iterates[3])
    count_float = step_count[0].astype(F32)
    new_embed, new_embed_first, new_embed_second = adam_update(
        embed_weight, embed_first, embed_second, embed_share, factor, count_float
    )
    new_small, new_small_first, new_small_second = adam_update(
        small_params, small_first, small_second, small_share, factor, count_float
    )
    new_head, new_head_first, new_head_second = adam_update(
        head_weight, head_first, head_second, head_grad, factor, count_float
    )
    new_bias, new_bias_first, new_bias_second = adam_update(
        head_bias, bias_first, bias_second, bias_grad, factor, count_float
    )
    return (
        loss_value,
        grad_norm,
        new_embed,
        new_embed_first,
        new_embed_second,
        new_qkv,
        moments[0],
        new_output,
        moments[1],
        new_up,
        moments[2],
        new_down,
        moments[3],
        new_small,
        new_small_first,
        new_small_second,
        new_head,
        new_head_first,
        new_head_second,
        new_bias,
        new_bias_first,
        new_bias_second,
    )


def solution(mesh):
    both = P(None, ("pack", "seq"))
    head = P("seq", "pack")
    line = P(("pack", "seq"))
    return jax.shard_map(
        body,
        mesh=mesh,
        in_specs=(P("pack", "seq", None), P("pack", None), P("pack", None), P(), P())
        + (both,) * 14
        + (head,) * 3
        + (line,) * 3,
        out_specs=(P(), P()) + (both,) * 14 + (head,) * 3 + (line,) * 3,
        check_vma=False,
    )
```

```python
import math

import jax
import jax.numpy as jnp
from jax import lax
from jax.experimental import pallas as pl
from jax.experimental.pallas import tpu as pltpu
from jax.sharding import PartitionSpec as P

HEAD_DIM = 64
LABELS = 21843
PACK_LEN = 1024
MAXLEN = 128
NS_STEPS = 2
BLOCK = 128
PAIR = 2 * HEAD_DIM

HIGHEST_PREC = lax.Precision.HIGHEST
NS_PREC = lax.Precision.HIGH
CLIP_NORM = 1.0
MUON_MU = 0.95
MUON_RATE = 1.0
ADAM_RATE = 0.02
BETA_ONE = 0.9
BETA_TWO = 0.95
DECAY = 0.01
COEF_ONE = 3.4445
COEF_TWO = -4.775
COEF_THREE = 2.0315
SCALE = HEAD_DIM ** (-0.5)
LOW = jnp.bfloat16
F32 = jnp.float32
NEG = -1e30
NO_COST = pl.CostEstimate(flops=0, bytes_accessed=0, transcendentals=0)


def swap(value, axis, bit):
    return lax.ppermute(value, axis, [(i, i ^ bit) for i in range(lax.axis_size(axis))])


def pick(value, index, dim=0):
    return lax.dynamic_index_in_dim(value, index, dim, keepdims=False)


def tree_sum(parts):
    while len(parts) > 1:
        parts = [parts[i] + parts[i + 1] for i in range(0, len(parts), 2)]
    return parts[0]


def relative(value, axis):
    return [value] + [swap(value, axis, k) for k in range(1, lax.axis_size(axis))]


def absolute(parts, place):
    return [_choose(parts, place, j) for j in range(len(parts))]


def _choose(parts, place, j):
    out = parts[j]
    for other in range(1, len(parts)):
        out = jnp.where(place == other, parts[j ^ other], out)
    return out


def all_sum(value, axis):
    return tree_sum(relative(value, axis))


def hold(*values):
    return lax.optimization_barrier(values)


def other_chips():
    return list(range(2, lax.axis_size("pack"), 2))


def relative_packs():
    same = [0] + other_chips()
    return jnp.array(same + [k + 1 for k in same], jnp.int32)


def relative_slots():
    count = lax.axis_size("pack")
    offset = lax.axis_index("pack") ^ jnp.arange(count, dtype=jnp.int32)
    return (offset >> 1) + (offset & 1) * (count // 2)


def gather_blocks(block):
    own = jnp.stack([block] + [swap(block, "pack", k) for k in other_chips()])
    return own, swap(own, "pack", 1)


def by_index(parts, place):
    if len(parts) <= 8:
        return jnp.stack(absolute(parts, place))
    value = jnp.stack(parts)
    shape, bit = value.shape, 1
    while bit < len(parts):
        value = value.reshape((-1, 2, bit) + shape[1:])
        turned = jnp.concatenate([value[:, 1:], value[:, :1]], axis=1)
        value = jnp.where((place & bit) == 0, value, turned)
        bit *= 2
    return value.reshape(shape)


def by_core(own, other, dim):
    return jnp.where(
        (lax.axis_index("pack") & 1) == 0, jnp.stack([own, other], axis=dim), jnp.stack([other, own], axis=dim)
    )


class Gather:
    def __init__(self, shard):
        self.shard = shard

    def along_seq(self):
        self.block = by_index(relative(self.shard, "seq"), lax.axis_index("seq"))

    def send_seq(self):
        self.parts = relative(self.shard, "seq")

    def join_seq(self):
        self.block = by_index(self.parts, lax.axis_index("seq"))

    def doubling(self):
        place, count, bit = lax.axis_index("seq"), lax.axis_size("seq"), 1
        block = self.shard[None]
        while bit < count:
            other = swap(block, "seq", bit)
            block = jnp.where(
                (place & bit) == 0,
                jnp.concatenate([block, other], axis=0),
                jnp.concatenate([other, block], axis=0),
            )
            bit *= 2
        self.block = block
        return block

    def in_plane(self):
        self.parts = [self.block] + [swap(self.block, "pack", k) for k in other_chips()]

    def pieces(self, spots):
        mine = by_index(self.parts, lax.axis_index("pack") >> 1)
        other = swap(mine, "pack", 1)
        return [
            by_core(mine[:, :, here:there], other[:, :, here:there], 1).reshape(-1, there - here, mine.shape[-1])
            for here, there in zip(spots[:-1], spots[1:])
        ]

    def halves(self):
        own = jnp.stack(self.parts)
        return own, swap(own, "pack", 1)


class Scatter:
    def __init__(self, order, width, relative=False):
        self.left = [1 << b for b in reversed(range(lax.axis_size("pack").bit_length() - 1))]
        chips = [b for b in self.left if b > 1]
        self.order = [1] + (chips if order == 0 else chips[::-1])
        self.relative, self.width = relative, width

    def start_halves(self, keep, send):
        self.left.remove(1)
        self.bit = self.order.pop(0)
        shape = (2,) * len(self.left) + (lax.axis_size("seq"), -1, self.width)
        self.keep = keep.reshape(shape)
        return send.reshape(shape)

    def start_joined(self, value):
        self.left.remove(1)
        self.order.pop(0)
        self.value = value
        return self.send()

    def send(self):
        self.bit = bit = self.order.pop(0)
        dim = self.left.index(bit)
        self.left.remove(bit)
        if self.relative:
            self.keep = lax.index_in_dim(self.value, 0, dim, keepdims=False)
            return lax.index_in_dim(self.value, 1, dim, keepdims=False)
        mine = (lax.axis_index("pack") & bit) // bit
        self.keep = pick(self.value, mine, dim)
        return pick(self.value, 1 - mine, dim)

    def step(self, sent):
        self.value = self.keep + swap(sent, "pack", self.bit)
        return self.send() if self.order else None

    def finish(self, sent):
        while sent is not None:
            sent = self.step(sent)


class SeqScatter:
    def __init__(self, value):
        self.value, self.bit = value, 1

    def send(self):
        tail = self.value.shape[-2:]
        split = self.value.reshape((-1, 2) + tail)
        mine = (lax.axis_index("seq") & self.bit) // self.bit
        self.keep = pick(split, mine, 1)
        return pick(split, 1 - mine, 1)

    def step(self, sent):
        self.value = self.keep + swap(sent, "seq", self.bit)
        self.bit *= 2
        return self.send() if self.bit < lax.axis_size("seq") else None

    def result(self):
        return self.value.reshape(self.value.shape[-2:])


def late_halves(*grads):
    seq_count, pack_count = lax.axis_size("seq"), lax.axis_size("pack")
    chips = (2,) * (pack_count.bit_length() - 2)
    core = lax.axis_index("pack") & 1

    def half(which):
        pieces = [
            pick(grad.reshape(chips + (2, seq_count, -1, grad.shape[1])), which, len(chips)) for grad in grads
        ]
        return jnp.concatenate(pieces, axis=-2)

    return half(core), half(1 - core)


def pack_scatter(value):
    half = value.shape[0] // 2
    mine = value[:half] + swap(value[half:], "pack", 1)
    parts = [mine[0]] + [swap(mine[k // 2], "pack", k) for k in other_chips()]
    return tree_sum(parts)


def column_all_sum(value, beside):
    seq_place, count = lax.axis_index("seq"), lax.axis_size("seq")
    core = lax.axis_index("pack") & 1
    split = value.reshape(2, count, -1, value.shape[1])
    mine = pick(split, core) + swap(pick(split, 1 - core), "pack", 1)
    parts = [pick(mine, seq_place)] + [swap(pick(mine, seq_place ^ k), "seq", k) for k in range(1, count)]
    total, *beside = hold(tree_sum(parts), *beside)
    mine = by_index(relative(total, "seq"), seq_place)
    return by_core(mine, swap(mine, "pack", 1), 0).reshape(value.shape), beside


def fold(matrix):
    count, width = matrix.shape[0] // BLOCK, matrix.shape[0]

    def row(i):
        return matrix[i * BLOCK : (i + 1) * BLOCK, i * BLOCK :]

    return jnp.concatenate(
        [jnp.concatenate([row(i), row(count - 1 - i)], axis=1) for i in range(count // 2)], axis=0
    )


def unfold_kernel(folded_ref, out_ref, scale_ref):
    width = out_ref.shape[0]
    count = width // BLOCK

    def block(i, j):
        line = min(i, count - 1 - i)
        column = (j - i) * BLOCK + (0 if line == i else width - line * BLOCK)
        return folded_ref[line * BLOCK : (line + 1) * BLOCK, column : column + BLOCK]

    row = lax.broadcasted_iota(jnp.int32, (BLOCK, BLOCK), 0)
    column = lax.broadcasted_iota(jnp.int32, (BLOCK, BLOCK), 1)
    diagonal = jnp.zeros((BLOCK, BLOCK), F32)
    for i in range(count):
        diagonal += jnp.where(row == column, block(i, i), 0.0)
    trace = jnp.sum(jnp.sum(diagonal, axis=0, keepdims=True), axis=1, keepdims=True)
    scale = 1.0 / (jnp.sqrt(trace) + 1e-07)
    for i in range(count):
        for j in range(i, count):
            value = block(i, j) * scale * scale
            out_ref[i * BLOCK : (i + 1) * BLOCK, j * BLOCK : (j + 1) * BLOCK] = value
            if j > i:
                out_ref[j * BLOCK : (j + 1) * BLOCK, i * BLOCK : (i + 1) * BLOCK] = value.T
    scale_ref[...] = jnp.broadcast_to(scale, scale_ref.shape)


def unfold(folded, width):
    whole = pl.BlockSpec(memory_space=pltpu.VMEM)
    matrix, scale = pl.pallas_call(
        unfold_kernel,
        in_specs=[whole],
        out_specs=[whole, whole],
        out_shape=[jax.ShapeDtypeStruct((width, width), F32), jax.ShapeDtypeStruct((8, BLOCK), F32)],
        compiler_params=pltpu.CompilerParams(vmem_limit_bytes=32 << 20),
        cost_estimate=NO_COST,
    )(folded)
    return matrix, scale[0, 0]


def sum_plane(value):
    return sum_chips(value + swap(value, "pack", 1))


def sum_chips(value):
    return tree_sum([value] + [swap(value, "pack", k) for k in other_chips()])


def _dot(left, right, dims):
    return lax.dot_general(left, right, (dims, ((), ())), preferred_element_type=F32)


NT = ((1,), (1,))
TN = ((0,), (0,))
NN = ((1,), (0,))


def _window(ref, block, blocks, column):
    places = (jnp.maximum(block - 1, 0), block, jnp.minimum(block + 1, blocks - 1))
    return jnp.concatenate(
        [ref[pl.ds(pl.multiple_of(place * BLOCK, BLOCK), BLOCK), column : column + PAIR] for place in places],
        axis=0,
    )


def _halves(value):
    lane = lax.broadcasted_iota(jnp.int32, value.shape, 1)
    zero = jnp.zeros_like(value)
    return jnp.concatenate(
        [jnp.where(lane < HEAD_DIM, value, zero), jnp.where(lane < HEAD_DIM, zero, value)], axis=0
    )


def _merge(value):
    return jnp.concatenate([value[:HEAD_DIM, :BLOCK], value[HEAD_DIM:, BLOCK:]], axis=0).T


def attend_kernel(width, blocks, rows_ref, query_id_ref, key_id_ref, out_ref, log_ref):
    block = pl.program_id(0)
    here = pl.ds(pl.multiple_of(block * BLOCK, BLOCK), BLOCK)
    allowed = key_id_ref[pl.ds(pl.multiple_of(block * BLOCK, BLOCK), 3 * BLOCK), :] == query_id_ref[0]
    for pair in range(width // PAIR):
        column = pair * PAIR
        queries = _halves(rows_ref[here, column : column + PAIR] * SCALE)
        keys = _window(rows_ref, block, blocks, width + column)
        values = _window(rows_ref, block, blocks, 2 * width + column)
        mixed = []
        for lanes in (slice(0, BLOCK), slice(BLOCK, 2 * BLOCK)):
            scores = jnp.where(allowed, _dot(keys, queries[lanes], NT), NEG)
            top = jnp.max(scores, axis=0, keepdims=True)
            raised = jnp.exp(scores - top)
            total = jnp.sum(raised, axis=0, keepdims=True)
            probs = (raised * (1.0 / total)).astype(LOW)
            log_ref[0, pair : pair + 1, lanes] = top + jnp.log(total)
            mixed.append(_dot(values, probs, TN))
        out_ref[:, column : column + PAIR] = _merge(jnp.concatenate(mixed, axis=1)).astype(LOW)


def attend_back_kernel(
    width, blocks, rows_ref, grad_ref, log_ref, query_id_ref, key_id_ref, out_ref, key_sum, value_sum
):
    block = pl.program_id(0)

    @pl.when(block == 0)
    def _():
        key_sum[...] = jnp.zeros_like(key_sum)
        value_sum[...] = jnp.zeros_like(value_sum)

    span = pl.ds(pl.multiple_of(block * BLOCK, BLOCK), 3 * BLOCK)
    here = pl.ds(pl.multiple_of(block * BLOCK, BLOCK), BLOCK)
    allowed = key_id_ref[span, :] == query_id_ref[0]
    allowed = jnp.concatenate([allowed, allowed], axis=1)
    for pair in range(width // PAIR):
        column = pair * PAIR
        lanes = slice(column, column + PAIR)
        queries = _halves(rows_ref[here, lanes] * SCALE)
        grads = _halves(grad_ref[here, lanes])
        keys = _window(rows_ref, block, blocks, width + column)
        values = _window(rows_ref, block, blocks, 2 * width + column)
        scores = jnp.where(allowed, _dot(keys, queries, NT), NEG)
        probs = jnp.exp(scores - log_ref[0, pair : pair + 1, :])
        grad_probs = _dot(values, grads, NT)
        inner = jnp.sum(probs * grad_probs, axis=0, keepdims=True)
        grad_scores = (probs * (grad_probs - inner)).astype(LOW)
        out_ref[here, lanes] = (_merge(_dot(keys, grad_scores, TN)) * SCALE).astype(LOW)
        key_sum[span, lanes] += _dot(grad_scores, queries, NN)
        value_sum[span, lanes] += _dot(probs.astype(LOW), grads, NN)

    @pl.when(block == blocks - 1)
    def _():
        def write(place, carry):
            into = pl.ds(pl.multiple_of(place * BLOCK, BLOCK), BLOCK)
            source = pl.ds(pl.multiple_of((place + 1) * BLOCK, BLOCK), BLOCK)
            out_ref[into, width : 2 * width] = key_sum[source, :].astype(LOW)
            out_ref[into, 2 * width :] = value_sum[source, :].astype(LOW)
            return carry

        lax.fori_loop(0, blocks, write, 0)


def _params():
    return pltpu.CompilerParams(dimension_semantics=("arbitrary",), vmem_limit_bytes=56 << 20)


def attend(qkv_rows, query_id, key_id):
    rows, triple = qkv_rows.shape
    width, blocks = triple // 3, rows // BLOCK
    heads = width // HEAD_DIM
    return pl.pallas_call(
        lambda *refs: attend_kernel(width, blocks, *refs),
        grid=(blocks,),
        in_specs=[
            pl.BlockSpec((rows, triple), lambda i: (0, 0)),
            pl.BlockSpec((1, 1, BLOCK), lambda i: (i, 0, 0)),
            pl.BlockSpec((rows + 2 * BLOCK, 1), lambda i: (0, 0)),
        ],
        out_specs=[
            pl.BlockSpec((BLOCK, width), lambda i: (i, 0)),
            pl.BlockSpec((1, heads // 2, 2 * BLOCK), lambda i: (i, 0, 0)),
        ],
        out_shape=[
            jax.ShapeDtypeStruct((rows, width), LOW),
            jax.ShapeDtypeStruct((blocks, heads // 2, 2 * BLOCK), F32),
        ],
        compiler_params=_params(),
        cost_estimate=NO_COST,
    )(qkv_rows, query_id, key_id)


def attend_back(qkv_rows, grad_rows, log_total, query_id, key_id):
    rows, triple = qkv_rows.shape
    width, blocks = triple // 3, rows // BLOCK
    heads = width // HEAD_DIM
    return pl.pallas_call(
        lambda *refs: attend_back_kernel(width, blocks, *refs),
        grid=(blocks,),
        in_specs=[
            pl.BlockSpec((rows, triple), lambda i: (0, 0)),
            pl.BlockSpec((rows, width), lambda i: (0, 0)),
            pl.BlockSpec((1, heads // 2, 2 * BLOCK), lambda i: (i, 0, 0)),
            pl.BlockSpec((1, 1, BLOCK), lambda i: (i, 0, 0)),
            pl.BlockSpec((rows + 2 * BLOCK, 1), lambda i: (0, 0)),
        ],
        out_specs=pl.BlockSpec((rows, triple), lambda i: (0, 0)),
        out_shape=jax.ShapeDtypeStruct((rows, triple), LOW),
        scratch_shapes=[
            pltpu.VMEM((rows + 2 * BLOCK, width), F32),
            pltpu.VMEM((rows + 2 * BLOCK, width), F32),
        ],
        compiler_params=_params(),
        cost_estimate=NO_COST,
    )(qkv_rows, grad_rows, log_total, query_id, key_id)


def layer_norm(values, gain_row, bias_row):
    centre = values - jnp.mean(values, axis=-1, keepdims=True)
    spread = jnp.mean(centre * centre, axis=-1, keepdims=True)
    return centre * lax.rsqrt(spread + 1e-06) * gain_row + bias_row


def norm_back_kernel(
    groups, keep_sum, values_ref, cot_ref, more_ref, gain_ref, low_ref, sum_ref, out_ref=None
):
    @pl.when(pl.program_id(0) == 0)
    def _():
        sum_ref[...] = jnp.zeros_like(sum_ref)

    values = values_ref[...]
    if groups:
        group = lax.broadcasted_iota(jnp.int32, (values.shape[0], groups), 1)
        chosen = jnp.where(more_ref[...] == group, 1.0, 0.0)
        cot = jnp.dot(chosen, cot_ref[...], precision=HIGHEST_PREC, preferred_element_type=F32)
    else:
        cot = cot_ref[...]
    centre = values - jnp.mean(values, axis=-1, keepdims=True)
    scale = lax.rsqrt(jnp.mean(centre * centre, axis=-1, keepdims=True) + 1e-06)
    normed = centre * scale
    scaled = cot * gain_ref[...]
    grad = scale * (
        scaled
        - jnp.mean(scaled, axis=-1, keepdims=True)
        - normed * jnp.mean(scaled * normed, axis=-1, keepdims=True)
    )
    if not groups:
        grad = grad + more_ref[...]
    low = grad.astype(LOW)
    if keep_sum:
        out_ref[...] = grad
    low_ref[...] = low
    for row, value in enumerate((cot * normed, cot, low.astype(F32))):
        sum_ref[row : row + 1, :] += jnp.sum(value, axis=0, keepdims=True)


def norm_back(values, gain_row, cotangent, more, keep_sum=True):
    rows, width = values.shape
    groups = cotangent.shape[0] if more.shape[1] == 1 else 0
    tile = rows // 8
    block = pl.BlockSpec((tile, width), lambda i: (i, 0))
    line = pl.BlockSpec((1, width), lambda i: (0, 0))
    out_specs = [block, pl.BlockSpec((8, width), lambda i: (0, 0))]
    out_shape = [jax.ShapeDtypeStruct((rows, width), LOW), jax.ShapeDtypeStruct((8, width), F32)]
    if keep_sum:
        out_specs.append(block)
        out_shape.append(jax.ShapeDtypeStruct((rows, width), F32))
    return pl.pallas_call(
        lambda *refs: norm_back_kernel(groups, keep_sum, *refs),
        grid=(8,),
        in_specs=[
            block,
            pl.BlockSpec((groups, width), lambda i: (0, 0)) if groups else block,
            pl.BlockSpec((tile, 1), lambda i: (i, 0)) if groups else block,
            line,
        ],
        out_specs=out_specs,
        out_shape=out_shape,
        compiler_params=_params(),
        cost_estimate=NO_COST,
    )(values, cotangent, more, gain_row[None])


def small_kernel(spots_ref, first_ref, second_ref, last_ref, qkv_ref, up_ref, out_ref):
    width, slots = out_ref.shape[1], spots_ref.shape[0]
    out_ref[...] = jnp.zeros_like(out_ref)
    rows = [(first_ref, 0), (first_ref, 1), (second_ref, 0), (second_ref, 1), (last_ref, 0), (last_ref, 1)]
    rows += [(first_ref, 2), (qkv_ref, 0), (qkv_ref, 2), (second_ref, 2), (last_ref, 2)]
    for row, (ref, which) in enumerate(rows):
        if ref is qkv_ref:
            out_ref[row : row + 1, :] = ref[:, which * width : (which + 1) * width]
        else:
            out_ref[row : row + 1, :] = ref[which : which + 1, :]
    for slot in range(slots):
        out_ref[pl.ds(16 + spots_ref[slot], 1), :] = up_ref[slot : slot + 1, :]


def small_sums(first, second, last, qkv_sum, up_sums):
    width, count = first.shape[1], lax.axis_size("pack")
    spots = relative_packs() ^ lax.axis_index("pack")
    up_sum = jnp.concatenate(up_sums).reshape(count, -1)
    arrays = [first, second, last, qkv_sum[None], jnp.pad(up_sum, ((0, 0), (0, width - up_sum.shape[1])))]
    return pl.pallas_call(
        small_kernel,
        in_specs=[pl.BlockSpec(memory_space=pltpu.SMEM)] + [pl.BlockSpec(memory_space=pltpu.VMEM)] * len(arrays),
        out_specs=pl.BlockSpec(memory_space=pltpu.VMEM),
        out_shape=jax.ShapeDtypeStruct((16 + count, width), F32),
        compiler_params=pltpu.CompilerParams(vmem_limit_bytes=16 << 20),
        cost_estimate=NO_COST,
    )(spots, *arrays)


def gelu(values):
    return 0.5 * values * (1.0 + lax.erf(values * math.sqrt(0.5)))


def gelu_slope(values):
    return 0.5 * (1.0 + lax.erf(values * math.sqrt(0.5))) + values * (
        math.sqrt(0.5 / math.pi) * jnp.exp(-0.5 * values * values)
    )


def as_rows(width, *values):
    rows = [jnp.pad(value.reshape(1, -1), ((0, 0), (0, width - value.size))) for value in values]
    return jnp.pad(jnp.concatenate(rows), ((0, 8 - len(rows)), (0, 0)))


def from_rows(cells, shape):
    rows, columns = shape
    flat = cells[:, 0, : rows * columns].reshape(-1, rows, columns)
    return flat.transpose(1, 0, 2).reshape(rows, -1)


def mm(spec, left, right):
    return jnp.einsum(spec, left, right, preferred_element_type=F32)


def column_sum(rows):
    return jnp.sum(rows.astype(F32), axis=0)


def hmul(left, right):
    return jnp.dot(left, right, precision=NS_PREC, preferred_element_type=F32)


def ortho(columns, beside):
    gram_part = lax.dot_general(columns, columns, (TN, ((), ())), precision=NS_PREC, preferred_element_type=F32)
    folded, beside = column_all_sum(fold(gram_part), beside)
    gram_mat, scale = unfold(folded, columns.shape[1])
    iterate = columns * scale
    eye = jnp.eye(gram_mat.shape[0], dtype=F32)
    for step in range(NS_STEPS):
        if step < NS_STEPS - 1:
            square = hmul(gram_mat, gram_mat)
            poly = COEF_ONE * eye + COEF_TWO * gram_mat + COEF_THREE * square
            poly_gram = COEF_ONE * gram_mat + COEF_TWO * square + COEF_THREE * hmul(square, gram_mat)
            iterate = hmul(iterate, poly)
            gram_mat = hmul(poly, poly_gram)
        else:
            first_pass = hmul(iterate, gram_mat)
            iterate = COEF_ONE * iterate + COEF_TWO * first_pass + COEF_THREE * hmul(first_pass, gram_mat)
    return iterate, beside


def to_columns(shards):
    chip = lax.axis_index("pack") >> 1
    most = max(m.shape[0] for m in shards)
    filled = [jnp.pad(m, ((0, most - m.shape[0]), (0, 0))) for m in shards]
    filled += [jnp.zeros_like(filled[0])] * (lax.axis_size("pack") // 2 - len(shards))
    stacked = jnp.stack(filled)
    parts = [pick(stacked, chip)]
    parts += [swap(pick(stacked, chip ^ (k // 2)), "pack", k) for k in other_chips()]
    return jnp.stack(parts)


def from_columns(value, counts):
    back = [value[0]] + [swap(value[k // 2], "pack", k) for k in other_chips()]
    return [_choose(back, lax.axis_index("pack") >> 1, m)[:count] for m, count in enumerate(counts)]


def muon_update(weight, iterate):
    col_ratio = math.sqrt(
        max(1.0, iterate.shape[1] * lax.axis_size(("pack", "seq")) / weight.shape[0])
    )
    return weight * (1.0 - MUON_RATE * DECAY) - MUON_RATE * col_ratio * iterate


def adam_update(weight, first_moment, second_moment, gradient, factor, count_float):
    scaled = factor * gradient
    new_first = BETA_ONE * first_moment + (1.0 - BETA_ONE) * scaled
    new_second = BETA_TWO * second_moment + (1.0 - BETA_TWO) * scaled * scaled
    first_hat = new_first / (1.0 - jnp.power(BETA_ONE, count_float))
    second_hat = new_second / (1.0 - jnp.power(BETA_TWO, count_float))
    new_weight = weight - ADAM_RATE * (first_hat / (jnp.sqrt(second_hat) + 1e-08) + DECAY * weight)
    return (new_weight, new_first, new_second)


def deal_rows(lengths, keep_mask, shard_len):
    packs, images = lengths.shape
    seq_count, seq_place = lax.axis_size("seq"), lax.axis_index("seq")
    image_range = jnp.arange(images, dtype=jnp.int32)
    upto = image_range[None, :] <= image_range[:, None]
    ends = jnp.sum(jnp.where(upto[None], lengths[:, None, :], 0), axis=2, dtype=jnp.int32)
    starts = ends - lengths
    cuts = jnp.arange(1, seq_count, dtype=jnp.int32) * shard_len
    straddles = (starts[:, None, :] < cuts[None, :, None]) & (ends[:, None, :] > cuts[None, :, None])
    behind = jnp.sum(jnp.where(straddles, cuts[None, :, None] - starts[:, None, :], 0), axis=2, dtype=jnp.int32)
    ahead = jnp.sum(jnp.where(straddles, ends[:, None, :] - cuts[None, :, None], 0), axis=2, dtype=jnp.int32)
    excess = jnp.zeros_like(cuts)
    moves = []
    for pack in range(packs):
        more, less = excess + ahead[pack], excess - behind[pack]
        forward = jnp.abs(more) <= jnp.abs(less)
        excess = jnp.where(forward, more, less)
        moves.append(jnp.where(forward, ahead[pack], -behind[pack]))
    borders = jnp.concatenate(
        [
            jnp.zeros((packs, 1), jnp.int32),
            cuts[None, :] + jnp.stack(moves),
            jnp.full((packs, 1), PACK_LEN, jnp.int32),
        ],
        axis=1,
    )
    first = lax.dynamic_index_in_dim(borders, seq_place, 1, keepdims=False)
    held = lax.dynamic_index_in_dim(borders, seq_place + 1, 1, keepdims=False) - first
    pack_range = jnp.arange(packs, dtype=jnp.int32)
    before = jnp.sum(jnp.where(pack_range[None, :] < pack_range[:, None], held[None, :], 0), axis=1, dtype=jnp.int32)
    row = jnp.arange(packs * shard_len + MAXLEN, dtype=jnp.int32)
    in_pack = (row[:, None] >= before[None, :]) & (row[:, None] < (before + held)[None, :])
    valid = jnp.any(in_pack, axis=1)

    def of_pack(values):
        return jnp.sum(jnp.where(in_pack, values, 0), axis=1, dtype=jnp.int32)

    pack_of = of_pack(pack_range[None, :])
    place = of_pack(row[:, None] - before[None, :] + first[None, :])
    window = shard_len + 2 * MAXLEN
    source = jnp.where(valid, pack_of * window + place - (seq_place * shard_len - MAXLEN), -1)
    row_ends = jnp.sum(jnp.where(in_pack[:, :, None], ends[None], 0), axis=1, dtype=jnp.int32)
    row_starts = jnp.sum(jnp.where(in_pack[:, :, None], starts[None], 0), axis=1, dtype=jnp.int32)
    image_of = jnp.sum((place[:, None] >= row_ends).astype(jnp.int32), axis=1, dtype=jnp.int32)
    is_first = jnp.any(place[:, None] == row_starts, axis=1)
    keep_rows = mm("rp,pj->rj", in_pack.astype(LOW), (keep_mask > 0).astype(LOW))
    spot = jnp.arange(PACK_LEN, dtype=jnp.int32)
    kept = jnp.any((place[:, None] == spot[None, :]) & (keep_rows > 0.5), axis=1)
    live = valid & (kept | is_first)
    group = jnp.where(valid, pack_of * images + image_of, -1)

    spots = jnp.arange(PACK_LEN, dtype=jnp.int32)[None, None, :]
    inside = (spots >= starts[:, :, None]) & (spots < ends[:, :, None])
    counted = inside & ((keep_mask > 0)[:, None, :] | (spots == starts[:, :, None]))
    counts = jnp.sum(counted.astype(F32), axis=2)
    return source, group, live, counts.reshape(-1)


def body(
    patches,
    lengths,
    keep_mask,
    labels,
    step_count,
    embed_weight,
    embed_first,
    embed_second,
    qkv_weight,
    qkv_moment,
    output_weight,
    output_moment,
    up_weight,
    up_moment,
    down_weight,
    down_moment,
    small_params,
    small_first,
    small_second,
    head_weight,
    head_first,
    head_second,
    head_bias,
    bias_first,
    bias_second,
):
    packs, shard_len, patch_in = patches.shape
    images = lengths.shape[1]
    width = qkv_weight.shape[0]
    seq_count, seq_place = lax.axis_size("seq"), lax.axis_index("seq")
    pack_count, pack_place = lax.axis_size("pack"), lax.axis_index("pack")
    small_rows = small_params.shape[0]

    bundle = [
        embed_weight.T,
        qkv_weight.T,
        output_weight.T,
        as_rows(width, small_params, head_bias),
    ]
    spots = [0]
    for piece in bundle:
        spots.append(spots[-1] + piece.shape[0])
    first = Gather(jnp.concatenate([piece.astype(LOW) for piece in bundle]))
    up_gather, down_gather = Gather(up_weight.T.astype(LOW)), Gather(down_weight.T.astype(LOW))
    first.along_seq()
    first.block, patches = hold(first.block, patches)
    first.in_plane()
    ends = seq_count - 1
    from_left = lax.ppermute(patches[:, shard_len - MAXLEN :], "seq", [(i, i + 1) for i in range(ends)])
    from_right = lax.ppermute(patches[:, :MAXLEN], "seq", [(i + 1, i) for i in range(ends)])
    window = jnp.concatenate([from_left, patches, from_right], axis=1).reshape(-1, patch_in)
    source, group, live, counts = deal_rows(lengths, keep_mask, shard_len)
    chosen = (source[:, None] == jnp.arange(window.shape[0], dtype=jnp.int32)[None, :]).astype(LOW)
    tokens = mm("rw,wi->ri", chosen, window).astype(LOW)
    tokens, up_gather.shard, *first.parts = hold(tokens, up_gather.shard, *first.parts)
    up_gather.send_seq()
    embed_full, qkv_full, output_full, small_full = first.pieces(spots)
    embed_full, qkv_full, output_full = (
        value.reshape(-1, width) for value in (embed_full, qkv_full, output_full)
    )
    (gain_bias,) = hold(from_rows(small_full, small_params.shape).astype(F32))
    bias_full = lax.dynamic_slice_in_dim(small_full, pack_place * seq_count, seq_count, 0)
    bias_full = bias_full[:, 1, : head_bias.shape[0]].reshape(-1)

    rows = tokens.shape[0]
    query_id = group.reshape(rows // BLOCK, 1, BLOCK)
    key_id = jnp.pad(jnp.where(live, group, -2), (BLOCK, BLOCK), constant_values=-2)[:, None]
    group_count = packs * images
    member = (
        (group[None, :] == jnp.arange(group_count, dtype=jnp.int32)[:, None]) & live[None, :]
    ).astype(F32)

    embedded = mm("ri,di->rd", tokens, embed_full) + gain_bias[6]
    embedded, up_gather.parts[0], down_gather.shard = hold(embedded, up_gather.parts[0], down_gather.shard)
    up_gather.join_seq()
    up_gather.in_plane()
    down_gather.doubling()
    normed_one = layer_norm(embedded, gain_bias[0], gain_bias[1]).astype(LOW)
    qkv_bias = jnp.concatenate([gain_bias[7], jnp.zeros_like(gain_bias[7]), gain_bias[8]])
    qkv_rows = (mm("rd,ed->re", normed_one, qkv_full) + qkv_bias).astype(LOW)
    qkv_rows, down_gather.block, head_low, *up_gather.parts = hold(
        qkv_rows, down_gather.block, head_weight.astype(LOW), *up_gather.parts
    )
    head_full = lax.all_gather(head_low, "seq", axis=0, tiled=True)
    down_gather.in_plane()
    up_full = [half.reshape(-1, width) for half in up_gather.halves()]
    attn_low, log_total = attend(qkv_rows, query_id, key_id)
    attn_low, *down_gather.parts = hold(attn_low, *down_gather.parts)
    down_full = [half.reshape(-1, width) for half in down_gather.halves()]
    after_attn = embedded + mm("re,de->rd", attn_low, output_full) + gain_bias[9]
    normed_two = layer_norm(after_attn, gain_bias[2], gain_bias[3]).astype(LOW)
    up_bias = jnp.take(
        gain_bias[11:15].reshape(pack_count, -1), relative_packs() ^ pack_place, axis=0
    ).reshape(2, -1)
    up_rows = [mm("rd,fd->rf", normed_two, up_full[half]) + up_bias[half] for half in range(2)]
    active = [gelu(rows).astype(LOW) for rows in up_rows]
    after_mlp = (
        after_attn
        + (mm("rf,fd->rd", active[0], down_full[0]) + mm("rf,fd->rd", active[1], down_full[1]))
        + gain_bias[10]
    )
    final_rows = layer_norm(after_mlp, gain_bias[4], gain_bias[5])
    pool_sums = jnp.dot(member, final_rows, precision=HIGHEST_PREC, preferred_element_type=F32)
    pooled_mine = (pool_sums / counts[:, None]).astype(LOW)

    img_share = group_count // seq_count
    split = pooled_mine.reshape(seq_count, img_share, width)
    pooled_low = tree_sum(
        [pick(split, seq_place).astype(F32)]
        + [swap(pick(split, seq_place ^ k), "seq", k).astype(F32) for k in range(1, seq_count)]
    ).astype(LOW)
    pooled_rows = jnp.concatenate(gather_blocks(pooled_low), axis=0).reshape(-1, width)
    depth = head_weight.shape[0]
    label_cols = head_full.shape[1]
    logits = mm("nd,dc->nc", pooled_rows, head_full) + bias_full.astype(F32)
    label_rows = jnp.take(
        pick(labels.reshape(pack_count, seq_count, img_share), seq_place, 1),
        relative_packs() ^ pack_place,
        axis=0,
    ).reshape(-1)
    class_ids = pack_place * label_cols + jnp.arange(label_cols, dtype=jnp.int32)
    valid = (class_ids < LABELS).astype(F32)
    target = (label_rows[:, None] == class_ids[None, :]).astype(F32)
    image_total = labels.shape[0] * labels.shape[1]
    loss_part = jnp.sum(valid[None, :] * (jax.nn.softplus(logits) - target * logits)) / image_total
    grad_logits = (valid[None, :] * (jax.nn.sigmoid(logits) - target) / image_total).astype(LOW)
    pooled_part = mm("nc,dc->nd", grad_logits, head_full).reshape(pack_count, img_share, width)
    pooled_grad = pack_scatter(pooled_part)
    pooled_grad = jnp.concatenate(absolute(relative(pooled_grad, "seq"), seq_place), axis=0)
    pooled_grad = pooled_grad / counts[:, None]

    traded, pooled_grad = hold(jnp.concatenate([pooled_rows, grad_logits], axis=1), pooled_grad)
    traded = lax.all_gather(traded, "seq", axis=0, tiled=True)

    grad_mlp_low, sums_last, grad_mlp = norm_back(
        after_mlp, gain_bias[4], pooled_grad, jnp.where(live, group, -1)[:, None]
    )
    down_sum, up_sum = Scatter(0, width, True), Scatter(1, width, True)
    half = width // 2
    late_sums = [Scatter(0, half), Scatter(1, half)]
    pair_sums = [Scatter(0, half), Scatter(1, half)]
    down_out = mm("rf,rd->fd", active[1], grad_mlp_low)
    down_keep = mm("rf,rd->fd", active[0], grad_mlp_low)
    grad_mlp_low, down_out, down_keep = hold(grad_mlp_low, down_out, down_keep)
    down_out = down_sum.start_halves(down_keep, down_out)
    grad_upper = [
        (mm("rd,fd->rf", grad_mlp_low, down_full[side]) * gelu_slope(up_rows[side])).astype(LOW)
        for side in range(2)
    ]
    up_out = mm("rf,rd->fd", grad_upper[1], normed_two)
    up_keep = mm("rf,rd->fd", grad_upper[0], normed_two)
    grad_upper[0], grad_upper[1], up_out, up_keep = hold(*grad_upper, up_out, up_keep)
    up_out = up_sum.start_halves(up_keep, up_out)
    grad_normed = mm("rf,fd->rd", grad_upper[0], up_full[0]) + mm("rf,fd->rd", grad_upper[1], up_full[1])
    down_out = down_sum.step(down_out)
    grad_normed, down_out = hold(grad_normed, down_out)
    grad_attn_low, sums_second, grad_attn = norm_back(
        after_attn, gain_bias[2], grad_normed, grad_mlp
    )
    grad_mixed = mm("rd,de->re", grad_attn_low, output_full).astype(LOW)
    up_out = up_sum.step(up_out)
    grad_mixed, up_out = hold(grad_mixed, up_out)
    grad_qkv = attend_back(qkv_rows, grad_mixed, log_total, query_id, key_id)
    down_out, up_out = down_sum.step(down_out), up_sum.step(up_out)
    grad_qkv, down_out, up_out = hold(grad_qkv, down_out, up_out)
    grad_normed = mm("re,ed->rd", grad_qkv, qkv_full)
    grad_embed_rows, sums_first = norm_back(embedded, gain_bias[0], grad_normed, grad_attn, keep_sum=False)
    output_grad = mm("rd,re->de", grad_attn_low, attn_low)
    embed_grad = mm("rd,ri->di", grad_embed_rows, tokens)
    down_sum.finish(down_out)
    up_sum.finish(up_out)
    early = jnp.concatenate([down_sum.value, up_sum.value], axis=1)
    pair_keep, pair_out = late_halves(output_grad, embed_grad)
    grad_qkv, pair_out, early = hold(grad_qkv, pair_out, early)
    early = lax.psum_scatter(early, "seq", scatter_dimension=0)
    late_keep, late_out = late_halves(mm("re,rd->ed", grad_qkv, normed_one))
    pair = pair_keep + swap(pair_out, "pack", 1)
    pair_outs = [
        each.start_joined(part) for each, part in zip(pair_sums, (pair[..., :half], pair[..., half:]))
    ]
    late_out, grad_qkv, traded, *pair_outs = hold(late_out, grad_qkv, traded, *pair_outs)
    all_logits = traded[:, width:]
    bias_grad = pick(column_sum(all_logits).reshape(seq_count, -1), seq_place)
    late = late_keep + swap(late_out, "pack", 1)
    late_outs = [
        each.start_joined(part) for each, part in zip(late_sums, (late[..., :half], late[..., half:]))
    ]
    bias_grad, grad_qkv, traded, grad_upper[0], grad_upper[1], *held = hold(
        bias_grad, grad_qkv, traded, *grad_upper, *late_outs, *[each.keep for each in pair_sums]
    )
    late_outs = held[:2]
    pair_sums[0].keep, pair_sums[1].keep = held[2:]
    all_pooled = pick(traded[:, :width].reshape(-1, seq_count, head_weight.shape[0]), seq_place, 1)
    head_grad = mm("nd,nc->dc", all_pooled, traded[:, width:])
    small_mine = small_sums(
        sums_first, sums_second, sums_last, column_sum(grad_qkv), [column_sum(side) for side in grad_upper]
    )
    for each, sent in zip(pair_sums, pair_outs):
        each.finish(sent)
    pair = jnp.concatenate([each.value for each in pair_sums], axis=2)
    late_outs = [each.step(sent) for each, sent in zip(late_sums, late_outs)]
    small_mine, head_grad, pair, *late_outs = hold(small_mine, head_grad, pair, *late_outs)
    small_total = small_mine + swap(small_mine, "pack", 1)
    for each, sent in zip(late_sums, late_outs):
        each.finish(sent)
    late_sum = SeqScatter(
        jnp.concatenate([jnp.concatenate([each.value for each in late_sums], axis=2), pair], axis=1)
    )
    late_out, small_total, early = hold(late_sum.send(), small_total, early)
    small_total = sum_chips(small_total)
    late_out = late_sum.step(late_out)
    late_out, small_total = hold(late_out, small_total)
    small_total = all_sum(small_total, "seq")
    while late_out is not None:
        late_out = late_sum.step(late_out)
    late_sum.value, small_total = hold(late_sum.value, small_total)
    down_share, up_share = jnp.split(early, 2)
    late_share = late_sum.result()
    widths = [qkv_weight.shape[1], output_weight.shape[1], embed_weight.shape[1]]
    qkv_share, output_share = late_share[: widths[0]], late_share[widths[0] : widths[0] + widths[1]]
    embed_share = late_share[widths[0] + widths[1] :].T
    hidden = down_weight.shape[1] * seq_count
    small_total = jnp.concatenate(
        [small_total[:11], small_total[16:, :hidden].reshape(small_rows - 11, width)], axis=0
    )
    place = pack_place * seq_count + seq_place
    small_share = pick(small_total.reshape(small_rows, pack_count * seq_count, -1), place, 1)

    shares = (early, late_share, head_grad, bias_grad)
    square_sum = sum((jnp.sum(piece * piece) for piece in shares))
    sums = jnp.broadcast_to(jnp.stack([loss_part, square_sum])[:, None], (2, BLOCK))
    sums = sum_plane(all_sum(sums, "seq"))
    loss_value, square_total = sums[0, 0], sums[1, 0] + jnp.sum(small_total * small_total)
    grad_norm = jnp.sqrt(square_total)
    factor = jnp.minimum(1.0, CLIP_NORM / (grad_norm + 1e-06))
    muon_shares = (qkv_share, output_share, up_share, down_share)
    moments = [
        MUON_MU * moment.T + factor * share
        for moment, share in zip((qkv_moment, output_moment, up_moment, down_moment), muon_shares)
    ]
    columns = to_columns(moments)
    count_float = step_count[0].astype(F32)
    iterates, (new_head, new_head_first, new_head_second) = ortho(
        columns.reshape(-1, width),
        adam_update(head_weight, head_first, head_second, head_grad, factor, count_float),
    )
    iterates = iterates.reshape(columns.shape)
    iterates = [iterate.T for iterate in from_columns(iterates, [m.shape[0] for m in moments])]
    moments = [moment.T for moment in moments]
    new_qkv = muon_update(qkv_weight, iterates[0])
    new_output = muon_update(output_weight, iterates[1])
    new_up = muon_update(up_weight, iterates[2])
    new_down = muon_update(down_weight, iterates[3])
    new_embed, new_embed_first, new_embed_second = adam_update(
        embed_weight, embed_first, embed_second, embed_share, factor, count_float
    )
    new_small, new_small_first, new_small_second = adam_update(
        small_params, small_first, small_second, small_share, factor, count_float
    )
    new_bias, new_bias_first, new_bias_second = adam_update(
        head_bias, bias_first, bias_second, bias_grad, factor, count_float
    )
    return (
        loss_value,
        grad_norm,
        new_embed,
        new_embed_first,
        new_embed_second,
        new_qkv,
        moments[0],
        new_output,
        moments[1],
        new_up,
        moments[2],
        new_down,
        moments[3],
        new_small,
        new_small_first,
        new_small_second,
        new_head,
        new_head_first,
        new_head_second,
        new_bias,
        new_bias_first,
        new_bias_second,
    )


def solution(mesh):
    both = P(None, ("pack", "seq"))
    head = P("seq", "pack")
    line = P(("pack", "seq"))
    return jax.shard_map(
        body,
        mesh=mesh,
        in_specs=(P("pack", "seq", None), P("pack", None), P("pack", None), P(), P())
        + (both,) * 14
        + (head,) * 3
        + (line,) * 3,
        out_specs=(P(), P()) + (both,) * 14 + (head,) * 3 + (line,) * 3,
        check_vma=False,
    )
```

```python
import math

import jax
import jax.numpy as jnp
from jax import lax
from jax.experimental import pallas as pl
from jax.experimental.pallas import tpu as pltpu
from jax.sharding import PartitionSpec as P

HEAD_DIM = 64
LABELS = 21843
PACK_LEN = 1024
MAXLEN = 128
NS_STEPS = 2
BLOCK = 128
PAIR = 2 * HEAD_DIM

HIGHEST_PREC = lax.Precision.HIGHEST
NS_PREC = lax.Precision.HIGH
CLIP_NORM = 1.0
MUON_MU = 0.95
MUON_RATE = 1.0
ADAM_RATE = 0.02
BETA_ONE = 0.9
BETA_TWO = 0.95
DECAY = 0.01
COEF_ONE = 3.4445
COEF_TWO = -4.775
COEF_THREE = 2.0315
SCALE = HEAD_DIM ** (-0.5)
LOW = jnp.bfloat16
F32 = jnp.float32
NEG = -1e30
NO_COST = pl.CostEstimate(flops=0, bytes_accessed=0, transcendentals=0)


def swap(value, axis, bit):
    return lax.ppermute(value, axis, [(i, i ^ bit) for i in range(lax.axis_size(axis))])


def pick(value, index, dim=0):
    return lax.dynamic_index_in_dim(value, index, dim, keepdims=False)


def tree_sum(parts):
    while len(parts) > 1:
        parts = [parts[i] + parts[i + 1] for i in range(0, len(parts), 2)]
    return parts[0]


def relative(value, axis):
    return [value] + [swap(value, axis, k) for k in range(1, lax.axis_size(axis))]


def absolute(parts, place):
    return [_choose(parts, place, j) for j in range(len(parts))]


def _choose(parts, place, j):
    out = parts[j]
    for other in range(1, len(parts)):
        out = jnp.where(place == other, parts[j ^ other], out)
    return out


def all_sum(value, axis):
    return tree_sum(relative(value, axis))


def hold(*values):
    return lax.optimization_barrier(values)


def other_chips():
    return list(range(2, lax.axis_size("pack"), 2))


def relative_packs():
    same = [0] + other_chips()
    return jnp.array(same + [k + 1 for k in same], jnp.int32)


def relative_slots():
    count = lax.axis_size("pack")
    offset = lax.axis_index("pack") ^ jnp.arange(count, dtype=jnp.int32)
    return (offset >> 1) + (offset & 1) * (count // 2)


def gather_blocks(block):
    own = jnp.stack([block] + [swap(block, "pack", k) for k in other_chips()])
    return own, swap(own, "pack", 1)


def by_index(parts, place):
    if len(parts) <= 8:
        return jnp.stack(absolute(parts, place))
    value = jnp.stack(parts)
    shape, bit = value.shape, 1
    while bit < len(parts):
        value = value.reshape((-1, 2, bit) + shape[1:])
        turned = jnp.concatenate([value[:, 1:], value[:, :1]], axis=1)
        value = jnp.where((place & bit) == 0, value, turned)
        bit *= 2
    return value.reshape(shape)


def by_core(own, other, dim):
    return jnp.where(
        (lax.axis_index("pack") & 1) == 0, jnp.stack([own, other], axis=dim), jnp.stack([other, own], axis=dim)
    )


class Gather:
    def __init__(self, shard):
        self.shard = shard

    def along_seq(self):
        self.block = by_index(relative(self.shard, "seq"), lax.axis_index("seq"))

    def send_seq(self):
        self.parts = relative(self.shard, "seq")

    def join_seq(self):
        self.block = by_index(self.parts, lax.axis_index("seq"))

    def doubling(self):
        place, count, bit = lax.axis_index("seq"), lax.axis_size("seq"), 1
        block = self.shard[None]
        while bit < count:
            other = swap(block, "seq", bit)
            block = jnp.where(
                (place & bit) == 0,
                jnp.concatenate([block, other], axis=0),
                jnp.concatenate([other, block], axis=0),
            )
            bit *= 2
        self.block = block
        return block

    def in_plane(self):
        self.parts = [self.block] + [swap(self.block, "pack", k) for k in other_chips()]

    def pieces(self, spots):
        mine = by_index(self.parts, lax.axis_index("pack") >> 1)
        other = swap(mine, "pack", 1)
        return [
            by_core(mine[:, :, here:there], other[:, :, here:there], 1).reshape(-1, there - here, mine.shape[-1])
            for here, there in zip(spots[:-1], spots[1:])
        ]

    def halves(self):
        own = jnp.stack(self.parts)
        return own, swap(own, "pack", 1)


class Scatter:
    def __init__(self, order, width, relative=False):
        self.left = [1 << b for b in reversed(range(lax.axis_size("pack").bit_length() - 1))]
        chips = [b for b in self.left if b > 1]
        self.order = [1] + (chips if order == 0 else chips[::-1])
        self.relative, self.width = relative, width

    def start_halves(self, keep, send):
        self.left.remove(1)
        self.bit = self.order.pop(0)
        shape = (2,) * len(self.left) + (lax.axis_size("seq"), -1, self.width)
        self.keep = keep.reshape(shape)
        return send.reshape(shape)

    def start_joined(self, value):
        self.left.remove(1)
        self.order.pop(0)
        self.value = value
        return self.send()

    def send(self):
        self.bit = bit = self.order.pop(0)
        dim = self.left.index(bit)
        self.left.remove(bit)
        if self.relative:
            self.keep = lax.index_in_dim(self.value, 0, dim, keepdims=False)
            return lax.index_in_dim(self.value, 1, dim, keepdims=False)
        mine = (lax.axis_index("pack") & bit) // bit
        self.keep = pick(self.value, mine, dim)
        return pick(self.value, 1 - mine, dim)

    def step(self, sent):
        self.value = self.keep + swap(sent, "pack", self.bit)
        return self.send() if self.order else None

    def finish(self, sent):
        while sent is not None:
            sent = self.step(sent)


class SeqScatter:
    def __init__(self, value):
        self.value, self.bit = value, 1

    def send(self):
        tail = self.value.shape[-2:]
        split = self.value.reshape((-1, 2) + tail)
        mine = (lax.axis_index("seq") & self.bit) // self.bit
        self.keep = pick(split, mine, 1)
        return pick(split, 1 - mine, 1)

    def step(self, sent):
        self.value = self.keep + swap(sent, "seq", self.bit)
        self.bit *= 2
        return self.send() if self.bit < lax.axis_size("seq") else None

    def result(self):
        return self.value.reshape(self.value.shape[-2:])


def late_halves(*grads):
    seq_count, pack_count = lax.axis_size("seq"), lax.axis_size("pack")
    chips = (2,) * (pack_count.bit_length() - 2)
    core = lax.axis_index("pack") & 1

    def half(which):
        pieces = [
            pick(grad.reshape(chips + (2, seq_count, -1, grad.shape[1])), which, len(chips)) for grad in grads
        ]
        return jnp.concatenate(pieces, axis=-2)

    return half(core), half(1 - core)


def pack_scatter(value):
    half = value.shape[0] // 2
    mine = value[:half] + swap(value[half:], "pack", 1)
    parts = [mine[0]] + [swap(mine[k // 2], "pack", k) for k in other_chips()]
    return tree_sum(parts)


def column_all_sum(value, beside):
    seq_place, count = lax.axis_index("seq"), lax.axis_size("seq")
    core = lax.axis_index("pack") & 1
    split = value.reshape(2, count, -1, value.shape[1])
    mine = pick(split, core) + swap(pick(split, 1 - core), "pack", 1)
    parts = [pick(mine, seq_place)] + [swap(pick(mine, seq_place ^ k), "seq", k) for k in range(1, count)]
    total, *beside = hold(tree_sum(parts), *beside)
    mine = by_index(relative(total, "seq"), seq_place)
    return by_core(mine, swap(mine, "pack", 1), 0).reshape(value.shape), beside


def fold(matrix):
    count, width = matrix.shape[0] // BLOCK, matrix.shape[0]

    def row(i):
        return matrix[i * BLOCK : (i + 1) * BLOCK, i * BLOCK :]

    return jnp.concatenate(
        [jnp.concatenate([row(i), row(count - 1 - i)], axis=1) for i in range(count // 2)], axis=0
    )


def unfold_kernel(folded_ref, out_ref, scale_ref):
    width = out_ref.shape[0]
    count = width // BLOCK

    def block(i, j):
        line = min(i, count - 1 - i)
        column = (j - i) * BLOCK + (0 if line == i else width - line * BLOCK)
        return folded_ref[line * BLOCK : (line + 1) * BLOCK, column : column + BLOCK]

    row = lax.broadcasted_iota(jnp.int32, (BLOCK, BLOCK), 0)
    column = lax.broadcasted_iota(jnp.int32, (BLOCK, BLOCK), 1)
    diagonal = jnp.zeros((BLOCK, BLOCK), F32)
    for i in range(count):
        diagonal += jnp.where(row == column, block(i, i), 0.0)
    trace = jnp.sum(jnp.sum(diagonal, axis=0, keepdims=True), axis=1, keepdims=True)
    scale = 1.0 / (jnp.sqrt(trace) + 1e-07)
    for i in range(count):
        for j in range(i, count):
            value = block(i, j) * scale * scale
            out_ref[i * BLOCK : (i + 1) * BLOCK, j * BLOCK : (j + 1) * BLOCK] = value
            if j > i:
                out_ref[j * BLOCK : (j + 1) * BLOCK, i * BLOCK : (i + 1) * BLOCK] = value.T
    scale_ref[...] = jnp.broadcast_to(scale, scale_ref.shape)


def unfold(folded, width):
    whole = pl.BlockSpec(memory_space=pltpu.VMEM)
    matrix, scale = pl.pallas_call(
        unfold_kernel,
        in_specs=[whole],
        out_specs=[whole, whole],
        out_shape=[jax.ShapeDtypeStruct((width, width), F32), jax.ShapeDtypeStruct((8, BLOCK), F32)],
        compiler_params=pltpu.CompilerParams(vmem_limit_bytes=32 << 20),
        cost_estimate=NO_COST,
    )(folded)
    return matrix, scale[0, 0]


def sum_plane(value):
    return sum_chips(value + swap(value, "pack", 1))


def sum_chips(value):
    return tree_sum([value] + [swap(value, "pack", k) for k in other_chips()])


def _dot(left, right, dims):
    return lax.dot_general(left, right, (dims, ((), ())), preferred_element_type=F32)


NT = ((1,), (1,))
TN = ((0,), (0,))
NN = ((1,), (0,))


def _window(ref, block, blocks, column):
    places = (jnp.maximum(block - 1, 0), block, jnp.minimum(block + 1, blocks - 1))
    return jnp.concatenate(
        [ref[pl.ds(pl.multiple_of(place * BLOCK, BLOCK), BLOCK), column : column + PAIR] for place in places],
        axis=0,
    )


def _halves(value):
    lane = lax.broadcasted_iota(jnp.int32, value.shape, 1)
    zero = jnp.zeros_like(value)
    return jnp.concatenate(
        [jnp.where(lane < HEAD_DIM, value, zero), jnp.where(lane < HEAD_DIM, zero, value)], axis=0
    )


def _merge(value):
    return jnp.concatenate([value[:HEAD_DIM, :BLOCK], value[HEAD_DIM:, BLOCK:]], axis=0).T


def attend_kernel(width, blocks, rows_ref, query_id_ref, key_id_ref, out_ref, log_ref):
    block = pl.program_id(0)
    here = pl.ds(pl.multiple_of(block * BLOCK, BLOCK), BLOCK)
    allowed = key_id_ref[pl.ds(pl.multiple_of(block * BLOCK, BLOCK), 3 * BLOCK), :] == query_id_ref[0]
    for pair in range(width // PAIR):
        column = pair * PAIR
        queries = _halves(rows_ref[here, column : column + PAIR] * SCALE)
        keys = _window(rows_ref, block, blocks, width + column)
        values = _window(rows_ref, block, blocks, 2 * width + column)
        mixed = []
        for lanes in (slice(0, BLOCK), slice(BLOCK, 2 * BLOCK)):
            scores = jnp.where(allowed, _dot(keys, queries[lanes], NT), NEG)
            top = jnp.max(scores, axis=0, keepdims=True)
            raised = jnp.exp(scores - top)
            total = jnp.sum(raised, axis=0, keepdims=True)
            probs = (raised * (1.0 / total)).astype(LOW)
            log_ref[0, pair : pair + 1, lanes] = top + jnp.log(total)
            mixed.append(_dot(values, probs, TN))
        out_ref[:, column : column + PAIR] = _merge(jnp.concatenate(mixed, axis=1)).astype(LOW)


def attend_back_kernel(
    width, blocks, rows_ref, grad_ref, log_ref, query_id_ref, key_id_ref, out_ref, key_sum, value_sum
):
    block = pl.program_id(0)

    @pl.when(block == 0)
    def _():
        key_sum[...] = jnp.zeros_like(key_sum)
        value_sum[...] = jnp.zeros_like(value_sum)

    span = pl.ds(pl.multiple_of(block * BLOCK, BLOCK), 3 * BLOCK)
    here = pl.ds(pl.multiple_of(block * BLOCK, BLOCK), BLOCK)
    allowed = key_id_ref[span, :] == query_id_ref[0]
    allowed = jnp.concatenate([allowed, allowed], axis=1)
    for pair in range(width // PAIR):
        column = pair * PAIR
        lanes = slice(column, column + PAIR)
        queries = _halves(rows_ref[here, lanes] * SCALE)
        grads = _halves(grad_ref[here, lanes])
        keys = _window(rows_ref, block, blocks, width + column)
        values = _window(rows_ref, block, blocks, 2 * width + column)
        scores = jnp.where(allowed, _dot(keys, queries, NT), NEG)
        probs = jnp.exp(scores - log_ref[0, pair : pair + 1, :])
        grad_probs = _dot(values, grads, NT)
        inner = jnp.sum(probs * grad_probs, axis=0, keepdims=True)
        grad_scores = (probs * (grad_probs - inner)).astype(LOW)
        out_ref[here, lanes] = (_merge(_dot(keys, grad_scores, TN)) * SCALE).astype(LOW)
        key_sum[span, lanes] += _dot(grad_scores, queries, NN)
        value_sum[span, lanes] += _dot(probs.astype(LOW), grads, NN)

    @pl.when(block == blocks - 1)
    def _():
        def write(place, carry):
            into = pl.ds(pl.multiple_of(place * BLOCK, BLOCK), BLOCK)
            source = pl.ds(pl.multiple_of((place + 1) * BLOCK, BLOCK), BLOCK)
            out_ref[into, width : 2 * width] = key_sum[source, :].astype(LOW)
            out_ref[into, 2 * width :] = value_sum[source, :].astype(LOW)
            return carry

        lax.fori_loop(0, blocks, write, 0)


def _params():
    return pltpu.CompilerParams(dimension_semantics=("arbitrary",), vmem_limit_bytes=56 << 20)


def attend(qkv_rows, query_id, key_id):
    rows, triple = qkv_rows.shape
    width, blocks = triple // 3, rows // BLOCK
    heads = width // HEAD_DIM
    return pl.pallas_call(
        lambda *refs: attend_kernel(width, blocks, *refs),
        grid=(blocks,),
        in_specs=[
            pl.BlockSpec((rows, triple), lambda i: (0, 0)),
            pl.BlockSpec((1, 1, BLOCK), lambda i: (i, 0, 0)),
            pl.BlockSpec((rows + 2 * BLOCK, 1), lambda i: (0, 0)),
        ],
        out_specs=[
            pl.BlockSpec((BLOCK, width), lambda i: (i, 0)),
            pl.BlockSpec((1, heads // 2, 2 * BLOCK), lambda i: (i, 0, 0)),
        ],
        out_shape=[
            jax.ShapeDtypeStruct((rows, width), LOW),
            jax.ShapeDtypeStruct((blocks, heads // 2, 2 * BLOCK), F32),
        ],
        compiler_params=_params(),
        cost_estimate=NO_COST,
    )(qkv_rows, query_id, key_id)


def attend_back(qkv_rows, grad_rows, log_total, query_id, key_id):
    rows, triple = qkv_rows.shape
    width, blocks = triple // 3, rows // BLOCK
    heads = width // HEAD_DIM
    return pl.pallas_call(
        lambda *refs: attend_back_kernel(width, blocks, *refs),
        grid=(blocks,),
        in_specs=[
            pl.BlockSpec((rows, triple), lambda i: (0, 0)),
            pl.BlockSpec((rows, width), lambda i: (0, 0)),
            pl.BlockSpec((1, heads // 2, 2 * BLOCK), lambda i: (i, 0, 0)),
            pl.BlockSpec((1, 1, BLOCK), lambda i: (i, 0, 0)),
            pl.BlockSpec((rows + 2 * BLOCK, 1), lambda i: (0, 0)),
        ],
        out_specs=pl.BlockSpec((rows, triple), lambda i: (0, 0)),
        out_shape=jax.ShapeDtypeStruct((rows, triple), LOW),
        scratch_shapes=[
            pltpu.VMEM((rows + 2 * BLOCK, width), F32),
            pltpu.VMEM((rows + 2 * BLOCK, width), F32),
        ],
        compiler_params=_params(),
        cost_estimate=NO_COST,
    )(qkv_rows, grad_rows, log_total, query_id, key_id)


def layer_norm(values, gain_row, bias_row, mean=None):
    centre = values - (jnp.mean(values, axis=-1, keepdims=True) if mean is None else mean)
    spread = jnp.mean(centre * centre, axis=-1, keepdims=True)
    return centre * lax.rsqrt(spread + 1e-06) * gain_row + bias_row


def norm_back_kernel(
    groups, keep_sum, values_ref, cot_ref, more_ref, gain_ref, low_ref, sum_ref, out_ref=None
):
    @pl.when(pl.program_id(0) == 0)
    def _():
        sum_ref[...] = jnp.zeros_like(sum_ref)

    values = values_ref[...]
    if groups:
        group = lax.broadcasted_iota(jnp.int32, (values.shape[0], groups), 1)
        chosen = jnp.where(more_ref[...] == group, 1.0, 0.0)
        cot = jnp.dot(chosen, cot_ref[...], precision=HIGHEST_PREC, preferred_element_type=F32)
    else:
        cot = cot_ref[...]
    centre = values - jnp.mean(values, axis=-1, keepdims=True)
    scale = lax.rsqrt(jnp.mean(centre * centre, axis=-1, keepdims=True) + 1e-06)
    normed = centre * scale
    scaled = cot * gain_ref[...]
    grad = scale * (
        scaled
        - jnp.mean(scaled, axis=-1, keepdims=True)
        - normed * jnp.mean(scaled * normed, axis=-1, keepdims=True)
    )
    if not groups:
        grad = grad + more_ref[...]
    low = grad.astype(LOW)
    if keep_sum:
        out_ref[...] = grad
    low_ref[...] = low
    for row, value in enumerate((cot * normed, cot, low.astype(F32))):
        sum_ref[row : row + 1, :] += jnp.sum(value, axis=0, keepdims=True)


def norm_back(values, gain_row, cotangent, more, keep_sum=True):
    rows, width = values.shape
    groups = cotangent.shape[0] if more.shape[1] == 1 else 0
    tile = rows // 8
    block = pl.BlockSpec((tile, width), lambda i: (i, 0))
    line = pl.BlockSpec((1, width), lambda i: (0, 0))
    out_specs = [block, pl.BlockSpec((8, width), lambda i: (0, 0))]
    out_shape = [jax.ShapeDtypeStruct((rows, width), LOW), jax.ShapeDtypeStruct((8, width), F32)]
    if keep_sum:
        out_specs.append(block)
        out_shape.append(jax.ShapeDtypeStruct((rows, width), F32))
    return pl.pallas_call(
        lambda *refs: norm_back_kernel(groups, keep_sum, *refs),
        grid=(8,),
        in_specs=[
            block,
            pl.BlockSpec((groups, width), lambda i: (0, 0)) if groups else block,
            pl.BlockSpec((tile, 1), lambda i: (i, 0)) if groups else block,
            line,
        ],
        out_specs=out_specs,
        out_shape=out_shape,
        compiler_params=_params(),
        cost_estimate=NO_COST,
    )(values, cotangent, more, gain_row[None])


def small_kernel(spots_ref, first_ref, second_ref, last_ref, qkv_ref, up_ref, out_ref):
    width, slots = out_ref.shape[1], spots_ref.shape[0]
    out_ref[...] = jnp.zeros_like(out_ref)
    rows = [(first_ref, 0), (first_ref, 1), (second_ref, 0), (second_ref, 1), (last_ref, 0), (last_ref, 1)]
    rows += [(first_ref, 2), (qkv_ref, 0), (qkv_ref, 2), (second_ref, 2), (last_ref, 2)]
    for row, (ref, which) in enumerate(rows):
        if ref is qkv_ref:
            out_ref[row : row + 1, :] = ref[:, which * width : (which + 1) * width]
        else:
            out_ref[row : row + 1, :] = ref[which : which + 1, :]
    for slot in range(slots):
        out_ref[pl.ds(16 + spots_ref[slot], 1), :] = up_ref[slot : slot + 1, :]


def small_sums(first, second, last, qkv_sum, up_sums):
    width, count = first.shape[1], lax.axis_size("pack")
    spots = relative_packs() ^ lax.axis_index("pack")
    up_sum = jnp.concatenate(up_sums).reshape(count, -1)
    arrays = [first, second, last, qkv_sum[None], jnp.pad(up_sum, ((0, 0), (0, width - up_sum.shape[1])))]
    return pl.pallas_call(
        small_kernel,
        in_specs=[pl.BlockSpec(memory_space=pltpu.SMEM)] + [pl.BlockSpec(memory_space=pltpu.VMEM)] * len(arrays),
        out_specs=pl.BlockSpec(memory_space=pltpu.VMEM),
        out_shape=jax.ShapeDtypeStruct((16 + count, width), F32),
        compiler_params=pltpu.CompilerParams(vmem_limit_bytes=16 << 20),
        cost_estimate=NO_COST,
    )(spots, *arrays)


def gelu(values):
    return 0.5 * values * (1.0 + lax.erf(values * math.sqrt(0.5)))


def gelu_slope(values):
    return 0.5 * (1.0 + lax.erf(values * math.sqrt(0.5))) + values * (
        math.sqrt(0.5 / math.pi) * jnp.exp(-0.5 * values * values)
    )


def as_rows(width, *values):
    rows = [jnp.pad(value.reshape(1, -1), ((0, 0), (0, width - value.size))) for value in values]
    return jnp.pad(jnp.concatenate(rows), ((0, 8 - len(rows)), (0, 0)))


def from_rows(cells, shape):
    rows, columns = shape
    flat = cells[:, 0, : rows * columns].reshape(-1, rows, columns)
    return flat.transpose(1, 0, 2).reshape(rows, -1)


def mm(spec, left, right):
    return jnp.einsum(spec, left, right, preferred_element_type=F32)


def column_sum(rows):
    return jnp.sum(rows.astype(F32), axis=0)


def hmul(left, right):
    return jnp.dot(left, right, precision=NS_PREC, preferred_element_type=F32)


def ortho(columns, beside):
    gram_part = lax.dot_general(columns, columns, (TN, ((), ())), precision=NS_PREC, preferred_element_type=F32)
    folded, beside = column_all_sum(fold(gram_part), beside)
    gram_mat, scale = unfold(folded, columns.shape[1])
    iterate = columns * scale
    eye = jnp.eye(gram_mat.shape[0], dtype=F32)
    for step in range(NS_STEPS):
        if step < NS_STEPS - 1:
            square = hmul(gram_mat, gram_mat)
            poly = COEF_ONE * eye + COEF_TWO * gram_mat + COEF_THREE * square
            poly_gram = COEF_ONE * gram_mat + COEF_TWO * square + COEF_THREE * hmul(square, gram_mat)
            iterate = hmul(iterate, poly)
            gram_mat = hmul(poly, poly_gram)
        else:
            first_pass = hmul(iterate, gram_mat)
            iterate = COEF_ONE * iterate + COEF_TWO * first_pass + COEF_THREE * hmul(first_pass, gram_mat)
    return iterate, beside


def to_columns(shards):
    chip = lax.axis_index("pack") >> 1
    most = max(m.shape[0] for m in shards)
    filled = [jnp.pad(m, ((0, most - m.shape[0]), (0, 0))) for m in shards]
    filled += [jnp.zeros_like(filled[0])] * (lax.axis_size("pack") // 2 - len(shards))
    stacked = jnp.stack(filled)
    parts = [pick(stacked, chip)]
    parts += [swap(pick(stacked, chip ^ (k // 2)), "pack", k) for k in other_chips()]
    return jnp.stack(parts)


def from_columns(value, counts):
    back = [value[0]] + [swap(value[k // 2], "pack", k) for k in other_chips()]
    return [_choose(back, lax.axis_index("pack") >> 1, m)[:count] for m, count in enumerate(counts)]


def muon_update(weight, iterate):
    col_ratio = math.sqrt(
        max(1.0, iterate.shape[1] * lax.axis_size(("pack", "seq")) / weight.shape[0])
    )
    return weight * (1.0 - MUON_RATE * DECAY) - MUON_RATE * col_ratio * iterate


def adam_update(weight, first_moment, second_moment, gradient, factor, count_float):
    scaled = factor * gradient
    new_first = BETA_ONE * first_moment + (1.0 - BETA_ONE) * scaled
    new_second = BETA_TWO * second_moment + (1.0 - BETA_TWO) * scaled * scaled
    first_hat = new_first / (1.0 - jnp.power(BETA_ONE, count_float))
    second_hat = new_second / (1.0 - jnp.power(BETA_TWO, count_float))
    new_weight = weight - ADAM_RATE * (first_hat / (jnp.sqrt(second_hat) + 1e-08) + DECAY * weight)
    return (new_weight, new_first, new_second)


def deal_rows(lengths, keep_mask, shard_len):
    packs, images = lengths.shape
    seq_count, seq_place = lax.axis_size("seq"), lax.axis_index("seq")
    image_range = jnp.arange(images, dtype=jnp.int32)
    upto = image_range[None, :] <= image_range[:, None]
    ends = jnp.sum(jnp.where(upto[None], lengths[:, None, :], 0), axis=2, dtype=jnp.int32)
    starts = ends - lengths
    cuts = jnp.arange(1, seq_count, dtype=jnp.int32) * shard_len
    straddles = (starts[:, None, :] < cuts[None, :, None]) & (ends[:, None, :] > cuts[None, :, None])
    behind = jnp.sum(jnp.where(straddles, cuts[None, :, None] - starts[:, None, :], 0), axis=2, dtype=jnp.int32)
    ahead = jnp.sum(jnp.where(straddles, ends[:, None, :] - cuts[None, :, None], 0), axis=2, dtype=jnp.int32)
    excess = jnp.zeros_like(cuts)
    moves = []
    for pack in range(packs):
        more, less = excess + ahead[pack], excess - behind[pack]
        forward = jnp.abs(more) <= jnp.abs(less)
        excess = jnp.where(forward, more, less)
        moves.append(jnp.where(forward, ahead[pack], -behind[pack]))
    borders = jnp.concatenate(
        [
            jnp.zeros((packs, 1), jnp.int32),
            cuts[None, :] + jnp.stack(moves),
            jnp.full((packs, 1), PACK_LEN, jnp.int32),
        ],
        axis=1,
    )
    first = lax.dynamic_index_in_dim(borders, seq_place, 1, keepdims=False)
    held = lax.dynamic_index_in_dim(borders, seq_place + 1, 1, keepdims=False) - first
    pack_range = jnp.arange(packs, dtype=jnp.int32)
    before = jnp.sum(jnp.where(pack_range[None, :] < pack_range[:, None], held[None, :], 0), axis=1, dtype=jnp.int32)
    row = jnp.arange(packs * shard_len + MAXLEN, dtype=jnp.int32)
    in_pack = (row[:, None] >= before[None, :]) & (row[:, None] < (before + held)[None, :])
    valid = jnp.any(in_pack, axis=1)

    def of_pack(values):
        return jnp.sum(jnp.where(in_pack, values, 0), axis=1, dtype=jnp.int32)

    pack_of = of_pack(pack_range[None, :])
    place = of_pack(row[:, None] - before[None, :] + first[None, :])
    window = shard_len + 2 * MAXLEN
    source = jnp.where(valid, pack_of * window + place - (seq_place * shard_len - MAXLEN), -1)
    row_ends = jnp.sum(jnp.where(in_pack[:, :, None], ends[None], 0), axis=1, dtype=jnp.int32)
    row_starts = jnp.sum(jnp.where(in_pack[:, :, None], starts[None], 0), axis=1, dtype=jnp.int32)
    image_of = jnp.sum((place[:, None] >= row_ends).astype(jnp.int32), axis=1, dtype=jnp.int32)
    is_first = jnp.any(place[:, None] == row_starts, axis=1)
    keep_rows = mm("rp,pj->rj", in_pack.astype(LOW), (keep_mask > 0).astype(LOW))
    spot = jnp.arange(PACK_LEN, dtype=jnp.int32)
    kept = jnp.any((place[:, None] == spot[None, :]) & (keep_rows > 0.5), axis=1)
    live = valid & (kept | is_first)
    group = jnp.where(valid, pack_of * images + image_of, -1)

    spots = jnp.arange(PACK_LEN, dtype=jnp.int32)[None, None, :]
    inside = (spots >= starts[:, :, None]) & (spots < ends[:, :, None])
    counted = inside & ((keep_mask > 0)[:, None, :] | (spots == starts[:, :, None]))
    counts = jnp.sum(counted.astype(F32), axis=2)
    return source, group, live, counts.reshape(-1)


def body(
    patches,
    lengths,
    keep_mask,
    labels,
    step_count,
    embed_weight,
    embed_first,
    embed_second,
    qkv_weight,
    qkv_moment,
    output_weight,
    output_moment,
    up_weight,
    up_moment,
    down_weight,
    down_moment,
    small_params,
    small_first,
    small_second,
    head_weight,
    head_first,
    head_second,
    head_bias,
    bias_first,
    bias_second,
):
    packs, shard_len, patch_in = patches.shape
    images = lengths.shape[1]
    width = qkv_weight.shape[0]
    seq_count, seq_place = lax.axis_size("seq"), lax.axis_index("seq")
    pack_count, pack_place = lax.axis_size("pack"), lax.axis_index("pack")
    small_rows = small_params.shape[0]

    bundle = [
        embed_weight.T,
        qkv_weight.T,
        output_weight.T,
        as_rows(width, small_params, head_bias),
    ]
    spots = [0]
    for piece in bundle:
        spots.append(spots[-1] + piece.shape[0])
    first = Gather(jnp.concatenate([piece.astype(LOW) for piece in bundle]))
    up_gather, down_gather = Gather(up_weight.T.astype(LOW)), Gather(down_weight.T.astype(LOW))
    first.along_seq()
    first.block, patches = hold(first.block, patches)
    first.in_plane()
    ends = seq_count - 1
    from_left = lax.ppermute(patches[:, shard_len - MAXLEN :], "seq", [(i, i + 1) for i in range(ends)])
    from_right = lax.ppermute(patches[:, :MAXLEN], "seq", [(i + 1, i) for i in range(ends)])
    window = jnp.concatenate([from_left, patches, from_right], axis=1).reshape(-1, patch_in)
    source, group, live, counts = deal_rows(lengths, keep_mask, shard_len)
    chosen = (source[:, None] == jnp.arange(window.shape[0], dtype=jnp.int32)[None, :]).astype(LOW)
    tokens = mm("rw,wi->ri", chosen, window).astype(LOW)
    tokens, up_gather.shard, *first.parts = hold(tokens, up_gather.shard, *first.parts)
    up_gather.send_seq()
    embed_full, qkv_full, output_full, small_full = first.pieces(spots)
    embed_full, qkv_full, output_full = (
        value.reshape(-1, width) for value in (embed_full, qkv_full, output_full)
    )
    (gain_bias,) = hold(from_rows(small_full, small_params.shape).astype(F32))
    bias_full = lax.dynamic_slice_in_dim(small_full, pack_place * seq_count, seq_count, 0)
    bias_full = bias_full[:, 1, : head_bias.shape[0]].reshape(-1)

    rows = tokens.shape[0]
    query_id = group.reshape(rows // BLOCK, 1, BLOCK)
    key_id = jnp.pad(jnp.where(live, group, -2), (BLOCK, BLOCK), constant_values=-2)[:, None]
    group_count = packs * images
    member = (
        (group[None, :] == jnp.arange(group_count, dtype=jnp.int32)[:, None]) & live[None, :]
    ).astype(F32)

    embedded = mm("ri,di->rd", tokens, embed_full) + gain_bias[6]
    mean_one = jnp.mean(embedded, axis=-1, keepdims=True)
    embedded, mean_one, up_gather.parts[0], down_gather.shard = hold(
        embedded, mean_one, up_gather.parts[0], down_gather.shard
    )
    up_gather.join_seq()
    up_gather.in_plane()
    down_gather.doubling()
    normed_one = layer_norm(embedded, gain_bias[0], gain_bias[1], mean_one).astype(LOW)
    qkv_bias = jnp.concatenate([gain_bias[7], jnp.zeros_like(gain_bias[7]), gain_bias[8]])
    qkv_rows = (mm("rd,ed->re", normed_one, qkv_full) + qkv_bias).astype(LOW)
    qkv_rows, down_gather.block, head_low, *up_gather.parts = hold(
        qkv_rows, down_gather.block, head_weight.astype(LOW), *up_gather.parts
    )
    head_full = lax.all_gather(head_low, "seq", axis=0, tiled=True)
    down_gather.in_plane()
    up_full = [half.reshape(-1, width) for half in up_gather.halves()]
    attn_low, log_total = attend(qkv_rows, query_id, key_id)
    attn_low, *down_gather.parts = hold(attn_low, *down_gather.parts)
    down_full = [half.reshape(-1, width) for half in down_gather.halves()]
    after_attn = embedded + mm("re,de->rd", attn_low, output_full) + gain_bias[9]
    normed_two = layer_norm(after_attn, gain_bias[2], gain_bias[3]).astype(LOW)
    up_bias = jnp.take(
        gain_bias[11:15].reshape(pack_count, -1), relative_packs() ^ pack_place, axis=0
    ).reshape(2, -1)
    up_rows = [mm("rd,fd->rf", normed_two, up_full[half]) + up_bias[half] for half in range(2)]
    active = [gelu(rows).astype(LOW) for rows in up_rows]
    after_mlp = (
        after_attn
        + (mm("rf,fd->rd", active[0], down_full[0]) + mm("rf,fd->rd", active[1], down_full[1]))
        + gain_bias[10]
    )
    final_rows = layer_norm(after_mlp, gain_bias[4], gain_bias[5])
    pool_sums = jnp.dot(member, final_rows, precision=HIGHEST_PREC, preferred_element_type=F32)
    pooled_mine = (pool_sums / counts[:, None]).astype(LOW)

    img_share = group_count // seq_count
    split = pooled_mine.reshape(seq_count, img_share, width)
    pooled_low = tree_sum(
        [pick(split, seq_place).astype(F32)]
        + [swap(pick(split, seq_place ^ k), "seq", k).astype(F32) for k in range(1, seq_count)]
    ).astype(LOW)
    pooled_rows = jnp.concatenate(gather_blocks(pooled_low), axis=0).reshape(-1, width)
    depth = head_weight.shape[0]
    label_cols = head_full.shape[1]
    logits = mm("nd,dc->nc", pooled_rows, head_full) + bias_full.astype(F32)
    label_rows = jnp.take(
        pick(labels.reshape(pack_count, seq_count, img_share), seq_place, 1),
        relative_packs() ^ pack_place,
        axis=0,
    ).reshape(-1)
    class_ids = pack_place * label_cols + jnp.arange(label_cols, dtype=jnp.int32)
    valid = (class_ids < LABELS).astype(F32)
    target = (label_rows[:, None] == class_ids[None, :]).astype(F32)
    image_total = labels.shape[0] * labels.shape[1]
    loss_part = jnp.sum(valid[None, :] * (jax.nn.softplus(logits) - target * logits)) / image_total
    grad_logits = (valid[None, :] * (jax.nn.sigmoid(logits) - target) / image_total).astype(LOW)
    pooled_part = mm("nc,dc->nd", grad_logits, head_full).reshape(pack_count, img_share, width)
    pooled_grad = pack_scatter(pooled_part)
    pooled_grad = jnp.concatenate(absolute(relative(pooled_grad, "seq"), seq_place), axis=0)
    pooled_grad = pooled_grad / counts[:, None]

    traded, pooled_grad = hold(jnp.concatenate([pooled_rows, grad_logits], axis=1), pooled_grad)
    traded = lax.all_gather(traded, "seq", axis=0, tiled=True)

    grad_mlp_low, sums_last, grad_mlp = norm_back(
        after_mlp, gain_bias[4], pooled_grad, jnp.where(live, group, -1)[:, None]
    )
    down_sum, up_sum = Scatter(0, width, True), Scatter(1, width, True)
    half = width // 2
    late_sums = [Scatter(0, half), Scatter(1, half)]
    pair_sums = [Scatter(0, half), Scatter(1, half)]
    down_out = mm("rf,rd->fd", active[1], grad_mlp_low)
    down_keep = mm("rf,rd->fd", active[0], grad_mlp_low)
    grad_mlp_low, down_out, down_keep = hold(grad_mlp_low, down_out, down_keep)
    down_out = down_sum.start_halves(down_keep, down_out)
    grad_upper = [
        (mm("rd,fd->rf", grad_mlp_low, down_full[side]) * gelu_slope(up_rows[side])).astype(LOW)
        for side in range(2)
    ]
    up_out = mm("rf,rd->fd", grad_upper[1], normed_two)
    up_keep = mm("rf,rd->fd", grad_upper[0], normed_two)
    grad_upper[0], grad_upper[1], up_out, up_keep = hold(*grad_upper, up_out, up_keep)
    up_out = up_sum.start_halves(up_keep, up_out)
    grad_normed = mm("rf,fd->rd", grad_upper[0], up_full[0]) + mm("rf,fd->rd", grad_upper[1], up_full[1])
    down_out = down_sum.step(down_out)
    grad_normed, down_out = hold(grad_normed, down_out)
    grad_attn_low, sums_second, grad_attn = norm_back(
        after_attn, gain_bias[2], grad_normed, grad_mlp
    )
    grad_mixed = mm("rd,de->re", grad_attn_low, output_full).astype(LOW)
    up_out = up_sum.step(up_out)
    grad_mixed, up_out = hold(grad_mixed, up_out)
    grad_qkv = attend_back(qkv_rows, grad_mixed, log_total, query_id, key_id)
    down_out, up_out = down_sum.step(down_out), up_sum.step(up_out)
    grad_qkv, down_out, up_out = hold(grad_qkv, down_out, up_out)
    grad_normed = mm("re,ed->rd", grad_qkv, qkv_full)
    grad_embed_rows, sums_first = norm_back(embedded, gain_bias[0], grad_normed, grad_attn, keep_sum=False)
    output_grad = mm("rd,re->de", grad_attn_low, attn_low)
    embed_grad = mm("rd,ri->di", grad_embed_rows, tokens)
    down_sum.finish(down_out)
    up_sum.finish(up_out)
    early = jnp.concatenate([down_sum.value, up_sum.value], axis=1)
    pair_keep, pair_out = late_halves(output_grad, embed_grad)
    grad_qkv, pair_out, early = hold(grad_qkv, pair_out, early)
    early = lax.psum_scatter(early, "seq", scatter_dimension=0)
    late_keep, late_out = late_halves(mm("re,rd->ed", grad_qkv, normed_one))
    pair = pair_keep + swap(pair_out, "pack", 1)
    pair_outs = [
        each.start_joined(part) for each, part in zip(pair_sums, (pair[..., :half], pair[..., half:]))
    ]
    late_out, grad_qkv, traded, *pair_outs = hold(late_out, grad_qkv, traded, *pair_outs)
    all_logits = traded[:, width:]
    bias_grad = pick(column_sum(all_logits).reshape(seq_count, -1), seq_place)
    late = late_keep + swap(late_out, "pack", 1)
    late_outs = [
        each.start_joined(part) for each, part in zip(late_sums, (late[..., :half], late[..., half:]))
    ]
    bias_grad, grad_qkv, traded, grad_upper[0], grad_upper[1], *held = hold(
        bias_grad, grad_qkv, traded, *grad_upper, *late_outs, *[each.keep for each in pair_sums]
    )
    late_outs = held[:2]
    pair_sums[0].keep, pair_sums[1].keep = held[2:]
    all_pooled = pick(traded[:, :width].reshape(-1, seq_count, head_weight.shape[0]), seq_place, 1)
    head_grad = mm("nd,nc->dc", all_pooled, traded[:, width:])
    small_mine = small_sums(
        sums_first, sums_second, sums_last, column_sum(grad_qkv), [column_sum(side) for side in grad_upper]
    )
    for each, sent in zip(pair_sums, pair_outs):
        each.finish(sent)
    pair = jnp.concatenate([each.value for each in pair_sums], axis=2)
    late_outs = [each.step(sent) for each, sent in zip(late_sums, late_outs)]
    small_mine, head_grad, pair, *late_outs = hold(small_mine, head_grad, pair, *late_outs)
    small_total = small_mine + swap(small_mine, "pack", 1)
    for each, sent in zip(late_sums, late_outs):
        each.finish(sent)
    late_sum = SeqScatter(
        jnp.concatenate([jnp.concatenate([each.value for each in late_sums], axis=2), pair], axis=1)
    )
    late_out, small_total, early = hold(late_sum.send(), small_total, early)
    small_total = sum_chips(small_total)
    late_out = late_sum.step(late_out)
    late_out, small_total = hold(late_out, small_total)
    small_total = all_sum(small_total, "seq")
    while late_out is not None:
        late_out = late_sum.step(late_out)
    late_sum.value, small_total = hold(late_sum.value, small_total)
    down_share, up_share = jnp.split(early, 2)
    late_share = late_sum.result()
    widths = [qkv_weight.shape[1], output_weight.shape[1], embed_weight.shape[1]]
    qkv_share, output_share = late_share[: widths[0]], late_share[widths[0] : widths[0] + widths[1]]
    embed_share = late_share[widths[0] + widths[1] :].T
    hidden = down_weight.shape[1] * seq_count
    small_total = jnp.concatenate(
        [small_total[:11], small_total[16:, :hidden].reshape(small_rows - 11, width)], axis=0
    )
    place = pack_place * seq_count + seq_place
    small_share = pick(small_total.reshape(small_rows, pack_count * seq_count, -1), place, 1)

    shares = (early, late_share, head_grad, bias_grad)
    square_sum = sum((jnp.sum(piece * piece) for piece in shares))
    sums = jnp.broadcast_to(jnp.stack([loss_part, square_sum])[:, None], (2, BLOCK))
    sums = sum_plane(all_sum(sums, "seq"))
    loss_value, square_total = sums[0, 0], sums[1, 0] + jnp.sum(small_total * small_total)
    grad_norm = jnp.sqrt(square_total)
    factor = jnp.minimum(1.0, CLIP_NORM / (grad_norm + 1e-06))
    muon_shares = (qkv_share, output_share, up_share, down_share)
    moments = [
        MUON_MU * moment.T + factor * share
        for moment, share in zip((qkv_moment, output_moment, up_moment, down_moment), muon_shares)
    ]
    columns = to_columns(moments)
    count_float = step_count[0].astype(F32)
    iterates, (new_head, new_head_first, new_head_second) = ortho(
        columns.reshape(-1, width),
        adam_update(head_weight, head_first, head_second, head_grad, factor, count_float),
    )
    iterates = iterates.reshape(columns.shape)
    iterates = [iterate.T for iterate in from_columns(iterates, [m.shape[0] for m in moments])]
    moments = [moment.T for moment in moments]
    new_qkv = muon_update(qkv_weight, iterates[0])
    new_output = muon_update(output_weight, iterates[1])
    new_up = muon_update(up_weight, iterates[2])
    new_down = muon_update(down_weight, iterates[3])
    new_embed, new_embed_first, new_embed_second = adam_update(
        embed_weight, embed_first, embed_second, embed_share, factor, count_float
    )
    new_small, new_small_first, new_small_second = adam_update(
        small_params, small_first, small_second, small_share, factor, count_float
    )
    new_bias, new_bias_first, new_bias_second = adam_update(
        head_bias, bias_first, bias_second, bias_grad, factor, count_float
    )
    return (
        loss_value,
        grad_norm,
        new_embed,
        new_embed_first,
        new_embed_second,
        new_qkv,
        moments[0],
        new_output,
        moments[1],
        new_up,
        moments[2],
        new_down,
        moments[3],
        new_small,
        new_small_first,
        new_small_second,
        new_head,
        new_head_first,
        new_head_second,
        new_bias,
        new_bias_first,
        new_bias_second,
    )


def solution(mesh):
    both = P(None, ("pack", "seq"))
    head = P("seq", "pack")
    line = P(("pack", "seq"))
    return jax.shard_map(
        body,
        mesh=mesh,
        in_specs=(P("pack", "seq", None), P("pack", None), P("pack", None), P(), P())
        + (both,) * 14
        + (head,) * 3
        + (line,) * 3,
        out_specs=(P(), P()) + (both,) * 14 + (head,) * 3 + (line,) * 3,
        check_vma=False,
    )
```
